32 devices in a mesh: fsdp: 32 (over z, y, x, core).
Axes of the slice: x: 2, y: 2, z: 4, core: 2. Of those that a mesh axis runs over, the one named last changes fastest.
Arguments:
- token_ids: int32 [32768], P('fsdp'), may hold values from 0 to 31999
- segment_ids: int32 [32768], P('fsdp'), may hold values from 0 to 15, as said below
- parent_segments: int32 [32, 16], P('fsdp'), may hold values from 0 to 14, as said below
- expert_choice: int32 [32768, 2], P('fsdp'), may hold values from 0 to 7, all different within a row
- drop_order: int32 [32, 2048], P('fsdp'), may hold values from 0 to 2047, each once within a row
- loss_positions: int32 [4096], P('fsdp'), may hold values from 0 to 1023
- target_ids: int32 [4096, 2], P('fsdp'), may hold values from 0 to 31999
- embedding: bfloat16 [32000, 768], P('fsdp'), may hold values from -0.3125 to 0.3125
- attention_weights: bfloat16 [3072, 768], P('fsdp'), may hold values from -2 to 2
- router_weights: bfloat16 [6144], P('fsdp'), may hold values from -0.4375 to 0.4375
- small_params: bfloat16 [2688], P('fsdp'), may hold values from -3 to 3
- inward_weights: bfloat16 [32, 768, 768], P('fsdp'), may hold values from -0.21875 to 0.21875
- outward_weights: bfloat16 [32, 768, 768], P('fsdp'), may hold values from -0.109375 to 0.109375
- embedding_moment: float32 [32000, 768], P('fsdp'), may hold values from -0.00083921955 to 0.00083921955
- embedding_square: float32 [32000, 768], P('fsdp'), may hold values from 2.4152587e-09 to 9.661035e-09
- attention_moment: float32 [3072, 768], P('fsdp'), may hold values from -0.00083921955 to 0.00083921955
- attention_square: float32 [3072, 768], P('fsdp'), may hold values from 2.4152587e-09 to 9.661035e-09
- router_moment: float32 [6144], P('fsdp'), may hold values from -0.00083921955 to 0.00083921955
- router_square: float32 [6144], P('fsdp'), may hold values from 2.4152587e-09 to 9.661035e-09
- params_moment: float32 [2688], P('fsdp'), may hold values from -0.00083921955 to 0.00083921955
- params_square: float32 [2688], P('fsdp'), may hold values from 2.4152587e-09 to 9.661035e-09
- inward_moment: float32 [32, 768, 768], P('fsdp'), may hold values from -1.8649323e-06 to 1.8649323e-06
- inward_square: float32 [32, 768, 768], P('fsdp'), may hold values from 6.038147e-13 to 2.4152587e-12
- outward_moment: float32 [32, 768, 768], P('fsdp'), may hold values from -1.8649323e-06 to 1.8649323e-06
- outward_square: float32 [32, 768, 768], P('fsdp'), may hold values from 6.038147e-13 to 2.4152587e-12
Outputs:
- loss_parts: float32 [32], P('fsdp')
- grad_norm: float32 [], replicated
- embedding_moment_next: float32 [32000, 768], P('fsdp')
- embedding_square_next: float32 [32000, 768], P('fsdp')
- embedding_update: float32 [32000, 768], P('fsdp')
- attention_moment_next: float32 [3072, 768], P('fsdp')
- attention_square_next: float32 [3072, 768], P('fsdp')
- attention_update: float32 [3072, 768], P('fsdp')
- router_moment_next: float32 [6144], P('fsdp')
- router_square_next: float32 [6144], P('fsdp')
- router_update: float32 [6144], P('fsdp')
- params_moment_next: float32 [2688], P('fsdp')
- params_square_next: float32 [2688], P('fsdp')
- params_update: float32 [2688], P('fsdp')
- inward_moment_next: float32 [32, 768, 768], P('fsdp')
- inward_square_next: float32 [32, 768, 768], P('fsdp')
- inward_update: float32 [32, 768, 768], P('fsdp')
- outward_moment_next: float32 [32, 768, 768], P('fsdp')
- outward_square_next: float32 [32, 768, 768], P('fsdp')
- outward_update: float32 [32, 768, 768], P('fsdp')
The draws below stay inside these ranges and needn't reach their ends.
Inputs may be any that keep to these rules, and one draw needn't show every extreme that they name: `segment_ids`: on each device the first 256 tokens are segment 0, then the ids rise by one at each new segment up to 15; every segment holds at least one token. `parent_segments`: segment 0's parent is 0; every other segment's parent is a lower segment.
All inputs are finite; a program needn't handle non-finite values.
Results may differ from the reference program's by a relative error of at most 0.0024.
The reference program's roundings to bfloat16 on the way count: a program that leaves them out, or rounds other values in their place, can miss the bound.
Values may be sent and summed in bfloat16 or wider, within the bound.
A program may use at most 576 MiB of HBM per device.

```python
import math
import jax
import jax.numpy as jnp
import numpy as np
from jax import lax

D = 768
HEADS = 12
HEAD_DIM = 64
FF = 3072
V = 32000
NB = 32
SPLIT = 4
NSEG = 16
STEP = 10
TOK_DEV = 1024
EXPERTS = 8
CAP = 288
TRUNK = 256
TOKENS = 32768
LOSS_ROWS = 4096
NSMALL = 2688
PARAMS = 64692864
N_FSDP = 32


def draw_segment_ids(key, part):
    devices = TOKENS // TOK_DEV
    branch = TOK_DEV - TRUNK
    tree_keys = jax.random.split(key, devices)

    def one_tree(tree_key):
        cut_points = jax.random.permutation(tree_key, branch - 1)[:NSEG - 2] + 1
        offsets = jnp.arange(branch, dtype=jnp.int32)
        branch_ids = 1 + jnp.sum((cut_points[None, :] <= offsets[:, None]).astype(jnp.int32), axis=1)
        return jnp.concatenate([jnp.zeros((TRUNK,), jnp.int32), branch_ids.astype(jnp.int32)])
    return jax.vmap(one_tree)(tree_keys).reshape(-1).astype(jnp.int32)


def draw_parent_segments(key, part):
    devices = TOKENS // TOK_DEV
    upper_bound = jnp.maximum(jnp.arange(NSEG, dtype=jnp.int32), 1)
    return jax.random.randint(key, (devices, NSEG), 0, upper_bound[None, :]).astype(jnp.int32)


def draw_attention_weights(key, part):
    row_index = jnp.arange(4 * D)
    spread = jnp.where(row_index < 3 * D, 1.0, 4.0) * D ** (-0.5)
    normal = jnp.clip(jax.random.normal(key, (4 * D, D), jnp.float32), -3.0, 3.0)
    return (normal * spread[:, None]).astype(jnp.bfloat16)


def draw_small_params(key, part):
    gain_key, bias_key = jax.random.split(key)
    gains_part = jax.random.uniform(gain_key, (3 * D,), jnp.float32, 0.6, 1.4)
    bias_part = jnp.clip(jax.random.normal(bias_key, (HEADS * NB,), jnp.float32), -3.0, 3.0)
    return jnp.concatenate([gains_part, bias_part]).astype(jnp.bfloat16)


def place_ends(entries, stream_key, least, high):
    longest = entries.shape.index(max(entries.shape))
    spots = []
    for shift in (0, 1):
        where = [jax.random.randint(jax.random.fold_in(stream_key, axis), (), 0, length) for axis, length in enumerate(entries.shape)]
        where[longest] = (where[longest] + shift) % entries.shape[longest]
        spots.append(tuple(where))
    return entries.at[spots[0]].set(least).at[spots[1]].set(high)


def shard_levels(key, dims, shards, least, largest):
    gain = 1.0
    for dim, shards_of in shards:
        heights = jax.random.uniform(jax.random.fold_in(jax.random.fold_in(key, 6), dim), (shards_of,), jnp.float32, least / len(shards), largest / len(shards))
        gain = gain * jnp.repeat(jnp.exp(heights), dims[dim] // shards_of).reshape((-1,) + (1,) * (len(dims) - 1 - dim))
    return gain


def rank_table(number_of, skew):
    weights = [(1 << 20) // math.isqrt(rank ** skew) + 1 for rank in range(1, number_of + 1)]
    deviation = 1 + sum(weights) // (1 << 30)
    return np.cumsum(np.array([max(1, weight // deviation) for weight in weights]))


def skewed_ids(stream_key, extent, count, skew):
    grid = rank_table(count, skew)
    pick = jax.random.randint(jax.random.fold_in(stream_key, 1), extent, 0, int(grid[count - 1]))
    rank = jnp.searchsorted(jnp.asarray(grid, jnp.int32), pick, side="right")
    return jax.random.permutation(jax.random.fold_in(stream_key, 2), count)[rank].astype(jnp.int32)


def distinct(stream_key, rows, count, top, lift):
    ranking = jax.random.permutation(jax.random.fold_in(stream_key, 1), count)
    favour = ranking
    for power in range(3):
        favour = favour * favour // count
    favour = favour * lift // count
    lots = jax.random.randint(jax.random.fold_in(stream_key, 2), (rows, count), 0, 4096) + favour
    holders = jax.random.permutation(jax.random.fold_in(stream_key, 3), rows)[jnp.arange(count) % rows]
    lots = jnp.where(jnp.arange(rows)[:, None] == holders[None, :], 1 << 14, lots)
    merit = lots * count + jnp.arange(count)
    return lax.top_k(merit.astype(jnp.int32), top)[1].astype(jnp.int32)


def noise(rng, extent, deviation, reach, shards=(), kind=jnp.bfloat16):
    values = deviation * jax.random.normal(rng, extent, jnp.float32)
    if shards:
        values = values * shard_levels(rng, extent, shards, -0.22, 0.18)
    return jnp.clip(values, -reach, reach).astype(kind)


def setup_inputs(seed: int = 0) -> dict:
    key_of = jax.random.split(jax.random.key(seed), 26)
    token_ids = place_ends(skewed_ids(key_of[0], (TOKENS,), V, 2), jax.random.fold_in(key_of[0], 3), 0, V - 1).astype(jnp.int32)
    segment_ids = draw_segment_ids(jax.random.fold_in(key_of[25], 71), 0)
    parent_segments = draw_parent_segments(jax.random.fold_in(key_of[25], 71), 0)
    expert_choice = distinct(key_of[3], TOKENS, EXPERTS, 2, 4096)
    drop_order = jax.vmap(lambda own: jax.random.permutation(own, 2 * TOK_DEV))(jax.random.split(key_of[4], N_FSDP)).reshape((N_FSDP, 2 * TOK_DEV)).astype(jnp.int32)
    loss_positions = place_ends(jax.random.randint(key_of[5], (LOSS_ROWS,), 0, TOK_DEV), jax.random.fold_in(key_of[5], 1), 0, TOK_DEV - 1).astype(jnp.int32)
    target_ids = place_ends(skewed_ids(key_of[6], (LOSS_ROWS, 2), V, 2), jax.random.fold_in(key_of[6], 3), 0, V - 1).astype(jnp.int32)
    embedding = noise(key_of[7], (V, D), (D // 2) ** -0.5, 0.3125, ((0, 32),))
    attention_weights = draw_attention_weights(jax.random.fold_in(key_of[25], 71), 0)
    router_weights = noise(key_of[9], (D * EXPERTS,), (D // 4) ** -0.5, 0.4375, ((0, 32),))
    small_params = draw_small_params(jax.random.fold_in(key_of[25], 71), 0)
    inward_weights = noise(key_of[11], (EXPERTS * SPLIT, D, FF // SPLIT), D ** -0.5, 0.21875, ((0, 32),))
    outward_weights = noise(key_of[12], (EXPERTS * SPLIT, FF // SPLIT, D), FF ** -0.5, 0.109375, ((0, 32),))
    embedding_moment = noise(key_of[13], (V, D), (72 * (LOSS_ROWS * PARAMS) ** -0.5), 0.00083921955, ((0, 32),), jnp.float32)
    embedding_square = jnp.clip(jnp.exp(math.log(9.661034638952515e-09) - 1.3862944 * jax.random.uniform(key_of[14], (V, D), jnp.float32) ** shard_levels(key_of[14], (V, D), ((0, 32),), -0.2, 0.2)), 2.4152586597381287e-09, 9.661034638952515e-09)
    attention_moment = noise(key_of[15], (4 * D, D), (72 * (LOSS_ROWS * PARAMS) ** -0.5), 0.00083921955, ((0, 32),), jnp.float32)
    attention_square = jnp.clip(jnp.exp(math.log(9.661034638952515e-09) - 1.3862944 * jax.random.uniform(key_of[16], (4 * D, D), jnp.float32) ** shard_levels(key_of[16], (4 * D, D), ((0, 32),), -0.2, 0.2)), 2.4152586597381287e-09, 9.661034638952515e-09)
    router_moment = noise(key_of[17], (D * EXPERTS,), (72 * (LOSS_ROWS * PARAMS) ** -0.5), 0.00083921955, ((0, 32),), jnp.float32)
    router_square = jnp.clip(jnp.exp(math.log(9.661034638952515e-09) - 1.3862944 * jax.random.uniform(key_of[18], (D * EXPERTS,), jnp.float32) ** shard_levels(key_of[18], (D * EXPERTS,), ((0, 32),), -0.2, 0.2)), 2.4152586597381287e-09, 9.661034638952515e-09)
    params_moment = noise(key_of[19], (NSMALL,), (72 * (LOSS_ROWS * PARAMS) ** -0.5), 0.00083921955, ((0, 32),), jnp.float32)
    params_square = jnp.clip(jnp.exp(math.log(9.661034638952515e-09) - 1.3862944 * jax.random.uniform(key_of[20], (NSMALL,), jnp.float32) ** shard_levels(key_of[20], (NSMALL,), ((0, 32),), -0.2, 0.2)), 2.4152586597381287e-09, 9.661034638952515e-09)
    inward_moment = noise(key_of[21], (EXPERTS * SPLIT, D, FF // SPLIT), (0.16 * (LOSS_ROWS * PARAMS) ** -0.5), 1.8649323010322405e-06, ((0, 32),), jnp.float32)
    inward_square = jnp.clip(jnp.exp(math.log(2.415258748209026e-12) - 1.3862944 * jax.random.uniform(key_of[22], (EXPERTS * SPLIT, D, FF // SPLIT), jnp.float32) ** shard_levels(key_of[22], (EXPERTS * SPLIT, D, FF // SPLIT), ((0, 32),), -0.2, 0.2)), 6.038146870522565e-13, 2.415258748209026e-12)
    outward_moment = noise(key_of[23], (EXPERTS * SPLIT, FF // SPLIT, D), (0.16 * (LOSS_ROWS * PARAMS) ** -0.5), 1.8649323010322405e-06, ((0, 32),), jnp.float32)
    outward_square = jnp.clip(jnp.exp(math.log(2.415258748209026e-12) - 1.3862944 * jax.random.uniform(key_of[24], (EXPERTS * SPLIT, FF // SPLIT, D), jnp.float32) ** shard_levels(key_of[24], (EXPERTS * SPLIT, FF // SPLIT, D), ((0, 32),), -0.2, 0.2)), 6.038146870522565e-13, 2.415258748209026e-12)
    return dict(token_ids=token_ids, segment_ids=segment_ids, parent_segments=parent_segments, expert_choice=expert_choice, drop_order=drop_order, loss_positions=loss_positions, target_ids=target_ids, embedding=embedding, attention_weights=attention_weights, router_weights=router_weights, small_params=small_params, inward_weights=inward_weights, outward_weights=outward_weights, embedding_moment=embedding_moment, embedding_square=embedding_square, attention_moment=attention_moment, attention_square=attention_square, router_moment=router_moment, router_square=router_square, params_moment=params_moment, params_square=params_square, inward_moment=inward_moment, inward_square=inward_square, outward_moment=outward_moment, outward_square=outward_square)


@jax.custom_vjp
def low(v):
    return lax.optimization_barrier(v.astype(jnp.bfloat16)).astype(jnp.float32)

@jax.custom_vjp
def low_back(v):
    return v

def low_keep(v):
    return (low(v), None)

def low_pass(kept, grad):
    return (grad,)

def back_keep(v):
    return (v, None)

def back_low(kept, grad):
    return (low(grad),)
low.defvjp(low_keep, low_pass)
low_back.defvjp(back_keep, back_low)
bucket_marks = (16, 23, 32, 45, 64, 91, 128, 181, 256, 362, 512, 724, 1024, 1448, 2048, 2896)
learn_rate = 0.02
weight_decay = 0.1
clip_base = 8.0
highest = lax.Precision.HIGHEST

def rms_norm(values, gains):
    return values * lax.rsqrt(lax.optimization_barrier(jnp.mean(values * values, axis=-1, keepdims=True)) + 1e-06) * gains

def bucket_of(distance):
    distance = jnp.maximum(distance, 0).astype(jnp.int32)
    bucket = jnp.minimum(distance, 15).astype(jnp.int32)
    for border in bucket_marks:
        bucket = (bucket + (distance >= border).astype(jnp.int32)).astype(jnp.int32)
    return bucket.astype(jnp.int32)

def tree_layout(segments, parents):
    segment_count = parents.shape[0]
    identity_rows = jnp.eye(segment_count, dtype=jnp.int32)

    def widen(step_index, ancestry):
        return jnp.maximum(ancestry, ancestry[parents]).astype(jnp.int32)
    ancestry = lax.fori_loop(0, segment_count, widen, identity_rows)
    member = (segments[:, None] == jnp.arange(segment_count, dtype=jnp.int32)[None, :]).astype(jnp.int32)
    lengths = lax.optimization_barrier(jnp.sum(member, axis=0)).astype(jnp.int32)
    starts = (jnp.cumsum(lengths).astype(jnp.int32) - lengths).astype(jnp.int32)
    before = lax.optimization_barrier(jnp.sum((ancestry - identity_rows) * lengths[None, :], axis=1)).astype(jnp.int32)
    tree_depth = (lax.optimization_barrier(jnp.sum(member * (before - starts)[None, :], axis=1)).astype(jnp.int32) + jnp.arange(segments.shape[0], dtype=jnp.int32)).astype(jnp.int32)
    return (ancestry, tree_depth)

def attend_tree(inputs, tree_weights):
    residual, segments, parents = inputs
    query_weight, key_weight, value_weight, output_weight, gain_first, bias_table = tree_weights
    ancestry, tree_depth = tree_layout(segments, parents)
    length = residual.shape[0]
    normed = low(rms_norm(residual, gain_first))
    queries = low(low_back(jnp.dot(normed, query_weight, precision=highest))).reshape(length, HEADS, HEAD_DIM)
    keys_all = low(low_back(jnp.dot(normed, key_weight, precision=highest))).reshape(length, HEADS, HEAD_DIM)
    values_all = low(low_back(jnp.dot(normed, value_weight, precision=highest))).reshape(length, HEADS, HEAD_DIM)
    order_rows = jnp.arange(length, dtype=jnp.int32)
    allowed = (ancestry[segments][:, segments] > 0) & (order_rows[None, :] <= order_rows[:, None])
    buckets = bucket_of(tree_depth[:, None] - tree_depth[None, :])
    scores = jnp.einsum('ihd,jhd->hij', queries, keys_all, precision=highest) * 0.125 + low(bias_table)[:, buckets]
    scores = low_back(scores)
    scores = jnp.where(allowed[None], scores, -1e+30)
    row_peak = lax.optimization_barrier(jnp.max(scores, axis=-1, keepdims=True))
    raised = jnp.exp(scores - row_peak)
    probs = raised / lax.optimization_barrier(jnp.sum(raised, axis=-1, keepdims=True))
    mixed = jnp.einsum('hij,jhd->ihd', low(probs), values_all, precision=highest).reshape(length, D)
    mixed = low(low_back(mixed))
    return residual + low_back(jnp.dot(mixed, output_weight, precision=highest))

def expert_apply(inputs):
    expert_rows, inward, outward = inputs
    total_out = jnp.zeros(expert_rows.shape, expert_rows.dtype)
    for quarter in range(SPLIT):
        taken_rows = low_back(expert_rows)
        before_act = low_back(jnp.dot(taken_rows, inward[quarter], precision=highest))
        hidden = low(jax.nn.gelu(before_act, approximate=True))
        total_out = total_out + low(jnp.dot(hidden, outward[quarter], precision=highest))
    return low_back(total_out)

def slot_table(choices_dev, order_dev):
    flat_choice = choices_dev.reshape(-1).astype(jnp.int32)
    ranked = jnp.zeros_like(flat_choice).at[order_dev].set(flat_choice)
    rank_hits = (ranked[:, None] == jnp.arange(EXPERTS, dtype=jnp.int32)[None, :]).astype(jnp.int32)
    earlier = (jnp.cumsum(rank_hits, axis=0).astype(jnp.int32) - rank_hits).astype(jnp.int32)
    ranked_slot = lax.optimization_barrier(jnp.sum(earlier * rank_hits, axis=1)).astype(jnp.int32)
    return ranked_slot[order_dev].reshape(-1, 2).astype(jnp.int32)

def forward(embedding, attention_weights, router_weights, small_params, inward_weights, outward_weights, token_ids, segment_ids, parent_segments, expert_choice, target_row, loss_positions, target_ids):
    devices = parent_segments.shape[0]
    tokens_dev = token_ids.shape[0] // devices
    gain_first = small_params[0:D]
    gain_second = small_params[D:2 * D]
    gain_final = small_params[2 * D:3 * D]
    bias_table = small_params[3 * D:].reshape(HEADS, NB)
    tree_weights = (attention_weights[0:D], attention_weights[D:2 * D], attention_weights[2 * D:3 * D], attention_weights[3 * D:4 * D], gain_first, bias_table)
    embedded = embedding[token_ids] * math.sqrt(D)
    attended = lax.map(jax.checkpoint(lambda inputs: attend_tree(inputs, tree_weights)), (embedded.reshape(devices, tokens_dev, D), segment_ids.reshape(devices, tokens_dev), parent_segments))
    after_attn = attended.reshape(-1, D)
    routed_in = low(rms_norm(after_attn, gain_second))
    route_logits = low_back(jnp.dot(routed_in, router_weights.reshape(D, EXPERTS), precision=highest))
    chosen = jnp.take_along_axis(route_logits, expert_choice, axis=1)
    gate_peak = lax.optimization_barrier(jnp.max(chosen, axis=1, keepdims=True))
    raised_gate = jnp.exp(chosen - gate_peak)
    gate_weights = raised_gate / lax.optimization_barrier(jnp.sum(raised_gate, axis=1, keepdims=True))
    buffer_rows = EXPERTS * devices * CAP
    dispatched = jnp.zeros((buffer_rows + 1, D), routed_in.dtype).at[target_row.reshape(-1)].add(jnp.repeat(routed_in, 2, axis=0))
    per_expert = dispatched[:buffer_rows].reshape(EXPERTS, devices * CAP, D)
    expert_out = lax.map(jax.checkpoint(expert_apply), (per_expert, inward_weights.reshape(EXPERTS, SPLIT, D, FF // SPLIT), outward_weights.reshape(EXPERTS, SPLIT, FF // SPLIT, D)))
    padded = jnp.concatenate([expert_out.reshape(buffer_rows, D), jnp.zeros((1, D), expert_out.dtype)], axis=0)
    returned = padded[target_row]
    after_moe = after_attn + lax.optimization_barrier(jnp.sum(gate_weights[:, :, None] * returned, axis=1))
    normed_final = rms_norm(after_moe, gain_final)
    rows_pick = (loss_positions.reshape(devices, -1) + (tokens_dev * jnp.arange(devices, dtype=jnp.int32))[:, None]).reshape(-1).astype(jnp.int32)
    picked = low(normed_final[rows_pick])

    def row_loss(inputs):
        rows_part, wanted = inputs
        scores = low_back(jnp.dot(rows_part, embedding.T, precision=highest))
        row_peak = lax.optimization_barrier(jnp.max(scores, axis=1, keepdims=True))
        total_log = row_peak[:, 0] + jnp.log(lax.optimization_barrier(jnp.sum(jnp.exp(scores - row_peak), axis=1)))
        target_hits = jnp.take_along_axis(scores, wanted, axis=1)
        return jnp.sum(total_log - target_hits[:, 0] + 0.3 * (total_log - target_hits[:, 1]))
    losses = lax.map(jax.checkpoint(row_loss), (picked.reshape(devices, -1, D), target_ids.reshape(devices, -1, 2)))
    loss_parts = losses / picked.shape[0]
    return (jnp.sum(loss_parts), loss_parts)

def adam_step(weight, moment, square, gradient, factor):
    clipped = gradient * factor
    moment_next = 0.9 * moment + 0.1 * clipped
    square_next = 0.95 * square + 0.05 * clipped * clipped
    corrected_moment = moment_next / (1.0 - 0.9 ** STEP)
    corrected_square = square_next / (1.0 - 0.95 ** STEP)
    update = -learn_rate * (corrected_moment / (jnp.sqrt(corrected_square) + 1e-08) + weight_decay * weight)
    return (moment_next, square_next, update)

def reference(token_ids, segment_ids, parent_segments, expert_choice, drop_order, loss_positions, target_ids, embedding, attention_weights, router_weights, small_params, inward_weights, outward_weights, embedding_moment, embedding_square, attention_moment, attention_square, router_moment, router_square, params_moment, params_square, inward_moment, inward_square, outward_moment, outward_square):
    devices = parent_segments.shape[0]
    tokens_dev = token_ids.shape[0] // devices
    choice_dev = expert_choice.reshape(devices, tokens_dev, 2)
    slot_rows = lax.map(lambda inputs: slot_table(inputs[0], inputs[1]), (choice_dev, drop_order))
    device_ids = jnp.arange(devices, dtype=jnp.int32)[:, None, None]
    target_row = jnp.where(slot_rows < CAP, choice_dev * (devices * CAP) + device_ids * CAP + slot_rows, EXPERTS * devices * CAP).reshape(-1, 2).astype(jnp.int32)
    weights_f = (embedding.astype(jnp.float32), attention_weights.astype(jnp.float32), router_weights.astype(jnp.float32), small_params.astype(jnp.float32), inward_weights.astype(jnp.float32), outward_weights.astype(jnp.float32))

    def loss_of(table_w, attention_w, router_w, params_w, inward_w, outward_w):
        return forward(table_w, attention_w, router_w, params_w, inward_w, outward_w, token_ids, segment_ids, parent_segments, expert_choice, target_row, loss_positions, target_ids)
    loss_total, back_fn, loss_parts = jax.vjp(loss_of, *weights_f, has_aux=True)
    gradients = back_fn(jnp.ones((), loss_total.dtype))
    total_square = jnp.sum(gradients[0] * gradients[0])
    for gradient in gradients[1:]:
        total_square = total_square + jnp.sum(gradient * gradient)
    grad_norm = jnp.sqrt(total_square)
    factor = jnp.minimum(1.0, clip_base / math.sqrt(LOSS_ROWS) / grad_norm)
    table_m, table_s, table_u = adam_step(weights_f[0], embedding_moment, embedding_square, gradients[0], factor)
    attention_m, attention_s, attention_u = adam_step(weights_f[1], attention_moment, attention_square, gradients[1], factor)
    router_m, router_s, router_u = adam_step(weights_f[2], router_moment, router_square, gradients[2], factor)
    params_m, params_s, params_u = adam_step(weights_f[3], params_moment, params_square, gradients[3], factor)
    inward_m, inward_s, inward_u = adam_step(weights_f[4], inward_moment, inward_square, gradients[4], factor)
    outward_m, outward_s, outward_u = adam_step(weights_f[5], outward_moment, outward_square, gradients[5], factor)
    return (loss_parts, grad_norm, table_m, table_s, table_u, attention_m, attention_s, attention_u, router_m, router_s, router_u, params_m, params_s, params_u, inward_m, inward_s, inward_u, outward_m, outward_s, outward_u)
```

```python
import functools
import math

import jax
import jax.numpy as jnp
from jax import lax
from jax.experimental import pallas as pl
from jax.experimental.pallas import tpu as pltpu
from jax.sharding import PartitionSpec as P

HEADS = 12
NB = 32
SPLIT = 4
STEP = 10
ASK = 48
BLOCK = 4
WINDOW = 3
NT = (((1,), (1,)), ((), ()))
TN = (((0,), (0,)), ((), ()))
MESH = pl.DeviceIdType.MESH


bucket_marks = (16, 23, 32, 45, 64, 91, 128, 181, 256, 362, 512, 724, 1024, 1448, 2048, 2896)
learn_rate = 0.02
weight_decay = 0.1
clip_base = 8.0


def rms_norm(values, gains):
    return values * lax.rsqrt(jnp.mean(values * values, axis=-1, keepdims=True) + 1e-06) * gains


def bucket_of(distance):
    distance = jnp.maximum(distance, 0)
    bucket = jnp.minimum(distance, 15)
    for border in bucket_marks:
        bucket = bucket + (distance >= border).astype(jnp.int32)
    return bucket


def tree_layout(segments, parents):
    segment_count = parents.shape[0]
    identity_rows = jnp.eye(segment_count, dtype=jnp.float32)
    parent_rows = (parents[:, None] == jnp.arange(segment_count, dtype=jnp.int32)[None, :]).astype(
        jnp.float32
    )
    ancestry = jnp.minimum(identity_rows + parent_rows, 1.0)
    reached = 1
    while reached < segment_count - 1:
        ancestry = jnp.minimum(jnp.dot(ancestry, ancestry), 1.0)
        reached = 2 * reached
    member = (segments[:, None] == jnp.arange(segment_count, dtype=jnp.int32)[None, :]).astype(
        jnp.int32
    )
    lengths = jnp.sum(member, axis=0)
    starts = jnp.cumsum(lengths) - lengths
    before = jnp.sum((ancestry - identity_rows).astype(jnp.int32) * lengths[None, :], axis=1)
    tree_depth = jnp.sum(member * (before - starts)[None, :], axis=1) + jnp.arange(
        segments.shape[0], dtype=jnp.int32
    )
    reach_rows = jnp.dot(member.astype(jnp.float32), ancestry)
    linked = jnp.dot(reach_rows, member.astype(jnp.float32).T) > 0.5
    order = jnp.arange(segments.shape[0], dtype=jnp.int32)
    allowed = linked & (order[None, :] <= order[:, None])
    buckets = jnp.where(allowed, bucket_of(tree_depth[:, None] - tree_depth[None, :]), NB)
    prefix = (tree_depth[:, None] <= order[None, :]).astype(jnp.bfloat16)
    begins = jnp.asarray(tuple(range(16)) + bucket_marks, jnp.int32)
    edges = jnp.pad(
        tree_depth[:, None] - begins[None, :], ((0, 0), (0, 128 - NB)), constant_values=-1
    )
    return (buckets.astype(jnp.int32), prefix, edges)


def swap_kernel(peers, stride, src, dst, send_sems, recv_sems, own_sem):
    me = lax.axis_index("fsdp")
    spot, lane = me // stride, lax.rem(me, stride)
    barrier = pltpu.get_barrier_semaphore()

    def greet(step, carry):
        other = lax.rem(spot + step, peers) * stride + lane
        pl.semaphore_signal(barrier, inc=1, device_id=(other,), device_id_type=MESH)
        return carry

    lax.fori_loop(1, peers, greet, 0)
    pl.semaphore_wait(barrier, peers - 1)

    def transfer(step):
        other = lax.rem(spot + step, peers)
        return pltpu.make_async_remote_copy(
            src_ref=src.at[other],
            dst_ref=dst.at[spot],
            send_sem=send_sems.at[step],
            recv_sem=recv_sems.at[step],
            device_id=(other * stride + lane,),
            device_id_type=MESH,
        )

    def begin(step, carry):
        transfer(step).start()
        return carry

    lax.fori_loop(1, peers, begin, 0)
    own = pltpu.make_async_copy(src.at[spot], dst.at[spot], own_sem)
    own.start()

    def finish(step, carry):
        origin = lax.rem(spot + peers - step, peers)
        transfer(step).wait_send()
        pltpu.make_async_remote_copy(
            src_ref=src.at[origin],
            dst_ref=dst.at[origin],
            send_sem=send_sems.at[step],
            recv_sem=recv_sems.at[step],
            device_id=(origin * stride + lane,),
            device_id_type=MESH,
        ).wait_recv()
        return carry

    lax.fori_loop(1, peers, finish, 0)
    own.wait()


def swap_blocks(blocks, stride, call_id):
    peers = blocks.shape[0]
    return pl.pallas_call(
        functools.partial(swap_kernel, peers, stride),
        out_shape=jax.ShapeDtypeStruct(blocks.shape, blocks.dtype),
        in_specs=[pl.BlockSpec(memory_space=pl.ANY)],
        out_specs=pl.BlockSpec(memory_space=pl.ANY),
        scratch_shapes=[
            pltpu.SemaphoreType.DMA((peers,)),
            pltpu.SemaphoreType.DMA((peers,)),
            pltpu.SemaphoreType.DMA,
        ],
        compiler_params=pltpu.CompilerParams(collective_id=call_id, has_side_effects=True),
    )(blocks)


def around(step, size, at):
    return lax.rem(at + step, size)


def meet(others):
    barrier = pltpu.get_barrier_semaphore()
    for other in others:
        pl.semaphore_signal(barrier, inc=1, device_id=(other,), device_id_type=MESH)
    pl.semaphore_wait(barrier, len(others))


def chip_place(chips):
    me = lax.axis_index("fsdp")
    core = lax.rem(me, 2)
    chip = me // 2
    layers = chips // BLOCK
    layer, col = chip // BLOCK, lax.rem(chip, BLOCK)

    def device(other_layer, other_col):
        return (other_layer * BLOCK + other_col) * 2 + core

    others = [device(around(step, layers, layer), col) for step in range(1, layers)]
    others += [device(layer, around(turn, BLOCK, col)) for turn in range(1, BLOCK)]
    return layers, layer, col, device, others


def spread_kernel(chips, src, dst, layer_send, layer_recv, col_send, col_recv, own_sem):
    layers, layer, col, device, others = chip_place(chips)
    meet(others)
    chip = layer * BLOCK + col

    def to_layer(step, source, at):
        return pltpu.make_async_remote_copy(
            src_ref=source,
            dst_ref=dst.at[at],
            send_sem=layer_send.at[step],
            recv_sem=layer_recv.at[step],
            device_id=(device(around(step, layers, layer), col),),
            device_id_type=MESH,
        )

    def to_col(step, turn, source, at):
        return pltpu.make_async_remote_copy(
            src_ref=source,
            dst_ref=dst.at[at],
            send_sem=col_send.at[step, turn],
            recv_sem=col_recv.at[step, turn],
            device_id=(device(layer, around(turn, BLOCK, col)),),
            device_id_type=MESH,
        )

    for step in range(1, layers):
        to_layer(step, src, chip).start()
    for turn in range(1, BLOCK):
        to_col(0, turn, src, chip).start()
    own = pltpu.make_async_copy(src, dst.at[chip], own_sem)
    own.start()
    for step in range(1, layers):
        origin = around(layers - step, layers, layer) * BLOCK + col
        to_layer(step, src, origin).wait_recv()
        for turn in range(1, BLOCK):
            to_col(step, turn, dst.at[origin], origin).start()
    for step in range(layers):
        for turn in range(1, BLOCK):
            at = around(layers - step, layers, layer) * BLOCK + around(BLOCK - turn, BLOCK, col)
            to_col(step, turn, dst.at[at], at).wait_recv()
    for step in range(1, layers):
        to_layer(step, src, chip).wait_send()
    for step in range(layers):
        for turn in range(1, BLOCK):
            to_col(step, turn, src, chip).wait_send()
    own.wait()


def spread_rows(block, chips, call_id):
    layers = chips // BLOCK
    return pl.pallas_call(
        functools.partial(spread_kernel, chips),
        out_shape=jax.ShapeDtypeStruct((chips, *block.shape), block.dtype),
        in_specs=[pl.BlockSpec(memory_space=pl.ANY)],
        out_specs=pl.BlockSpec(memory_space=pl.ANY),
        scratch_shapes=[
            pltpu.SemaphoreType.DMA((layers,)),
            pltpu.SemaphoreType.DMA((layers,)),
            pltpu.SemaphoreType.DMA((layers, BLOCK)),
            pltpu.SemaphoreType.DMA((layers, BLOCK)),
            pltpu.SemaphoreType.DMA,
        ],
        compiler_params=pltpu.CompilerParams(collective_id=call_id, has_side_effects=True),
    )(block)


def gather_sum_kernel(
    chips, src, out, col_in, layer_out, layer_in, layer_send, layer_recv, col_send, col_recv
):
    layers, layer, col, device, others = chip_place(chips)
    meet(others)

    def to_col(step, turn):
        far = around(step, layers, layer)
        return pltpu.make_async_remote_copy(
            src_ref=src.at[far * BLOCK + around(turn, BLOCK, col)],
            dst_ref=col_in.at[step, turn],
            send_sem=col_send.at[step, turn],
            recv_sem=col_recv.at[step, turn],
            device_id=(device(layer, around(turn, BLOCK, col)),),
            device_id_type=MESH,
        )

    def to_layer(step):
        return pltpu.make_async_remote_copy(
            src_ref=layer_out.at[step],
            dst_ref=layer_in.at[step],
            send_sem=layer_send.at[step],
            recv_sem=layer_recv.at[step],
            device_id=(device(around(step, layers, layer), col),),
            device_id_type=MESH,
        )

    def block_sum(step):
        for turn in range(1, BLOCK):
            to_col(step, turn).wait_recv()
        total = src[around(step, layers, layer) * BLOCK + col].astype(jnp.float32)
        for turn in range(1, BLOCK):
            total = total + col_in[step, turn].astype(jnp.float32)
        return total

    steps = list(range(1, layers)) + [0]
    for step in steps:
        for turn in range(1, BLOCK):
            to_col(step, turn).start()
    for step in range(1, layers):
        layer_out[step] = block_sum(step).astype(jnp.bfloat16)
        to_layer(step).start()
    total = block_sum(0)
    for step in range(1, layers):
        to_layer(step).wait_recv()
        total = total + layer_in[step].astype(jnp.float32)
    out[...] = total
    for step in range(1, layers):
        to_layer(step).wait_send()
    for step in range(layers):
        for turn in range(1, BLOCK):
            to_col(step, turn).wait_send()


def gather_sum(blocks, call_id):
    chips, rows, width = blocks.shape
    layers = chips // BLOCK
    return pl.pallas_call(
        functools.partial(gather_sum_kernel, chips),
        out_shape=jax.ShapeDtypeStruct((rows, width), jnp.float32),
        in_specs=[pl.BlockSpec(memory_space=pltpu.VMEM)],
        out_specs=pl.BlockSpec(memory_space=pltpu.VMEM),
        scratch_shapes=[
            pltpu.VMEM((layers, BLOCK, rows, width), jnp.bfloat16),
            pltpu.VMEM((layers, rows, width), jnp.bfloat16),
            pltpu.VMEM((layers, rows, width), jnp.bfloat16),
            pltpu.SemaphoreType.DMA((layers,)),
            pltpu.SemaphoreType.DMA((layers,)),
            pltpu.SemaphoreType.DMA((layers, BLOCK)),
            pltpu.SemaphoreType.DMA((layers, BLOCK)),
        ],
        compiler_params=pltpu.CompilerParams(
            collective_id=call_id, has_side_effects=True, vmem_limit_bytes=56 * 1024 * 1024
        ),
    )(blocks)


def gelu_parts(values):
    root = math.sqrt(2.0 / math.pi)
    squared = values * values
    bend = jnp.tanh(root * (values + 0.044715 * (squared * values)))
    half = 0.5 * (1.0 + bend)
    slope = half + 0.5 * values * (1.0 - bend * bend) * (root * (1.0 + 0.134145 * squared))
    return values * half, slope


def trade_copies(peers, src, landed, done, returned, sems):
    me = lax.axis_index("fsdp")
    spot, lane = me // SPLIT, lax.rem(me, SPLIT)
    go_send, go_recv, back_send, back_recv = sems

    def device(other):
        return (other * SPLIT + lane,)

    def ahead(step):
        return lax.rem(spot + step, peers)

    def behind(step):
        return lax.rem(spot + peers - step, peers)

    def go(step, at):
        return pltpu.make_async_remote_copy(
            src_ref=src.at[ahead(step)],
            dst_ref=landed.at[at],
            send_sem=go_send.at[step],
            recv_sem=go_recv.at[step],
            device_id=device(ahead(step)),
            device_id_type=MESH,
        )

    def back(step, source, at):
        return pltpu.make_async_remote_copy(
            src_ref=done.at[source],
            dst_ref=returned.at[at],
            send_sem=back_send.at[step],
            recv_sem=back_recv.at[step],
            device_id=device(behind(step)),
            device_id_type=MESH,
        )

    barrier = pltpu.get_barrier_semaphore()

    def greet(step, carry):
        pl.semaphore_signal(barrier, inc=1, device_id=device(ahead(step)), device_id_type=MESH)
        return carry

    lax.fori_loop(1, peers, greet, 0)
    pl.semaphore_wait(barrier, peers - 1)
    return spot, behind, ahead, go, back


def trade_loop(peers, copies, work, own_copies):
    spot, behind, ahead, go, back = copies
    window = min(WINDOW, peers - 1)

    def begin(step, carry):
        go(step, spot).start()
        return carry

    lax.fori_loop(1, window + 1, begin, 0)
    own_in, own_out = own_copies
    own_in.start()
    own_in.wait()
    work(spot)
    own_out.start()

    def visit(step, carry):
        origin = behind(step)
        go(step, origin).wait_recv()

        @pl.when(step + window < peers)
        def _():
            go(step + window, spot).start()

        work(origin)
        back(step, origin, spot).start()
        return carry

    lax.fori_loop(1, peers, visit, 0)

    def finish(step, carry):
        go(step, spot).wait_send()
        back(step, behind(step), spot).wait_send()
        back(step, spot, ahead(step)).wait_recv()
        return carry

    lax.fori_loop(1, peers, finish, 0)
    own_out.wait()


def experts_kernel(peers, src, inward, outward, landed, returned, done, *sems):
    copies = trade_copies(peers, src, landed, done, returned, sems[:4])
    spot = copies[0]
    f32 = jnp.float32

    def work(at):
        rows = landed[at]
        total = jnp.zeros(rows.shape, f32)
        for quarter in range(SPLIT):
            before = jnp.dot(rows, inward[quarter], preferred_element_type=f32)
            hidden = gelu_parts(before)[0].astype(jnp.bfloat16)
            total = total + jnp.dot(hidden, outward[quarter], preferred_element_type=f32).astype(
                jnp.bfloat16
            ).astype(f32)
        done[at] = total.astype(jnp.bfloat16)

    trade_loop(
        peers,
        copies,
        work,
        (
            pltpu.make_async_copy(src.at[spot], landed.at[spot], sems[4]),
            pltpu.make_async_copy(done.at[spot], returned.at[spot], sems[5]),
        ),
    )


def experts_back_kernel(
    peers, src, rows_ref, inward, outward, returned, inward_grad, outward_grad, landed, done, *sems
):
    copies = trade_copies(peers, src, landed, done, returned, sems[:4])
    spot = copies[0]
    f32 = jnp.float32
    inward_grad[...] = jnp.zeros_like(inward_grad)
    outward_grad[...] = jnp.zeros_like(outward_grad)

    def work(at):
        rows = rows_ref[at]
        grads = landed[at]
        total = jnp.zeros(rows.shape, f32)
        for quarter in range(SPLIT):
            before = jnp.dot(rows, inward[quarter], preferred_element_type=f32)
            hidden, slope = gelu_parts(before)
            grad_hidden = lax.dot_general(grads, outward[quarter], NT, preferred_element_type=f32)
            grad_before = (grad_hidden * slope).astype(jnp.bfloat16)
            total = total + lax.dot_general(
                grad_before, inward[quarter], NT, preferred_element_type=f32
            ).astype(jnp.bfloat16).astype(f32)
            inward_grad[quarter] += lax.dot_general(
                rows, grad_before, TN, preferred_element_type=f32
            )
            outward_grad[quarter] += lax.dot_general(
                hidden.astype(jnp.bfloat16), grads, TN, preferred_element_type=f32
            )
        done[at] = total.astype(jnp.bfloat16)

    trade_loop(
        peers,
        copies,
        work,
        (
            pltpu.make_async_copy(src.at[spot], landed.at[spot], sems[4]),
            pltpu.make_async_copy(done.at[spot], returned.at[spot], sems[5]),
        ),
    )


def trade_call(body, call_id, outgoing, operands, outs, scratch):
    peers = outgoing.shape[0]
    anywhere = pl.BlockSpec(memory_space=pl.ANY)
    near = pl.BlockSpec(memory_space=pltpu.VMEM)
    return pl.pallas_call(
        functools.partial(body, peers),
        out_shape=[shape for shape, _ in outs],
        in_specs=[anywhere] + [near] * len(operands),
        out_specs=[near if inside else anywhere for _, inside in outs],
        scratch_shapes=scratch
        + [pltpu.SemaphoreType.DMA((peers,))] * 4
        + [pltpu.SemaphoreType.DMA] * 2,
        compiler_params=pltpu.CompilerParams(
            collective_id=call_id, has_side_effects=True, vmem_limit_bytes=60 * 1024 * 1024
        ),
    )(outgoing, *operands)


def run_experts(outgoing, inward, outward, call_id):
    same = jax.ShapeDtypeStruct(outgoing.shape, outgoing.dtype)
    return trade_call(
        experts_kernel,
        call_id,
        outgoing,
        (inward, outward),
        [(same, True), (same, False)],
        [pltpu.VMEM(outgoing.shape, outgoing.dtype)],
    )


def run_experts_back(outgoing, rows, inward, outward, call_id):
    same = jax.ShapeDtypeStruct(outgoing.shape, outgoing.dtype)
    wide = jax.ShapeDtypeStruct(inward.shape, jnp.float32)
    block = pltpu.VMEM(outgoing.shape, outgoing.dtype)
    return trade_call(
        experts_back_kernel,
        call_id,
        outgoing,
        (rows, inward, outward),
        [(same, False), (wide, True), (wide, True)],
        [block, block],
    )


def meet_all(devices):
    me = lax.axis_index("fsdp")
    barrier = pltpu.get_barrier_semaphore()

    def greet(step, carry):
        other = lax.rem(me + step, devices)
        pl.semaphore_signal(barrier, inc=1, device_id=(other,), device_id_type=MESH)
        return carry

    lax.fori_loop(1, devices, greet, 0)
    pl.semaphore_wait(barrier, devices - 1)


def swap_parts(devices, src, dst, send_sems, recv_sems, own_sem):
    me = lax.axis_index("fsdp")

    def transfer(step, at):
        other = lax.rem(me + step, devices)
        return pltpu.make_async_remote_copy(
            src_ref=src.at[other],
            dst_ref=dst.at[at],
            send_sem=send_sems.at[step],
            recv_sem=recv_sems.at[step],
            device_id=(other,),
            device_id_type=MESH,
        )

    own = pltpu.make_async_copy(src.at[me], dst.at[me], own_sem)

    def begin():
        def one(step, carry):
            transfer(step, me).start()
            return carry

        lax.fori_loop(1, devices, one, 0)
        own.start()

    def finish():
        def one(step, carry):
            transfer(step, me).wait_send()
            transfer(step, lax.rem(me + devices - step, devices)).wait_recv()
            return carry

        lax.fori_loop(1, devices, one, 0)
        own.wait()

    return begin, finish


def tail_kernel(
    chips,
    token_src,
    small_src,
    src,
    token_dst,
    small_dst,
    out,
    core_in,
    col_out,
    col_in,
    layer_out,
    layer_in,
    core_send,
    core_recv,
    layer_send,
    layer_recv,
    col_send,
    col_recv,
    *swap_sems,
):
    layers, layer, col, device, _ = chip_place(chips)
    me = lax.axis_index("fsdp")
    core = lax.rem(me, 2)
    f32 = jnp.float32
    token_begin, token_finish = swap_parts(2 * chips, token_src, token_dst, *swap_sems[:3])
    small_begin, small_finish = swap_parts(2 * chips, small_src, small_dst, *swap_sems[3:])
    meet_all(2 * chips)

    def place(step, turn):
        return around(step, layers, layer) * BLOCK + around(turn, BLOCK, col)

    def to_core(step, turn):
        return pltpu.make_async_remote_copy(
            src_ref=src.at[place(step, turn), 1 - core],
            dst_ref=core_in.at[step, turn],
            send_sem=core_send.at[step, turn],
            recv_sem=core_recv.at[step, turn],
            device_id=(me + 1 - 2 * core,),
            device_id_type=MESH,
        )

    def to_col(step, turn):
        return pltpu.make_async_remote_copy(
            src_ref=col_out.at[step, turn],
            dst_ref=col_in.at[step, turn],
            send_sem=col_send.at[step, turn],
            recv_sem=col_recv.at[step, turn],
            device_id=(device(layer, around(turn, BLOCK, col)),),
            device_id_type=MESH,
        )

    def to_layer(step):
        return pltpu.make_async_remote_copy(
            src_ref=layer_out.at[step],
            dst_ref=layer_in.at[step],
            send_sem=layer_send.at[step],
            recv_sem=layer_recv.at[step],
            device_id=(device(around(step, layers, layer), col),),
            device_id_type=MESH,
        )

    def chip_sum(step, turn):
        to_core(step, turn).wait_recv()
        return src[place(step, turn), core].astype(f32) + core_in[step, turn].astype(f32)

    def block_sum(step):
        total = chip_sum(step, 0)
        for turn in range(1, BLOCK):
            to_col(step, turn).wait_recv()
            total = total + col_in[step, turn].astype(f32)
        return total

    def step_of(number):
        return lax.rem(number + 1, layers)

    def core_begin(number, carry):
        for turn in range(BLOCK):
            to_core(step_of(number), lax.rem(turn + 1, BLOCK)).start()
        return carry

    def col_begin(number, carry):
        step = step_of(number)
        for turn in range(1, BLOCK):
            col_out[step, turn] = chip_sum(step, turn).astype(jnp.bfloat16)
            to_col(step, turn).start()
        return carry

    def layer_begin(step, carry):
        layer_out[step] = block_sum(step).astype(jnp.bfloat16)
        to_layer(step).start()
        return carry

    lax.fori_loop(0, layers, core_begin, 0)
    small_begin()
    token_begin()
    lax.fori_loop(0, layers, col_begin, 0)
    lax.fori_loop(1, layers, layer_begin, 0)
    out[...] = block_sum(0)

    def layer_finish(step, carry):
        to_layer(step).wait_recv()
        out[...] += layer_in[step].astype(f32)
        to_layer(step).wait_send()
        return carry

    def send_finish(step, carry):
        for turn in range(BLOCK):
            to_core(step, turn).wait_send()
        for turn in range(1, BLOCK):
            to_col(step, turn).wait_send()
        return carry

    lax.fori_loop(1, layers, layer_finish, 0)
    lax.fori_loop(0, layers, send_finish, 0)
    small_finish()
    token_finish()


def tail_exchange(tokens, small, blocks, call_id):
    chips, _, rows, width = blocks.shape
    layers = chips // BLOCK
    devices = 2 * chips
    near = pl.BlockSpec(memory_space=pltpu.VMEM)
    anywhere = pl.BlockSpec(memory_space=pl.ANY)
    grid_block = pltpu.VMEM((layers, BLOCK, rows, width), jnp.bfloat16)
    line_block = pltpu.VMEM((layers, rows, width), jnp.bfloat16)
    return pl.pallas_call(
        functools.partial(tail_kernel, chips),
        out_shape=[
            jax.ShapeDtypeStruct(tokens.shape, tokens.dtype),
            jax.ShapeDtypeStruct(small.shape, small.dtype),
            jax.ShapeDtypeStruct((rows, width), jnp.float32),
        ],
        in_specs=[anywhere, anywhere, near],
        out_specs=[anywhere, anywhere, near],
        scratch_shapes=[grid_block] * 3
        + [line_block] * 2
        + [pltpu.SemaphoreType.DMA((layers, BLOCK))] * 2
        + [pltpu.SemaphoreType.DMA((layers,))] * 2
        + [pltpu.SemaphoreType.DMA((layers, BLOCK))] * 2
        + [
            pltpu.SemaphoreType.DMA((devices,)),
            pltpu.SemaphoreType.DMA((devices,)),
            pltpu.SemaphoreType.DMA,
        ]
        * 2,
        compiler_params=pltpu.CompilerParams(
            collective_id=call_id, has_side_effects=True, vmem_limit_bytes=48 * 1024 * 1024
        ),
    )(tokens, small, blocks)


def head_kernel(
    chips,
    token_src,
    src,
    token_dst,
    dst,
    core_send,
    core_recv,
    layer_send,
    layer_recv,
    col_send,
    col_recv,
    own_sem,
    *swap_sems,
):
    layers, layer, col, device, _ = chip_place(chips)
    me = lax.axis_index("fsdp")
    core = lax.rem(me, 2)
    chip = layer * BLOCK + col
    token_begin, token_finish = swap_parts(2 * chips, token_src, token_dst, *swap_sems)
    meet_all(2 * chips)

    def to_layer(step, at):
        return pltpu.make_async_remote_copy(
            src_ref=src,
            dst_ref=dst.at[at, core],
            send_sem=layer_send.at[step],
            recv_sem=layer_recv.at[step],
            device_id=(device(around(step, layers, layer), col),),
            device_id_type=MESH,
        )

    def to_col(step, turn, source, at):
        return pltpu.make_async_remote_copy(
            src_ref=source,
            dst_ref=dst.at[at, core],
            send_sem=col_send.at[step, turn],
            recv_sem=col_recv.at[step, turn],
            device_id=(device(layer, around(turn, BLOCK, col)),),
            device_id_type=MESH,
        )

    def to_core(step, turn, source, at, side):
        return pltpu.make_async_remote_copy(
            src_ref=source,
            dst_ref=dst.at[at, side],
            send_sem=core_send.at[step, turn],
            recv_sem=core_recv.at[step, turn],
            device_id=(me + 1 - 2 * core,),
            device_id_type=MESH,
        )

    def origin(step, turn):
        return around(layers - step, layers, layer) * BLOCK + around(BLOCK - turn, BLOCK, col)

    def layer_start(step, carry):
        to_layer(step, chip).start()
        return carry

    lax.fori_loop(1, layers, layer_start, 0)
    for turn in range(1, BLOCK):
        to_col(0, turn, src, chip).start()
    to_core(0, 0, src, chip, core).start()
    own = pltpu.make_async_copy(src, dst.at[chip, core], own_sem)
    own.start()
    token_begin()

    def layer_pass(step, carry):
        at = origin(step, 0)
        to_layer(step, at).wait_recv()
        for turn in range(1, BLOCK):
            to_col(step, turn, dst.at[at, core], at).start()
        to_core(step, 0, dst.at[at, core], at, core).start()
        return carry

    lax.fori_loop(1, layers, layer_pass, 0)

    def col_pass(step, carry):
        for turn in range(1, BLOCK):
            at = origin(step, turn)
            to_col(step, turn, dst.at[at, core], at).wait_recv()
            to_core(step, turn, dst.at[at, core], at, core).start()
        return carry

    lax.fori_loop(0, layers, col_pass, 0)

    def layer_done(step, carry):
        to_layer(step, chip).wait_send()
        return carry

    def done(step, carry):
        for turn in range(BLOCK):
            if turn:
                to_col(step, turn, src, chip).wait_send()
            at = origin(step, turn)
            to_core(step, turn, src, at, 1 - core).wait_recv()
            to_core(step, turn, src, at, core).wait_send()
        return carry

    lax.fori_loop(1, layers, layer_done, 0)
    lax.fori_loop(0, layers, done, 0)
    own.wait()
    token_finish()


def head_exchange(tokens, block, call_id):
    devices = tokens.shape[0]
    chips = devices // 2
    layers = chips // BLOCK
    anywhere = pl.BlockSpec(memory_space=pl.ANY)
    return pl.pallas_call(
        functools.partial(head_kernel, chips),
        out_shape=[
            jax.ShapeDtypeStruct(tokens.shape, tokens.dtype),
            jax.ShapeDtypeStruct((chips, 2, *block.shape), block.dtype),
        ],
        in_specs=[anywhere] * 2,
        out_specs=[anywhere] * 2,
        scratch_shapes=[pltpu.SemaphoreType.DMA((layers, BLOCK))] * 2
        + [pltpu.SemaphoreType.DMA((layers,))] * 2
        + [pltpu.SemaphoreType.DMA((layers, BLOCK))] * 2
        + [
            pltpu.SemaphoreType.DMA,
            pltpu.SemaphoreType.DMA((devices,)),
            pltpu.SemaphoreType.DMA((devices,)),
            pltpu.SemaphoreType.DMA,
        ],
        compiler_params=pltpu.CompilerParams(collective_id=call_id, has_side_effects=True),
    )(tokens, block)


def pack_blocks(parts, devices):
    flat = jnp.concatenate(
        [jnp.broadcast_to(part, (devices, part.shape[-1])) for part in parts], axis=1
    )
    rows = -(-flat.shape[1] // 1024) * 8
    flat = jnp.pad(flat, ((0, 0), (0, rows * 128 - flat.shape[1])))
    return flat.reshape(devices, rows, 128)


def take_rows(mask, rows):
    return jnp.dot(mask.astype(jnp.bfloat16), rows, preferred_element_type=jnp.float32)


def take_rows_wide(mask, rows):
    high = lax.reduce_precision(rows, 8, 7)
    both = jnp.concatenate([high, rows - high], axis=1).astype(jnp.bfloat16)
    picked = take_rows(mask, both)
    width = rows.shape[1]
    return picked[:, :width] + picked[:, width:]


def bias_tile(table_row, buckets):
    rows, cols = buckets.shape
    spread = jnp.broadcast_to(table_row, (rows, 128))
    return jnp.concatenate(
        [
            jnp.take_along_axis(
                spread, buckets[:, at : at + 128], axis=1, mode="promise_in_bounds"
            )
            for at in range(0, cols, 128)
        ],
        axis=1,
    )


def attend_kernel(block, length, q_ref, k_ref, v_ref, bucket_ref, table_ref, out_ref, log_ref):
    lower = lax.broadcasted_iota(jnp.int32, (1, 128), 1) < 64
    pair = pl.program_id(0)
    zero = jnp.zeros((), jnp.bfloat16)
    for start in range(0, length, block):
        rows = pl.ds(start, block)
        seen = start + block
        logs = []
        mixed = []
        for half in range(2):
            mine = lower if half == 0 else ~lower
            queries = jnp.where(mine, q_ref[rows, :], zero) * 0.125
            values = jnp.where(mine, v_ref[0:seen, :], zero)
            scores = lax.dot_general(
                queries, k_ref[0:seen, :], NT, preferred_element_type=jnp.float32
            )
            table_row = table_ref[pl.ds(2 * pair + half, 1), :]
            scores = scores + bias_tile(table_row, bucket_ref[rows, 0:seen])
            peak = jnp.max(scores, axis=1, keepdims=True)
            raised = jnp.exp(scores - peak)
            totals = jnp.sum(raised, axis=1, keepdims=True)
            probs = (raised * (1.0 / totals)).astype(jnp.bfloat16)
            mixed.append(jnp.dot(probs, values, preferred_element_type=jnp.float32))
            logs.append(peak + jnp.log(totals))
        out_ref[rows, :] = (mixed[0] + mixed[1]).astype(jnp.bfloat16)
        log_ref[0, rows, :] = jnp.where(lower, logs[0], logs[1])


def attend(queries, keys, values, buckets, table, block):
    length, width = queries.shape
    cols = pl.BlockSpec((length, 128), lambda pair: (0, pair))
    return pl.pallas_call(
        functools.partial(attend_kernel, block, length),
        grid=(width // 128,),
        in_specs=[
            cols,
            cols,
            cols,
            pl.BlockSpec(buckets.shape, lambda pair: (0, 0)),
            pl.BlockSpec(table.shape, lambda pair: (0, 0)),
        ],
        out_specs=[cols, pl.BlockSpec((1, length, 128), lambda pair: (pair, 0, 0))],
        out_shape=[
            jax.ShapeDtypeStruct((length, width), jnp.bfloat16),
            jax.ShapeDtypeStruct((width // 128, length, 128), jnp.float32),
        ],
        compiler_params=pltpu.CompilerParams(vmem_limit_bytes=40 * 1024 * 1024),
    )(queries, keys, values, buckets, table)


def attend_back_kernel(
    block,
    length,
    q_ref,
    k_ref,
    v_ref,
    g_ref,
    log_ref,
    bucket_ref,
    table_ref,
    prefix_ref,
    edge_ref,
    dq_ref,
    dk_ref,
    dv_ref,
    edge_sum_ref,
    dk_acc,
    dv_acc,
):
    lower = lax.broadcasted_iota(jnp.int32, (1, 128), 1) < 64
    pair = pl.program_id(0)
    zero = jnp.zeros((), jnp.bfloat16)
    f32 = jnp.float32
    dk_acc[...] = jnp.zeros_like(dk_acc)
    dv_acc[...] = jnp.zeros_like(dv_acc)
    edge_sums = [jnp.zeros((8, 128), f32)] * 2
    for start in range(0, length, block):
        rows = pl.ds(start, block)
        seen = start + block
        edges = edge_ref[rows, :]
        lane_at = edges & 127
        dq_parts = []
        for half in range(2):
            mine = lower if half == 0 else ~lower
            queries = jnp.where(mine, q_ref[rows, :], zero) * 0.125
            grads = jnp.where(mine, g_ref[rows, :], zero)
            keys = jnp.where(mine, k_ref[0:seen, :], zero)
            scores = lax.dot_general(queries, keys, NT, preferred_element_type=f32)
            table_row = table_ref[pl.ds(2 * pair + half, 1), :]
            scores = scores + bias_tile(table_row, bucket_ref[rows, 0:seen])
            probs = jnp.exp(scores - log_ref[0, rows, 64 * half : 64 * half + 1])
            grad_probs = lax.dot_general(
                grads, v_ref[0:seen, :], NT, preferred_element_type=f32
            )
            inner_sum = jnp.sum(probs * grad_probs, axis=1, keepdims=True)
            grad_scores = (probs * (grad_probs - inner_sum)).astype(jnp.bfloat16)
            dq_parts.append(jnp.dot(grad_scores, keys, preferred_element_type=f32))
            dk_acc[0:seen, :] += lax.dot_general(
                grad_scores, queries, TN, preferred_element_type=f32
            )
            dv_acc[0:seen, :] += lax.dot_general(
                probs.astype(jnp.bfloat16), grads, TN, preferred_element_type=f32
            )
            upto = jnp.dot(grad_scores, prefix_ref[0:seen, 0:seen], preferred_element_type=f32)
            for at in range(0, seen, 128):
                read = jnp.take_along_axis(
                    upto[:, at : at + 128], lane_at, axis=1, mode="promise_in_bounds"
                )
                read = jnp.where((edges >= at) & (edges < at + 128), read, 0.0)
                edge_sums[half] = edge_sums[half] + jnp.sum(
                    read.reshape(block // 8, 8, 128), axis=0
                )
        dq_ref[rows, :] = ((dq_parts[0] + dq_parts[1]) * 0.125).astype(jnp.bfloat16)
    dk_ref[...] = dk_acc[...].astype(jnp.bfloat16)
    dv_ref[...] = dv_acc[...].astype(jnp.bfloat16)
    edge_sum_ref[0] = edge_sums[0]
    edge_sum_ref[1] = edge_sums[1]


def attend_back(queries, keys, values, grads, logs, buckets, table, prefix, edges, block):
    length, width = queries.shape
    cols = pl.BlockSpec((length, 128), lambda pair: (0, pair))
    low = jax.ShapeDtypeStruct((length, width), jnp.bfloat16)
    return pl.pallas_call(
        functools.partial(attend_back_kernel, block, length),
        grid=(width // 128,),
        in_specs=[
            cols,
            cols,
            cols,
            cols,
            pl.BlockSpec((1, length, 128), lambda pair: (pair, 0, 0)),
            pl.BlockSpec(buckets.shape, lambda pair: (0, 0)),
            pl.BlockSpec(table.shape, lambda pair: (0, 0)),
            pl.BlockSpec(prefix.shape, lambda pair: (0, 0)),
            pl.BlockSpec(edges.shape, lambda pair: (0, 0)),
        ],
        out_specs=[cols, cols, cols, pl.BlockSpec((2, 8, 128), lambda pair: (pair, 0, 0))],
        out_shape=[low, low, low, jax.ShapeDtypeStruct((width // 64, 8, 128), jnp.float32)],
        scratch_shapes=[pltpu.VMEM((length, 128), jnp.float32)] * 2,
        compiler_params=pltpu.CompilerParams(vmem_limit_bytes=48 * 1024 * 1024),
    )(queries, keys, values, grads, logs, buckets, table, prefix, edges)


def adam_step(weight, moment, square, gradient, factor):
    clipped = gradient * factor
    moment_next = 0.9 * moment + 0.1 * clipped
    square_next = 0.95 * square + 0.05 * clipped * clipped
    corrected_moment = moment_next / (1.0 - 0.9**STEP)
    corrected_square = square_next / (1.0 - 0.95**STEP)
    update = -learn_rate * (
        corrected_moment / (jnp.sqrt(corrected_square) + 1e-08)
        + weight_decay * weight.astype(jnp.float32)
    )
    return (moment_next, square_next, update)


def local(
    token_ids,
    segment_ids,
    parent_segments,
    expert_choice,
    drop_order,
    loss_positions,
    target_ids,
    embedding,
    attention_weights,
    router_weights,
    small_params,
    inward_weights,
    outward_weights,
    embedding_moment,
    embedding_square,
    attention_moment,
    attention_square,
    router_moment,
    router_square,
    params_moment,
    params_square,
    inward_moment,
    inward_square,
    outward_moment,
    outward_square,
):
    devices = lax.axis_size("fsdp")
    me = lax.axis_index("fsdp")
    length = token_ids.shape[0]
    vocab_rows, model_width = embedding.shape
    rows_loss = loss_positions.shape[0]
    experts_all = devices // SPLIT
    capacity = 9 * 2 * length // (8 * experts_all)
    slots = -(-capacity // 16) * 16
    block_rows = 128
    f32 = jnp.float32
    bf16 = jnp.bfloat16
    quads = [[SPLIT * e + q for q in range(SPLIT)] for e in range(experts_all)]
    router_size = router_weights.shape[0]
    params_size = small_params.shape[0]

    owner = token_ids // vocab_rows
    place = token_ids - owner * vocab_rows
    order = jnp.arange(length, dtype=jnp.int32)
    repeated = jnp.any(
        (token_ids[:, None] == token_ids[None, :]) & (order[None, :] < order[:, None]), axis=1
    )
    fresh = ~repeated
    rank = jnp.sum(
        (
            fresh[None, :]
            & (owner[None, :] == owner[:, None])
            & (token_ids[None, :] < token_ids[:, None])
        ).astype(jnp.int32),
        axis=1,
    )
    too_many = jnp.any(rank >= ASK).astype(f32)
    ask_row = jnp.where(rank < ASK, owner * ASK + rank, devices * ASK)
    ask_lines = jnp.arange(devices * ASK, dtype=jnp.int32)
    asked = jnp.sum(
        jnp.where(
            (ask_lines[:, None] == ask_row[None, :]) & fresh[None, :], place[None, :] + 1, 0
        ),
        axis=1,
    )
    hello = pack_blocks(
        (
            asked.reshape(devices, ASK).astype(f32),
            router_weights.astype(f32)[None],
            small_params.astype(f32)[None],
            target_ids.astype(f32).reshape(1, -1),
            too_many.reshape(1, 1),
        ),
        devices,
    )
    heard = swap_blocks(hello, 1, 1).reshape(devices, -1)
    spans = [ASK, router_size, params_size, 2 * rows_loss, 1]
    edges = [sum(spans[:i]) for i in range(len(spans) + 1)]
    wanted, router_full, params_full, targets_full, crowded = [
        heard[:, edges[i] : edges[i + 1]] for i in range(len(spans))
    ]
    wanted = wanted.reshape(-1).astype(jnp.int32) - 1
    router_full = router_full.reshape(-1).astype(bf16)
    params_full = params_full.reshape(-1)
    targets_full = targets_full.reshape(-1, 2).astype(jnp.int32)
    crowded = jnp.any(crowded > 0.5)
    inward_full = lax.all_gather(inward_weights[0], "fsdp", axis=0, axis_index_groups=quads)
    outward_full = lax.all_gather(outward_weights[0], "fsdp", axis=0, axis_index_groups=quads)

    siblings = [(device, device + 1 - 2 * (device % 2)) for device in range(devices)]
    chip_table = jnp.concatenate([embedding, lax.ppermute(embedding, "fsdp", siblings)], axis=0)

    wanted_mask = wanted[:, None] == jnp.arange(vocab_rows, dtype=jnp.int32)[None, :]
    served = take_rows(wanted_mask, embedding).astype(bf16).reshape(devices, ASK, model_width)
    attention_rows = attention_weights.shape[0]
    attention_pad = -attention_rows % 16
    served, attention_full = head_exchange(
        served, jnp.pad(attention_weights, ((0, attention_pad), (0, 0))), 2
    )
    served = served.reshape(devices * ASK, model_width)
    attention_full = attention_full[:, :, :attention_rows].reshape(-1, model_width)
    ask_mask = ask_row[:, None] == ask_lines[None, :]
    embedded_low = lax.cond(
        crowded,
        lambda: lax.all_gather(embedding, "fsdp", axis=0, tiled=True)[token_ids],
        lambda: take_rows(ask_mask, served).astype(bf16),
    )
    embedded = embedded_low.astype(f32) * math.sqrt(model_width)
    gain_first = params_full[:model_width]
    gain_second = params_full[model_width : 2 * model_width]
    gain_final = params_full[2 * model_width : 3 * model_width]
    bias_table = params_full[3 * model_width :].reshape(HEADS, NB)
    router_matrix = router_full.reshape(model_width, experts_all)
    buckets, prefix, edges = tree_layout(segment_ids, parent_segments[0])
    normed_first = rms_norm(embedded, gain_first).astype(bf16)
    queries, keys_all, values_all = [
        jnp.dot(
            normed_first,
            attention_full[part * model_width : (part + 1) * model_width],
            preferred_element_type=f32,
        ).astype(bf16)
        for part in range(3)
    ]
    bias_lines = jnp.pad(
        jnp.concatenate([bias_table, jnp.full((HEADS, 1), -1e30, f32)], axis=1),
        ((0, 16 - HEADS), (0, 127 - NB)),
    )
    mixed_all, log_totals = attend(queries, keys_all, values_all, buckets, bias_lines, block_rows)
    after_attn = embedded + jnp.dot(
        mixed_all, attention_full[3 * model_width :], preferred_element_type=f32
    )
    routed_in = rms_norm(after_attn, gain_second).astype(bf16)
    route_logits = jnp.dot(routed_in, router_matrix, preferred_element_type=f32)
    choice_onehot = (
        expert_choice[:, :, None] == jnp.arange(experts_all, dtype=jnp.int32)[None, None, :]
    ).astype(f32)
    chosen = jnp.sum(choice_onehot * route_logits[:, None, :], axis=-1)
    gate_peak = jnp.max(chosen, axis=1, keepdims=True)
    raised_gate = jnp.exp(chosen - gate_peak)
    gate_weights = raised_gate / jnp.sum(raised_gate, axis=1, keepdims=True)
    drop_rank = drop_order[0]
    flat_choice = expert_choice.reshape(-1)
    slot_index = jnp.sum(
        (
            (flat_choice[None, :] == flat_choice[:, None])
            & (drop_rank[None, :] < drop_rank[:, None])
        ).astype(jnp.int32),
        axis=1,
    ).reshape(length, 2)
    target_row = jnp.where(
        slot_index < capacity, expert_choice * slots + slot_index, experts_all * slots
    )
    slot_lines = jnp.arange(experts_all * slots, dtype=jnp.int32)
    first_out = target_row[:, 0][None, :] == slot_lines[:, None]
    second_out = target_row[:, 1][None, :] == slot_lines[:, None]
    first_in = target_row[:, 0][:, None] == slot_lines[None, :]
    second_in = target_row[:, 1][:, None] == slot_lines[None, :]
    outgoing = take_rows(first_out | second_out, routed_in).astype(bf16)
    expert_rows, returned_low = run_experts(
        outgoing.reshape(experts_all, slots, model_width), inward_full, outward_full, 7
    )
    returned_low = returned_low.reshape(experts_all * slots, model_width)
    returned_first = take_rows(first_in, returned_low)
    returned_second = take_rows(second_in, returned_low)
    after_moe = (
        after_attn + gate_weights[:, 0:1] * returned_first + gate_weights[:, 1:2] * returned_second
    )
    normed_final = rms_norm(after_moe, gain_final).astype(bf16)
    loss_mask = loss_positions[:, None] == order[None, :]
    picked = take_rows(loss_mask, normed_final).astype(bf16)
    scale_rows = 1.0 / (devices * rows_loss)

    chips = devices // 2
    core = lax.rem(me, 2)
    picked_all = spread_rows(picked, chips, 5).reshape(chips * rows_loss, model_width)
    scores = jnp.einsum("rd,vd->rv", picked_all, chip_table, preferred_element_type=f32)
    targets_here = jnp.where(
        core == 0,
        targets_full.reshape(chips, 2, rows_loss, 2)[:, 0],
        targets_full.reshape(chips, 2, rows_loss, 2)[:, 1],
    ).reshape(chips * rows_loss, 2)
    own_lines = jnp.arange(vocab_rows, dtype=jnp.int32)
    vocab_lines = jnp.concatenate(
        [own_lines + me * vocab_rows, own_lines + (me + 1 - 2 * core) * vocab_rows]
    )[None, :]
    first_hit = (targets_here[:, 0:1] == vocab_lines).astype(f32)
    second_hit = (targets_here[:, 1:2] == vocab_lines).astype(f32)
    part_peak = jnp.max(scores, axis=1)
    part_total = jnp.sum(jnp.exp(scores - part_peak[:, None]), axis=1)
    part_first = jnp.sum(first_hit * scores, axis=1)
    part_second = jnp.sum(second_hit * scores, axis=1)
    parts = swap_blocks(
        pack_blocks(
            [
                part.reshape(chips, rows_loss)
                for part in (part_peak, part_total, part_first, part_second)
            ],
            chips,
        ),
        2,
        6,
    ).reshape(chips, -1)[:, : 4 * rows_loss].reshape(chips, 4, rows_loss)
    row_peak = jnp.max(parts[:, 0], axis=0)
    row_total = jnp.sum(parts[:, 1] * jnp.exp(parts[:, 0] - row_peak[None]), axis=0)
    log_rows = row_peak + jnp.log(row_total)
    target_hits = jnp.sum(parts[:, 2:], axis=0)
    loss_local = jnp.sum(log_rows - target_hits[0] + 0.3 * (log_rows - target_hits[1]))
    log_all = (
        swap_blocks(pack_blocks((log_rows[None],), chips), 2, 3)
        .reshape(chips, -1)[:, :rows_loss]
        .reshape(-1)
    )
    pull = 1.3 * jnp.exp(scores - log_all[:, None]) - first_hit - 0.3 * second_hit
    pull = (pull * scale_rows).astype(bf16)
    picked_parts = jnp.dot(pull, chip_table, preferred_element_type=f32).astype(bf16)
    picked_grad = gather_sum(picked_parts.reshape(chips, rows_loss, model_width), 4)
    chip_grad = jnp.einsum("rv,rd->vd", pull, picked_all, preferred_element_type=f32)
    table_grad = chip_grad[:vocab_rows] + lax.ppermute(
        chip_grad[vocab_rows:], "fsdp", siblings
    )
    grad_normed = take_rows_wide(loss_mask.T, picked_grad)
    _, final_back = jax.vjp(rms_norm, after_moe, gain_final)
    grad_after_moe, grad_gain_final = final_back(grad_normed)
    grad_gates = jnp.stack(
        [
            jnp.sum(returned_first * grad_after_moe, axis=-1),
            jnp.sum(returned_second * grad_after_moe, axis=-1),
        ],
        axis=1,
    )
    grad_chosen = gate_weights * (
        grad_gates - jnp.sum(gate_weights * grad_gates, axis=1, keepdims=True)
    )
    grad_route = jnp.sum(choice_onehot * grad_chosen[:, :, None], axis=1).astype(bf16)
    router_grad = jnp.einsum(
        "td,te->de", routed_in, grad_route, preferred_element_type=f32
    ).reshape(-1)
    grad_routed = jnp.einsum("te,de->td", grad_route, router_matrix, preferred_element_type=f32)
    grad_slots = take_rows(
        first_out, (gate_weights[:, 0:1] * grad_after_moe).astype(bf16)
    ) + take_rows(second_out, (gate_weights[:, 1:2] * grad_after_moe).astype(bf16))
    grad_returned, inward_parts, outward_parts = run_experts_back(
        grad_slots.astype(bf16).reshape(experts_all, slots, model_width),
        expert_rows,
        inward_full,
        outward_full,
        8,
    )
    grad_returned = grad_returned.reshape(experts_all * slots, model_width)
    inward_grad = lax.psum_scatter(
        inward_parts, "fsdp", scatter_dimension=0, axis_index_groups=quads
    )[None]
    outward_grad = lax.psum_scatter(
        outward_parts, "fsdp", scatter_dimension=0, axis_index_groups=quads
    )[None]
    grad_routed = grad_routed + take_rows(first_in | second_in, grad_returned)
    _, second_back = jax.vjp(rms_norm, after_attn, gain_second)
    grad_norm_in, grad_gain_second = second_back(grad_routed)
    grad_after_attn = grad_after_moe + grad_norm_in
    grad_attn_low = grad_after_attn.astype(bf16)
    output_grad = jnp.einsum("td,te->de", mixed_all, grad_attn_low, preferred_element_type=f32)
    grad_mixed = jnp.einsum(
        "te,de->td", grad_attn_low, attention_full[3 * model_width :], preferred_element_type=f32
    ).astype(bf16)
    grad_queries_low, grad_keys_low, grad_values_low, edge_sums = attend_back(
        queries,
        keys_all,
        values_all,
        grad_mixed,
        log_totals,
        buckets,
        bias_lines,
        prefix,
        edges,
        block_rows,
    )
    edge_sums = jnp.sum(edge_sums, axis=1)[:, :NB]
    grad_bias = edge_sums - jnp.pad(edge_sums[:, 1:], ((0, 0), (0, 1)))
    projection_grads = []
    grad_normed_first = jnp.zeros((length, model_width), f32)
    for position, gradient_low in enumerate((grad_queries_low, grad_keys_low, grad_values_low)):
        projection_grads.append(
            jnp.einsum("td,te->de", normed_first, gradient_low, preferred_element_type=f32)
        )
        grad_normed_first = grad_normed_first + jnp.einsum(
            "te,de->td",
            gradient_low,
            attention_full[position * model_width : (position + 1) * model_width],
            preferred_element_type=f32,
        )
    attention_grad = jnp.concatenate(projection_grads + [output_grad], axis=0)
    _, first_back = jax.vjp(rms_norm, embedded, gain_first)
    grad_embed_in, grad_gain_first = first_back(grad_normed_first)
    grad_embedded = (grad_after_attn + grad_embed_in) * math.sqrt(model_width)
    params_grad = jnp.concatenate(
        [grad_gain_first, grad_gain_second, grad_gain_final, grad_bias.reshape(-1)]
    )
    ask_sums = take_rows_wide(ask_mask.T, grad_embedded).astype(bf16)
    attention_blocks = jnp.pad(
        attention_grad.astype(bf16).reshape(devices // 2, 2, attention_rows, model_width),
        ((0, 0), (0, 0), (0, attention_pad), (0, 0)),
    )
    small_blocks = pack_blocks(
        (router_grad.reshape(devices, router_size), params_grad.reshape(devices, params_size)),
        devices,
    )
    ask_sums, small_sums, attention_share = tail_exchange(
        ask_sums.reshape(devices, ASK, model_width), small_blocks, attention_blocks, 9
    )
    attention_share = attention_share[:attention_rows]
    small_share = jnp.sum(small_sums.reshape(devices, -1), axis=0)

    def lookup_wide():
        whole = jnp.zeros((devices * vocab_rows, model_width), f32).at[token_ids].add(grad_embedded)
        return lax.psum_scatter(whole, "fsdp", scatter_dimension=0, tiled=True)

    table_share = table_grad + lax.cond(
        crowded,
        lookup_wide,
        lambda: take_rows(wanted_mask.T, ask_sums.reshape(devices * ASK, model_width)),
    )
    router_share = small_share[:router_size]
    params_share = small_share[router_size : router_size + params_size]
    local_square = (
        jnp.sum(table_share * table_share)
        + jnp.sum(attention_share * attention_share)
        + jnp.sum(router_share * router_share)
        + jnp.sum(params_share * params_share)
        + jnp.sum(inward_grad * inward_grad)
        + jnp.sum(outward_grad * outward_grad)
    )
    total_square = jnp.sum(
        swap_blocks(pack_blocks((local_square.reshape(1, 1),), devices), 1, 11).reshape(devices, -1)[
            :, 0
        ]
    )
    grad_norm = jnp.sqrt(total_square)
    threshold = clip_base / math.sqrt(devices * rows_loss)
    factor = jnp.minimum(1.0, threshold / grad_norm)
    loss_parts = (loss_local * scale_rows).reshape(1)
    table_m, table_s, table_u = adam_step(
        embedding, embedding_moment, embedding_square, table_share, factor
    )
    attention_m, attention_s, attention_u = adam_step(
        attention_weights, attention_moment, attention_square, attention_share, factor
    )
    router_m, router_s, router_u = adam_step(
        router_weights, router_moment, router_square, router_share, factor
    )
    params_m, params_s, params_u = adam_step(
        small_params, params_moment, params_square, params_share, factor
    )
    inward_m, inward_s, inward_u = adam_step(
        inward_weights, inward_moment, inward_square, inward_grad, factor
    )
    outward_m, outward_s, outward_u = adam_step(
        outward_weights, outward_moment, outward_square, outward_grad, factor
    )
    return (
        loss_parts,
        grad_norm,
        table_m,
        table_s,
        table_u,
        attention_m,
        attention_s,
        attention_u,
        router_m,
        router_s,
        router_u,
        params_m,
        params_s,
        params_u,
        inward_m,
        inward_s,
        inward_u,
        outward_m,
        outward_s,
        outward_u,
    )


def solution(mesh):
    placed = (
        P("fsdp"),
        P("fsdp"),
        P("fsdp", None),
        P("fsdp", None),
        P("fsdp", None),
        P("fsdp"),
        P("fsdp", None),
        P("fsdp", None),
        P("fsdp", None),
        P("fsdp"),
        P("fsdp"),
        P("fsdp", None, None),
        P("fsdp", None, None),
        P("fsdp", None),
        P("fsdp", None),
        P("fsdp", None),
        P("fsdp", None),
        P("fsdp"),
        P("fsdp"),
        P("fsdp"),
        P("fsdp"),
        P("fsdp", None, None),
        P("fsdp", None, None),
        P("fsdp", None, None),
        P("fsdp", None, None),
    )
    return jax.shard_map(
        local,
        mesh=mesh,
        in_specs=placed,
        out_specs=(
            P("fsdp"),
            P(),
            P("fsdp", None),
            P("fsdp", None),
            P("fsdp", None),
            P("fsdp", None),
            P("fsdp", None),
            P("fsdp", None),
            P("fsdp"),
            P("fsdp"),
            P("fsdp"),
            P("fsdp"),
            P("fsdp"),
            P("fsdp"),
            P("fsdp", None, None),
            P("fsdp", None, None),
            P("fsdp", None, None),
            P("fsdp", None, None),
            P("fsdp", None, None),
            P("fsdp", None, None),
        ),
        check_vma=False,
    )
```

```python
import functools
import math

import jax
import jax.numpy as jnp
from jax import lax
from jax.experimental import pallas as pl
from jax.experimental.pallas import tpu as pltpu
from jax.sharding import PartitionSpec as P

HEADS = 12
NB = 32
SPLIT = 4
STEP = 10
ASK = 48
BLOCK = 4
WINDOW = 3
NT = (((1,), (1,)), ((), ()))
TN = (((0,), (0,)), ((), ()))
MESH = pl.DeviceIdType.MESH


bucket_marks = (16, 23, 32, 45, 64, 91, 128, 181, 256, 362, 512, 724, 1024, 1448, 2048, 2896)
learn_rate = 0.02
weight_decay = 0.1
clip_base = 8.0


def rms_norm(values, gains):
    return values * lax.rsqrt(jnp.mean(values * values, axis=-1, keepdims=True) + 1e-06) * gains


def bucket_of(distance):
    distance = jnp.maximum(distance, 0)
    bucket = jnp.minimum(distance, 15)
    for border in bucket_marks:
        bucket = bucket + (distance >= border).astype(jnp.int32)
    return bucket


def tree_layout(segments, parents):
    segment_count = parents.shape[0]
    identity_rows = jnp.eye(segment_count, dtype=jnp.float32)
    parent_rows = (parents[:, None] == jnp.arange(segment_count, dtype=jnp.int32)[None, :]).astype(
        jnp.float32
    )
    ancestry = jnp.minimum(identity_rows + parent_rows, 1.0)
    reached = 1
    while reached < segment_count - 1:
        ancestry = jnp.minimum(jnp.dot(ancestry, ancestry), 1.0)
        reached = 2 * reached
    member = (segments[:, None] == jnp.arange(segment_count, dtype=jnp.int32)[None, :]).astype(
        jnp.int32
    )
    lengths = jnp.sum(member, axis=0)
    starts = jnp.cumsum(lengths) - lengths
    before = jnp.sum((ancestry - identity_rows).astype(jnp.int32) * lengths[None, :], axis=1)
    tree_depth = jnp.sum(member * (before - starts)[None, :], axis=1) + jnp.arange(
        segments.shape[0], dtype=jnp.int32
    )
    reach_rows = jnp.dot(member.astype(jnp.float32), ancestry)
    linked = jnp.dot(reach_rows, member.astype(jnp.float32).T) > 0.5
    order = jnp.arange(segments.shape[0], dtype=jnp.int32)
    allowed = linked & (order[None, :] <= order[:, None])
    buckets = jnp.where(allowed, bucket_of(tree_depth[:, None] - tree_depth[None, :]), NB)
    prefix = (tree_depth[:, None] <= order[None, :]).astype(jnp.bfloat16)
    begins = jnp.asarray(tuple(range(16)) + bucket_marks, jnp.int32)
    edges = jnp.pad(
        tree_depth[:, None] - begins[None, :], ((0, 0), (0, 128 - NB)), constant_values=-1
    )
    return (buckets.astype(jnp.int32), prefix, edges)


def swap_kernel(peers, stride, src, dst, send_sems, recv_sems, own_sem):
    me = lax.axis_index("fsdp")
    spot, lane = me // stride, lax.rem(me, stride)
    barrier = pltpu.get_barrier_semaphore()

    def greet(step, carry):
        other = lax.rem(spot + step, peers) * stride + lane
        pl.semaphore_signal(barrier, inc=1, device_id=(other,), device_id_type=MESH)
        return carry

    lax.fori_loop(1, peers, greet, 0)
    pl.semaphore_wait(barrier, peers - 1)

    def transfer(step):
        other = lax.rem(spot + step, peers)
        return pltpu.make_async_remote_copy(
            src_ref=src.at[other],
            dst_ref=dst.at[spot],
            send_sem=send_sems.at[step],
            recv_sem=recv_sems.at[step],
            device_id=(other * stride + lane,),
            device_id_type=MESH,
        )

    def begin(step, carry):
        transfer(step).start()
        return carry

    lax.fori_loop(1, peers, begin, 0)
    own = pltpu.make_async_copy(src.at[spot], dst.at[spot], own_sem)
    own.start()

    def finish(step, carry):
        origin = lax.rem(spot + peers - step, peers)
        transfer(step).wait_send()
        pltpu.make_async_remote_copy(
            src_ref=src.at[origin],
            dst_ref=dst.at[origin],
            send_sem=send_sems.at[step],
            recv_sem=recv_sems.at[step],
            device_id=(origin * stride + lane,),
            device_id_type=MESH,
        ).wait_recv()
        return carry

    lax.fori_loop(1, peers, finish, 0)
    own.wait()


def swap_blocks(blocks, stride, call_id):
    peers = blocks.shape[0]
    return pl.pallas_call(
        functools.partial(swap_kernel, peers, stride),
        out_shape=jax.ShapeDtypeStruct(blocks.shape, blocks.dtype),
        in_specs=[pl.BlockSpec(memory_space=pl.ANY)],
        out_specs=pl.BlockSpec(memory_space=pl.ANY),
        scratch_shapes=[
            pltpu.SemaphoreType.DMA((peers,)),
            pltpu.SemaphoreType.DMA((peers,)),
            pltpu.SemaphoreType.DMA,
        ],
        compiler_params=pltpu.CompilerParams(collective_id=call_id, has_side_effects=True),
    )(blocks)


def around(step, size, at):
    return lax.rem(at + step, size)


def meet(others):
    barrier = pltpu.get_barrier_semaphore()
    for other in others:
        pl.semaphore_signal(barrier, inc=1, device_id=(other,), device_id_type=MESH)
    pl.semaphore_wait(barrier, len(others))


def chip_place(chips):
    me = lax.axis_index("fsdp")
    core = lax.rem(me, 2)
    chip = me // 2
    layers = chips // BLOCK
    layer, col = chip // BLOCK, lax.rem(chip, BLOCK)

    def device(other_layer, other_col):
        return (other_layer * BLOCK + other_col) * 2 + core

    others = [device(around(step, layers, layer), col) for step in range(1, layers)]
    others += [device(layer, around(turn, BLOCK, col)) for turn in range(1, BLOCK)]
    return layers, layer, col, device, others


def loss_kernel(
    chips,
    scale,
    picked,
    table,
    table_t,
    ids,
    targets,
    out,
    table_grad,
    loss_rows,
    rows,
    scores,
    pulls,
    picks,
    stat_out,
    stat_in,
    log_out,
    log_in,
    col_in,
    layer_out,
    layer_in,
    own_sem,
    layer_send,
    layer_recv,
    col_send,
    col_recv,
    sum_layer_send,
    sum_layer_recv,
    sum_col_send,
    sum_col_recv,
    stat_send,
    stat_recv,
    log_send,
    log_recv,
):
    layers, layer, col, device, _ = chip_place(chips)
    core = lax.rem(lax.axis_index("fsdp"), 2)
    chip = layer * BLOCK + col
    f32 = jnp.float32
    bf16 = jnp.bfloat16
    count, width = picked.shape
    group = BLOCK * count
    lines_all = table.shape[0]
    lines_step = min(512, lines_all)
    line_steps = lines_all // lines_step
    barrier = pltpu.get_barrier_semaphore()

    def far_chip(shift):
        return lax.rem(chip + shift, chips)

    def greet(shift, carry):
        pl.semaphore_signal(
            barrier, inc=1, device_id=(far_chip(shift) * 2 + core,), device_id_type=MESH
        )
        return carry

    lax.fori_loop(1, chips, greet, 0)
    pl.semaphore_wait(barrier, chips - 1)

    def to_layer(step, at):
        return pltpu.make_async_remote_copy(
            src_ref=picked,
            dst_ref=rows.at[at],
            send_sem=layer_send.at[step],
            recv_sem=layer_recv.at[step],
            device_id=(device(around(step, layers, layer), col),),
            device_id_type=MESH,
        )

    def to_col(step, turn, source, at):
        return pltpu.make_async_remote_copy(
            src_ref=source,
            dst_ref=rows.at[at],
            send_sem=col_send.at[step, turn],
            recv_sem=col_recv.at[step, turn],
            device_id=(device(layer, around(turn, BLOCK, col)),),
            device_id_type=MESH,
        )

    def origin(step, turn):
        return around(layers - step, layers, layer) * BLOCK + around(BLOCK - turn, BLOCK, col)

    def layer_start(step, carry):
        to_layer(step, chip).start()
        return carry

    lax.fori_loop(1, layers, layer_start, 0)
    for turn in range(1, BLOCK):
        to_col(0, turn, picked, chip).start()
    own = pltpu.make_async_copy(picked, rows.at[chip], own_sem)
    own.start()
    table_grad[...] = jnp.zeros_like(table_grad)
    stat_out[...] = jnp.zeros_like(stat_out)
    own.wait()

    def lines_of(number):
        return pl.ds(pl.multiple_of(number * lines_step, lines_step), lines_step)

    def layer_rows(far):
        return rows[pl.ds(far * BLOCK, BLOCK)].reshape(group, width)

    def score(lines, block):
        values = lax.dot_general(table[lines, :], block, NT, preferred_element_type=f32)
        return jnp.where(ids[lines, :] >= 0, values, -1e30)

    def to_owner(at):
        return pltpu.make_async_remote_copy(
            src_ref=stat_out.at[at],
            dst_ref=stat_in.at[chip],
            send_sem=stat_send.at[at],
            recv_sem=stat_recv.at[chip],
            device_id=(at * 2 + core,),
            device_id_type=MESH,
        )

    def from_chip(at):
        return pltpu.make_async_remote_copy(
            src_ref=stat_out.at[at],
            dst_ref=stat_in.at[at],
            send_sem=stat_send.at[at],
            recv_sem=stat_recv.at[at],
            device_id=(at * 2 + core,),
            device_id_type=MESH,
        )

    def measure(step, far):
        block = layer_rows(far)
        first = targets[far, 0:1, :]
        second = targets[far, 1:2, :]

        def peak_of(number, peak):
            lines = lines_of(number)
            values = score(lines, block)
            scores[lines, :] = values
            return jnp.maximum(peak, jnp.max(values, axis=0, keepdims=True))

        peak = lax.fori_loop(0, line_steps, peak_of, jnp.full((1, group), -1e30, f32))

        def total_of(number, carry):
            total, first_sum, second_sum = carry
            lines = lines_of(number)
            values = scores[lines, :]
            vocab = ids[lines, :]
            total = total + jnp.sum(jnp.exp(values - peak), axis=0, keepdims=True)
            first_sum = first_sum + jnp.sum(
                jnp.where(vocab == first, values, 0.0), axis=0, keepdims=True
            )
            second_sum = second_sum + jnp.sum(
                jnp.where(vocab == second, values, 0.0), axis=0, keepdims=True
            )
            return total, first_sum, second_sum

        zero = jnp.zeros((1, group), f32)
        sums = lax.fori_loop(0, line_steps, total_of, (zero, zero, zero))
        for part in range(BLOCK):
            lanes = slice(part * count, (part + 1) * count)
            at = far * BLOCK + part
            stat_out[at, 0:1, :] = peak[:, lanes]
            for number in range(3):
                stat_out[at, number + 1 : number + 2, :] = sums[number][:, lanes]

            @pl.when(jnp.logical_or(step != 0, part != col))
            def _():
                to_owner(at).start()

    def layer_pass(step, carry):
        at = origin(step, 0)

        @pl.when(step > 0)
        def _():
            to_layer(step, at).wait_recv()
            for turn in range(1, BLOCK):
                to_col(step, turn, rows.at[at], at).start()

        return carry

    def layer_measure(step, carry):
        for turn in range(1, BLOCK):
            at = origin(step, turn)
            to_col(step, turn, rows.at[at], at).wait_recv()
        measure(step, around(layers - step, layers, layer))
        return carry

    lax.fori_loop(0, layers, layer_pass, 0)
    lax.fori_loop(0, layers, layer_measure, 0)
    stat_in[chip] = stat_out[chip]

    def stat_wait(shift, carry):
        from_chip(far_chip(shift)).wait_recv()
        return carry

    lax.fori_loop(1, chips, stat_wait, 0)
    peaks = stat_in[:, 0, :]
    peak = jnp.max(peaks, axis=0, keepdims=True)
    total = jnp.sum(stat_in[:, 1, :] * jnp.exp(peaks - peak), axis=0, keepdims=True)
    first_hit = jnp.sum(stat_in[:, 2, :], axis=0, keepdims=True)
    second_hit = jnp.sum(stat_in[:, 3, :], axis=0, keepdims=True)
    log_rows = peak + jnp.log(total)
    loss_rows[...] = jnp.broadcast_to(
        log_rows - first_hit + 0.3 * (log_rows - second_hit), loss_rows.shape
    )
    log_out[...] = jnp.broadcast_to(log_rows, log_out.shape)
    log_in[chip] = log_out[...]

    def to_chip(shift, at):
        return pltpu.make_async_remote_copy(
            src_ref=log_out,
            dst_ref=log_in.at[at],
            send_sem=log_send.at[shift],
            recv_sem=log_recv.at[at],
            device_id=(far_chip(shift) * 2 + core,),
            device_id_type=MESH,
        )

    def log_begin(shift, carry):
        to_chip(shift, chip).start()
        return carry

    def log_wait(shift, carry):
        to_chip(shift, far_chip(shift)).wait_recv()
        return carry

    lax.fori_loop(1, chips, log_begin, 0)
    lax.fori_loop(1, chips, log_wait, 0)

    def pull_back(step):
        far = around(step, layers, layer)
        block = layer_rows(far)
        first = targets[far, 0:1, :]
        second = targets[far, 1:2, :]
        logs = jnp.concatenate(
            [log_in[far * BLOCK + part, 0:1, :] for part in range(BLOCK)], axis=1
        )

        def pull_of(number, carry):
            lines = lines_of(number)
            vocab = ids[lines, :]
            pull = (
                1.3 * jnp.exp(score(lines, block) - logs)
                - (vocab == first).astype(f32)
                - 0.3 * (vocab == second).astype(f32)
            )
            pull = (pull * scale).astype(bf16)
            pulls[lines, :] = pull
            table_grad[lines, :] += jnp.dot(pull, block, preferred_element_type=f32)
            return carry

        lax.fori_loop(0, line_steps, pull_of, 0)
        grads = jnp.dot(table_t[...], pulls[...], preferred_element_type=f32).astype(bf16)
        for part in range(BLOCK):
            picks[step, part] = grads[:, part * count : (part + 1) * count]

    def sum_to_col(step, turn):
        return pltpu.make_async_remote_copy(
            src_ref=picks.at[step, around(turn, BLOCK, col)],
            dst_ref=col_in.at[step, turn],
            send_sem=sum_col_send.at[step, turn],
            recv_sem=sum_col_recv.at[step, turn],
            device_id=(device(layer, around(turn, BLOCK, col)),),
            device_id_type=MESH,
        )

    def sum_to_layer(step):
        return pltpu.make_async_remote_copy(
            src_ref=layer_out.at[step],
            dst_ref=layer_in.at[step],
            send_sem=sum_layer_send.at[step],
            recv_sem=sum_layer_recv.at[step],
            device_id=(device(around(step, layers, layer), col),),
            device_id_type=MESH,
        )

    def block_sum(step):
        total = picks[step, col].astype(f32)
        for turn in range(1, BLOCK):
            sum_to_col(step, turn).wait_recv()
            total = total + col_in[step, turn].astype(f32)
        return total

    def pull_pass(number, carry):
        step = lax.rem(number + 1, layers)
        pull_back(step)
        for turn in range(1, BLOCK):
            sum_to_col(step, turn).start()

        @pl.when(number > 0)
        def _():
            layer_out[number] = block_sum(number).astype(bf16)
            sum_to_layer(number).start()

        return carry

    lax.fori_loop(0, layers, pull_pass, 0)
    out[...] = block_sum(0)

    def layer_finish(step, carry):
        sum_to_layer(step).wait_recv()
        out[...] += layer_in[step].astype(f32)
        sum_to_layer(step).wait_send()
        to_layer(step, chip).wait_send()
        return carry

    def col_finish(step, carry):
        for turn in range(1, BLOCK):
            to_col(step, turn, picked, chip).wait_send()
            sum_to_col(step, turn).wait_send()
        return carry

    def small_finish(shift, carry):
        from_chip(far_chip(shift)).wait_send()
        to_chip(shift, chip).wait_send()
        return carry

    lax.fori_loop(1, layers, layer_finish, 0)
    lax.fori_loop(0, layers, col_finish, 0)
    lax.fori_loop(1, chips, small_finish, 0)


def loss_exchange(picked, table, ids, targets, chips, scale, call_id):
    count, width = picked.shape
    layers = chips // BLOCK
    group = BLOCK * count
    lines_all = table.shape[0]
    f32 = jnp.float32
    bf16 = jnp.bfloat16
    near = pl.BlockSpec(memory_space=pltpu.VMEM)
    return pl.pallas_call(
        functools.partial(loss_kernel, chips, scale),
        out_shape=[
            jax.ShapeDtypeStruct((width, count), f32),
            jax.ShapeDtypeStruct((lines_all, width), f32),
            jax.ShapeDtypeStruct((8, count), f32),
        ],
        in_specs=[pl.BlockSpec(memory_space=pl.ANY)] + [near] * 4,
        out_specs=[near] * 3,
        scratch_shapes=[
            pltpu.VMEM((chips, count, width), bf16),
            pltpu.VMEM((lines_all, group), f32),
            pltpu.VMEM((lines_all, group), bf16),
            pltpu.VMEM((layers, BLOCK, width, count), bf16),
            pltpu.VMEM((chips, 8, count), f32),
            pltpu.VMEM((chips, 8, count), f32),
            pltpu.VMEM((8, count), f32),
            pltpu.VMEM((chips, 8, count), f32),
            pltpu.VMEM((layers, BLOCK, width, count), bf16),
            pltpu.VMEM((layers, width, count), bf16),
            pltpu.VMEM((layers, width, count), bf16),
            pltpu.SemaphoreType.DMA,
        ]
        + (
            [pltpu.SemaphoreType.DMA((layers,))] * 2
            + [pltpu.SemaphoreType.DMA((layers, BLOCK))] * 2
        )
        * 2
        + [pltpu.SemaphoreType.DMA((chips,))] * 4,
        compiler_params=pltpu.CompilerParams(
            collective_id=call_id, has_side_effects=True, vmem_limit_bytes=60 * 1024 * 1024
        ),
    )(picked, table, table.T, ids, targets)


def gelu_parts(values):
    root = math.sqrt(2.0 / math.pi)
    squared = values * values
    bend = jnp.tanh(root * (values + 0.044715 * (squared * values)))
    half = 0.5 * (1.0 + bend)
    slope = half + 0.5 * values * (1.0 - bend * bend) * (root * (1.0 + 0.134145 * squared))
    return values * half, slope


def trade_copies(peers, src, landed, done, returned, sems):
    me = lax.axis_index("fsdp")
    spot, lane = me // SPLIT, lax.rem(me, SPLIT)
    go_send, go_recv, back_send, back_recv = sems

    def device(other):
        return (other * SPLIT + lane,)

    def ahead(step):
        return lax.rem(spot + step, peers)

    def behind(step):
        return lax.rem(spot + peers - step, peers)

    def go(step, at):
        return pltpu.make_async_remote_copy(
            src_ref=src.at[ahead(step)],
            dst_ref=landed.at[at],
            send_sem=go_send.at[step],
            recv_sem=go_recv.at[step],
            device_id=device(ahead(step)),
            device_id_type=MESH,
        )

    def back(step, source, at):
        return pltpu.make_async_remote_copy(
            src_ref=done.at[source],
            dst_ref=returned.at[at],
            send_sem=back_send.at[step],
            recv_sem=back_recv.at[step],
            device_id=device(behind(step)),
            device_id_type=MESH,
        )

    barrier = pltpu.get_barrier_semaphore()

    def greet(step, carry):
        pl.semaphore_signal(barrier, inc=1, device_id=device(ahead(step)), device_id_type=MESH)
        return carry

    lax.fori_loop(1, peers, greet, 0)
    pl.semaphore_wait(barrier, peers - 1)
    return spot, behind, ahead, go, back


def trade_loop(peers, copies, work, own_copies):
    spot, behind, ahead, go, back = copies
    window = min(WINDOW, peers - 1)

    def begin(step, carry):
        go(step, spot).start()
        return carry

    lax.fori_loop(1, window + 1, begin, 0)
    own_in, own_out = own_copies
    own_in.start()
    own_in.wait()
    work(spot)
    own_out.start()

    def visit(step, carry):
        origin = behind(step)
        go(step, origin).wait_recv()

        @pl.when(step + window < peers)
        def _():
            go(step + window, spot).start()

        work(origin)
        back(step, origin, spot).start()
        return carry

    lax.fori_loop(1, peers, visit, 0)

    def finish(step, carry):
        go(step, spot).wait_send()
        back(step, behind(step), spot).wait_send()
        back(step, spot, ahead(step)).wait_recv()
        return carry

    lax.fori_loop(1, peers, finish, 0)
    own_out.wait()


def experts_kernel(peers, src, inward, outward, landed, returned, done, *sems):
    copies = trade_copies(peers, src, landed, done, returned, sems[:4])
    spot = copies[0]
    f32 = jnp.float32

    def work(at):
        rows = landed[at]
        total = jnp.zeros(rows.shape, f32)
        for quarter in range(SPLIT):
            before = jnp.dot(rows, inward[quarter], preferred_element_type=f32)
            hidden = gelu_parts(before)[0].astype(jnp.bfloat16)
            total = total + jnp.dot(hidden, outward[quarter], preferred_element_type=f32).astype(
                jnp.bfloat16
            ).astype(f32)
        done[at] = total.astype(jnp.bfloat16)

    trade_loop(
        peers,
        copies,
        work,
        (
            pltpu.make_async_copy(src.at[spot], landed.at[spot], sems[4]),
            pltpu.make_async_copy(done.at[spot], returned.at[spot], sems[5]),
        ),
    )


def experts_back_kernel(
    peers, src, rows_ref, inward, outward, returned, inward_grad, outward_grad, landed, done, *sems
):
    copies = trade_copies(peers, src, landed, done, returned, sems[:4])
    spot = copies[0]
    f32 = jnp.float32
    inward_grad[...] = jnp.zeros_like(inward_grad)
    outward_grad[...] = jnp.zeros_like(outward_grad)

    def work(at):
        rows = rows_ref[at]
        grads = landed[at]
        total = jnp.zeros(rows.shape, f32)
        for quarter in range(SPLIT):
            before = jnp.dot(rows, inward[quarter], preferred_element_type=f32)
            hidden, slope = gelu_parts(before)
            grad_hidden = lax.dot_general(grads, outward[quarter], NT, preferred_element_type=f32)
            grad_before = (grad_hidden * slope).astype(jnp.bfloat16)
            total = total + lax.dot_general(
                grad_before, inward[quarter], NT, preferred_element_type=f32
            ).astype(jnp.bfloat16).astype(f32)
            inward_grad[quarter] += lax.dot_general(
                rows, grad_before, TN, preferred_element_type=f32
            )
            outward_grad[quarter] += lax.dot_general(
                hidden.astype(jnp.bfloat16), grads, TN, preferred_element_type=f32
            )
        done[at] = total.astype(jnp.bfloat16)

    trade_loop(
        peers,
        copies,
        work,
        (
            pltpu.make_async_copy(src.at[spot], landed.at[spot], sems[4]),
            pltpu.make_async_copy(done.at[spot], returned.at[spot], sems[5]),
        ),
    )


def trade_call(body, call_id, outgoing, operands, outs, scratch):
    peers = outgoing.shape[0]
    anywhere = pl.BlockSpec(memory_space=pl.ANY)
    near = pl.BlockSpec(memory_space=pltpu.VMEM)
    return pl.pallas_call(
        functools.partial(body, peers),
        out_shape=[shape for shape, _ in outs],
        in_specs=[anywhere] + [near] * len(operands),
        out_specs=[near if inside else anywhere for _, inside in outs],
        scratch_shapes=scratch
        + [pltpu.SemaphoreType.DMA((peers,))] * 4
        + [pltpu.SemaphoreType.DMA] * 2,
        compiler_params=pltpu.CompilerParams(
            collective_id=call_id, has_side_effects=True, vmem_limit_bytes=60 * 1024 * 1024
        ),
    )(outgoing, *operands)


def run_experts(outgoing, inward, outward, call_id):
    same = jax.ShapeDtypeStruct(outgoing.shape, outgoing.dtype)
    return trade_call(
        experts_kernel,
        call_id,
        outgoing,
        (inward, outward),
        [(same, True), (same, False)],
        [pltpu.VMEM(outgoing.shape, outgoing.dtype)],
    )


def run_experts_back(outgoing, rows, inward, outward, call_id):
    same = jax.ShapeDtypeStruct(outgoing.shape, outgoing.dtype)
    wide = jax.ShapeDtypeStruct(inward.shape, jnp.float32)
    block = pltpu.VMEM(outgoing.shape, outgoing.dtype)
    return trade_call(
        experts_back_kernel,
        call_id,
        outgoing,
        (rows, inward, outward),
        [(same, False), (wide, True), (wide, True)],
        [block, block],
    )


def meet_all(devices):
    me = lax.axis_index("fsdp")
    barrier = pltpu.get_barrier_semaphore()

    def greet(step, carry):
        other = lax.rem(me + step, devices)
        pl.semaphore_signal(barrier, inc=1, device_id=(other,), device_id_type=MESH)
        return carry

    lax.fori_loop(1, devices, greet, 0)
    pl.semaphore_wait(barrier, devices - 1)


def swap_parts(devices, src, dst, send_sems, recv_sems, own_sem):
    me = lax.axis_index("fsdp")

    def transfer(step, at):
        other = lax.rem(me + step, devices)
        return pltpu.make_async_remote_copy(
            src_ref=src.at[other],
            dst_ref=dst.at[at],
            send_sem=send_sems.at[step],
            recv_sem=recv_sems.at[step],
            device_id=(other,),
            device_id_type=MESH,
        )

    own = pltpu.make_async_copy(src.at[me], dst.at[me], own_sem)

    def begin():
        def one(step, carry):
            transfer(step, me).start()
            return carry

        lax.fori_loop(1, devices, one, 0)
        own.start()

    def finish():
        def one(step, carry):
            transfer(step, me).wait_send()
            transfer(step, lax.rem(me + devices - step, devices)).wait_recv()
            return carry

        lax.fori_loop(1, devices, one, 0)
        own.wait()

    return begin, finish


def tail_kernel(
    chips,
    token_src,
    small_src,
    src,
    token_dst,
    small_dst,
    out,
    core_in,
    col_out,
    col_in,
    layer_out,
    layer_in,
    core_send,
    core_recv,
    layer_send,
    layer_recv,
    col_send,
    col_recv,
    *swap_sems,
):
    layers, layer, col, device, _ = chip_place(chips)
    me = lax.axis_index("fsdp")
    core = lax.rem(me, 2)
    f32 = jnp.float32
    token_begin, token_finish = swap_parts(2 * chips, token_src, token_dst, *swap_sems[:3])
    small_begin, small_finish = swap_parts(2 * chips, small_src, small_dst, *swap_sems[3:])
    meet_all(2 * chips)

    def place(step, turn):
        return around(step, layers, layer) * BLOCK + around(turn, BLOCK, col)

    def to_core(step, turn):
        return pltpu.make_async_remote_copy(
            src_ref=src.at[place(step, turn), 1 - core],
            dst_ref=core_in.at[step, turn],
            send_sem=core_send.at[step, turn],
            recv_sem=core_recv.at[step, turn],
            device_id=(me + 1 - 2 * core,),
            device_id_type=MESH,
        )

    def to_col(step, turn):
        return pltpu.make_async_remote_copy(
            src_ref=col_out.at[step, turn],
            dst_ref=col_in.at[step, turn],
            send_sem=col_send.at[step, turn],
            recv_sem=col_recv.at[step, turn],
            device_id=(device(layer, around(turn, BLOCK, col)),),
            device_id_type=MESH,
        )

    def to_layer(step):
        return pltpu.make_async_remote_copy(
            src_ref=layer_out.at[step],
            dst_ref=layer_in.at[step],
            send_sem=layer_send.at[step],
            recv_sem=layer_recv.at[step],
            device_id=(device(around(step, layers, layer), col),),
            device_id_type=MESH,
        )

    def chip_sum(step, turn):
        to_core(step, turn).wait_recv()
        return src[place(step, turn), core].astype(f32) + core_in[step, turn].astype(f32)

    def block_sum(step):
        total = chip_sum(step, 0)
        for turn in range(1, BLOCK):
            to_col(step, turn).wait_recv()
            total = total + col_in[step, turn].astype(f32)
        return total

    def step_of(number):
        return lax.rem(number + 1, layers)

    def core_begin(number, carry):
        for turn in range(BLOCK):
            to_core(step_of(number), lax.rem(turn + 1, BLOCK)).start()
        return carry

    def col_begin(number, carry):
        step = step_of(number)
        for turn in range(1, BLOCK):
            col_out[step, turn] = chip_sum(step, turn).astype(jnp.bfloat16)
            to_col(step, turn).start()
        return carry

    def layer_begin(step, carry):
        layer_out[step] = block_sum(step).astype(jnp.bfloat16)
        to_layer(step).start()
        return carry

    lax.fori_loop(0, layers, core_begin, 0)
    small_begin()
    token_begin()
    lax.fori_loop(0, layers, col_begin, 0)
    lax.fori_loop(1, layers, layer_begin, 0)
    out[...] = block_sum(0)

    def layer_finish(step, carry):
        to_layer(step).wait_recv()
        out[...] += layer_in[step].astype(f32)
        to_layer(step).wait_send()
        return carry

    def send_finish(step, carry):
        for turn in range(BLOCK):
            to_core(step, turn).wait_send()
        for turn in range(1, BLOCK):
            to_col(step, turn).wait_send()
        return carry

    lax.fori_loop(1, layers, layer_finish, 0)
    lax.fori_loop(0, layers, send_finish, 0)
    small_finish()
    token_finish()


def tail_exchange(tokens, small, blocks, call_id):
    chips, _, rows, width = blocks.shape
    layers = chips // BLOCK
    devices = 2 * chips
    near = pl.BlockSpec(memory_space=pltpu.VMEM)
    anywhere = pl.BlockSpec(memory_space=pl.ANY)
    grid_block = pltpu.VMEM((layers, BLOCK, rows, width), jnp.bfloat16)
    line_block = pltpu.VMEM((layers, rows, width), jnp.bfloat16)
    return pl.pallas_call(
        functools.partial(tail_kernel, chips),
        out_shape=[
            jax.ShapeDtypeStruct(tokens.shape, tokens.dtype),
            jax.ShapeDtypeStruct(small.shape, small.dtype),
            jax.ShapeDtypeStruct((rows, width), jnp.float32),
        ],
        in_specs=[anywhere, anywhere, near],
        out_specs=[anywhere, anywhere, near],
        scratch_shapes=[grid_block] * 3
        + [line_block] * 2
        + [pltpu.SemaphoreType.DMA((layers, BLOCK))] * 2
        + [pltpu.SemaphoreType.DMA((layers,))] * 2
        + [pltpu.SemaphoreType.DMA((layers, BLOCK))] * 2
        + [
            pltpu.SemaphoreType.DMA((devices,)),
            pltpu.SemaphoreType.DMA((devices,)),
            pltpu.SemaphoreType.DMA,
        ]
        * 2,
        compiler_params=pltpu.CompilerParams(
            collective_id=call_id, has_side_effects=True, vmem_limit_bytes=48 * 1024 * 1024
        ),
    )(tokens, small, blocks)


def head_kernel(
    chips,
    token_src,
    src,
    token_dst,
    dst,
    core_send,
    core_recv,
    layer_send,
    layer_recv,
    col_send,
    col_recv,
    own_sem,
    *swap_sems,
):
    layers, layer, col, device, _ = chip_place(chips)
    me = lax.axis_index("fsdp")
    core = lax.rem(me, 2)
    chip = layer * BLOCK + col
    token_begin, token_finish = swap_parts(2 * chips, token_src, token_dst, *swap_sems)
    meet_all(2 * chips)

    def to_layer(step, at):
        return pltpu.make_async_remote_copy(
            src_ref=src,
            dst_ref=dst.at[at, core],
            send_sem=layer_send.at[step],
            recv_sem=layer_recv.at[step],
            device_id=(device(around(step, layers, layer), col),),
            device_id_type=MESH,
        )

    def to_col(step, turn, source, at):
        return pltpu.make_async_remote_copy(
            src_ref=source,
            dst_ref=dst.at[at, core],
            send_sem=col_send.at[step, turn],
            recv_sem=col_recv.at[step, turn],
            device_id=(device(layer, around(turn, BLOCK, col)),),
            device_id_type=MESH,
        )

    def to_core(step, turn, source, at, side):
        return pltpu.make_async_remote_copy(
            src_ref=source,
            dst_ref=dst.at[at, side],
            send_sem=core_send.at[step, turn],
            recv_sem=core_recv.at[step, turn],
            device_id=(me + 1 - 2 * core,),
            device_id_type=MESH,
        )

    def origin(step, turn):
        return around(layers - step, layers, layer) * BLOCK + around(BLOCK - turn, BLOCK, col)

    def layer_start(step, carry):
        to_layer(step, chip).start()
        return carry

    lax.fori_loop(1, layers, layer_start, 0)
    for turn in range(1, BLOCK):
        to_col(0, turn, src, chip).start()
    to_core(0, 0, src, chip, core).start()
    own = pltpu.make_async_copy(src, dst.at[chip, core], own_sem)
    own.start()
    token_begin()

    def layer_pass(step, carry):
        at = origin(step, 0)
        to_layer(step, at).wait_recv()
        for turn in range(1, BLOCK):
            to_col(step, turn, dst.at[at, core], at).start()
        to_core(step, 0, dst.at[at, core], at, core).start()
        return carry

    lax.fori_loop(1, layers, layer_pass, 0)

    def col_pass(step, carry):
        for turn in range(1, BLOCK):
            at = origin(step, turn)
            to_col(step, turn, dst.at[at, core], at).wait_recv()
            to_core(step, turn, dst.at[at, core], at, core).start()
        return carry

    lax.fori_loop(0, layers, col_pass, 0)

    def layer_done(step, carry):
        to_layer(step, chip).wait_send()
        return carry

    def done(step, carry):
        for turn in range(BLOCK):
            if turn:
                to_col(step, turn, src, chip).wait_send()
            at = origin(step, turn)
            to_core(step, turn, src, at, 1 - core).wait_recv()
            to_core(step, turn, src, at, core).wait_send()
        return carry

    lax.fori_loop(1, layers, layer_done, 0)
    lax.fori_loop(0, layers, done, 0)
    own.wait()
    token_finish()


def head_exchange(tokens, block, call_id):
    devices = tokens.shape[0]
    chips = devices // 2
    layers = chips // BLOCK
    anywhere = pl.BlockSpec(memory_space=pl.ANY)
    return pl.pallas_call(
        functools.partial(head_kernel, chips),
        out_shape=[
            jax.ShapeDtypeStruct(tokens.shape, tokens.dtype),
            jax.ShapeDtypeStruct((chips, 2, *block.shape), block.dtype),
        ],
        in_specs=[anywhere] * 2,
        out_specs=[anywhere] * 2,
        scratch_shapes=[pltpu.SemaphoreType.DMA((layers, BLOCK))] * 2
        + [pltpu.SemaphoreType.DMA((layers,))] * 2
        + [pltpu.SemaphoreType.DMA((layers, BLOCK))] * 2
        + [
            pltpu.SemaphoreType.DMA,
            pltpu.SemaphoreType.DMA((devices,)),
            pltpu.SemaphoreType.DMA((devices,)),
            pltpu.SemaphoreType.DMA,
        ],
        compiler_params=pltpu.CompilerParams(collective_id=call_id, has_side_effects=True),
    )(tokens, block)


def pack_blocks(parts, devices):
    flat = jnp.concatenate(
        [jnp.broadcast_to(part, (devices, part.shape[-1])) for part in parts], axis=1
    )
    rows = -(-flat.shape[1] // 1024) * 8
    flat = jnp.pad(flat, ((0, 0), (0, rows * 128 - flat.shape[1])))
    return flat.reshape(devices, rows, 128)


def take_rows(mask, rows):
    return jnp.dot(mask.astype(jnp.bfloat16), rows, preferred_element_type=jnp.float32)


def take_rows_wide(mask, rows):
    high = lax.reduce_precision(rows, 8, 7)
    both = jnp.concatenate([high, rows - high], axis=1).astype(jnp.bfloat16)
    picked = take_rows(mask, both)
    width = rows.shape[1]
    return picked[:, :width] + picked[:, width:]


def bias_tile(table_row, buckets):
    rows, cols = buckets.shape
    spread = jnp.broadcast_to(table_row, (rows, 128))
    return jnp.concatenate(
        [
            jnp.take_along_axis(
                spread, buckets[:, at : at + 128], axis=1, mode="promise_in_bounds"
            )
            for at in range(0, cols, 128)
        ],
        axis=1,
    )


def attend_kernel(block, length, q_ref, k_ref, v_ref, bucket_ref, table_ref, out_ref, log_ref):
    lower = lax.broadcasted_iota(jnp.int32, (1, 128), 1) < 64
    pair = pl.program_id(0)
    zero = jnp.zeros((), jnp.bfloat16)
    for start in range(0, length, block):
        rows = pl.ds(start, block)
        seen = start + block
        logs = []
        mixed = []
        for half in range(2):
            mine = lower if half == 0 else ~lower
            queries = jnp.where(mine, q_ref[rows, :], zero) * 0.125
            values = jnp.where(mine, v_ref[0:seen, :], zero)
            scores = lax.dot_general(
                queries, k_ref[0:seen, :], NT, preferred_element_type=jnp.float32
            )
            table_row = table_ref[pl.ds(2 * pair + half, 1), :]
            scores = scores + bias_tile(table_row, bucket_ref[rows, 0:seen])
            peak = jnp.max(scores, axis=1, keepdims=True)
            raised = jnp.exp(scores - peak)
            totals = jnp.sum(raised, axis=1, keepdims=True)
            probs = (raised * (1.0 / totals)).astype(jnp.bfloat16)
            mixed.append(jnp.dot(probs, values, preferred_element_type=jnp.float32))
            logs.append(peak + jnp.log(totals))
        out_ref[rows, :] = (mixed[0] + mixed[1]).astype(jnp.bfloat16)
        log_ref[0, rows, :] = jnp.where(lower, logs[0], logs[1])


def attend(queries, keys, values, buckets, table, block):
    length, width = queries.shape
    cols = pl.BlockSpec((length, 128), lambda pair: (0, pair))
    return pl.pallas_call(
        functools.partial(attend_kernel, block, length),
        grid=(width // 128,),
        in_specs=[
            cols,
            cols,
            cols,
            pl.BlockSpec(buckets.shape, lambda pair: (0, 0)),
            pl.BlockSpec(table.shape, lambda pair: (0, 0)),
        ],
        out_specs=[cols, pl.BlockSpec((1, length, 128), lambda pair: (pair, 0, 0))],
        out_shape=[
            jax.ShapeDtypeStruct((length, width), jnp.bfloat16),
            jax.ShapeDtypeStruct((width // 128, length, 128), jnp.float32),
        ],
        compiler_params=pltpu.CompilerParams(vmem_limit_bytes=40 * 1024 * 1024),
    )(queries, keys, values, buckets, table)


def attend_back_kernel(
    block,
    length,
    q_ref,
    k_ref,
    v_ref,
    g_ref,
    log_ref,
    bucket_ref,
    table_ref,
    prefix_ref,
    edge_ref,
    dq_ref,
    dk_ref,
    dv_ref,
    edge_sum_ref,
    dk_acc,
    dv_acc,
):
    lower = lax.broadcasted_iota(jnp.int32, (1, 128), 1) < 64
    pair = pl.program_id(0)
    zero = jnp.zeros((), jnp.bfloat16)
    f32 = jnp.float32
    dk_acc[...] = jnp.zeros_like(dk_acc)
    dv_acc[...] = jnp.zeros_like(dv_acc)
    edge_sums = [jnp.zeros((8, 128), f32)] * 2
    for start in range(0, length, block):
        rows = pl.ds(start, block)
        seen = start + block
        edges = edge_ref[rows, :]
        lane_at = edges & 127
        dq_parts = []
        for half in range(2):
            mine = lower if half == 0 else ~lower
            queries = jnp.where(mine, q_ref[rows, :], zero) * 0.125
            grads = jnp.where(mine, g_ref[rows, :], zero)
            keys = jnp.where(mine, k_ref[0:seen, :], zero)
            scores = lax.dot_general(queries, keys, NT, preferred_element_type=f32)
            table_row = table_ref[pl.ds(2 * pair + half, 1), :]
            scores = scores + bias_tile(table_row, bucket_ref[rows, 0:seen])
            probs = jnp.exp(scores - log_ref[0, rows, 64 * half : 64 * half + 1])
            grad_probs = lax.dot_general(
                grads, v_ref[0:seen, :], NT, preferred_element_type=f32
            )
            inner_sum = jnp.sum(probs * grad_probs, axis=1, keepdims=True)
            grad_scores = (probs * (grad_probs - inner_sum)).astype(jnp.bfloat16)
            dq_parts.append(jnp.dot(grad_scores, keys, preferred_element_type=f32))
            dk_acc[0:seen, :] += lax.dot_general(
                grad_scores, queries, TN, preferred_element_type=f32
            )
            dv_acc[0:seen, :] += lax.dot_general(
                probs.astype(jnp.bfloat16), grads, TN, preferred_element_type=f32
            )
            upto = jnp.dot(grad_scores, prefix_ref[0:seen, 0:seen], preferred_element_type=f32)
            for at in range(0, seen, 128):
                read = jnp.take_along_axis(
                    upto[:, at : at + 128], lane_at, axis=1, mode="promise_in_bounds"
                )
                read = jnp.where((edges >= at) & (edges < at + 128), read, 0.0)
                edge_sums[half] = edge_sums[half] + jnp.sum(
                    read.reshape(block // 8, 8, 128), axis=0
                )
        dq_ref[rows, :] = ((dq_parts[0] + dq_parts[1]) * 0.125).astype(jnp.bfloat16)
    dk_ref[...] = dk_acc[...].astype(jnp.bfloat16)
    dv_ref[...] = dv_acc[...].astype(jnp.bfloat16)
    edge_sum_ref[0] = edge_sums[0]
    edge_sum_ref[1] = edge_sums[1]


def attend_back(queries, keys, values, grads, logs, buckets, table, prefix, edges, block):
    length, width = queries.shape
    cols = pl.BlockSpec((length, 128), lambda pair: (0, pair))
    low = jax.ShapeDtypeStruct((length, width), jnp.bfloat16)
    return pl.pallas_call(
        functools.partial(attend_back_kernel, block, length),
        grid=(width // 128,),
        in_specs=[
            cols,
            cols,
            cols,
            cols,
            pl.BlockSpec((1, length, 128), lambda pair: (pair, 0, 0)),
            pl.BlockSpec(buckets.shape, lambda pair: (0, 0)),
            pl.BlockSpec(table.shape, lambda pair: (0, 0)),
            pl.BlockSpec(prefix.shape, lambda pair: (0, 0)),
            pl.BlockSpec(edges.shape, lambda pair: (0, 0)),
        ],
        out_specs=[cols, cols, cols, pl.BlockSpec((2, 8, 128), lambda pair: (pair, 0, 0))],
        out_shape=[low, low, low, jax.ShapeDtypeStruct((width // 64, 8, 128), jnp.float32)],
        scratch_shapes=[pltpu.VMEM((length, 128), jnp.float32)] * 2,
        compiler_params=pltpu.CompilerParams(vmem_limit_bytes=48 * 1024 * 1024),
    )(queries, keys, values, grads, logs, buckets, table, prefix, edges)


def adam_step(weight, moment, square, gradient, factor):
    clipped = gradient * factor
    moment_next = 0.9 * moment + 0.1 * clipped
    square_next = 0.95 * square + 0.05 * clipped * clipped
    corrected_moment = moment_next / (1.0 - 0.9**STEP)
    corrected_square = square_next / (1.0 - 0.95**STEP)
    update = -learn_rate * (
        corrected_moment / (jnp.sqrt(corrected_square) + 1e-08)
        + weight_decay * weight.astype(jnp.float32)
    )
    return (moment_next, square_next, update)


def local(
    token_ids,
    segment_ids,
    parent_segments,
    expert_choice,
    drop_order,
    loss_positions,
    target_ids,
    embedding,
    attention_weights,
    router_weights,
    small_params,
    inward_weights,
    outward_weights,
    embedding_moment,
    embedding_square,
    attention_moment,
    attention_square,
    router_moment,
    router_square,
    params_moment,
    params_square,
    inward_moment,
    inward_square,
    outward_moment,
    outward_square,
):
    devices = lax.axis_size("fsdp")
    me = lax.axis_index("fsdp")
    length = token_ids.shape[0]
    vocab_rows, model_width = embedding.shape
    rows_loss = loss_positions.shape[0]
    experts_all = devices // SPLIT
    capacity = 9 * 2 * length // (8 * experts_all)
    slots = -(-capacity // 16) * 16
    block_rows = 128
    f32 = jnp.float32
    bf16 = jnp.bfloat16
    quads = [[SPLIT * e + q for q in range(SPLIT)] for e in range(experts_all)]
    router_size = router_weights.shape[0]
    params_size = small_params.shape[0]

    owner = token_ids // vocab_rows
    place = token_ids - owner * vocab_rows
    order = jnp.arange(length, dtype=jnp.int32)
    repeated = jnp.any(
        (token_ids[:, None] == token_ids[None, :]) & (order[None, :] < order[:, None]), axis=1
    )
    fresh = ~repeated
    rank = jnp.sum(
        (
            fresh[None, :]
            & (owner[None, :] == owner[:, None])
            & (token_ids[None, :] < token_ids[:, None])
        ).astype(jnp.int32),
        axis=1,
    )
    too_many = jnp.any(rank >= ASK).astype(f32)
    ask_row = jnp.where(rank < ASK, owner * ASK + rank, devices * ASK)
    ask_lines = jnp.arange(devices * ASK, dtype=jnp.int32)
    asked = jnp.sum(
        jnp.where(
            (ask_lines[:, None] == ask_row[None, :]) & fresh[None, :], place[None, :] + 1, 0
        ),
        axis=1,
    )
    hello = pack_blocks(
        (
            asked.reshape(devices, ASK).astype(f32),
            router_weights.astype(f32)[None],
            small_params.astype(f32)[None],
            target_ids.astype(f32).reshape(1, -1),
            too_many.reshape(1, 1),
        ),
        devices,
    )
    heard = swap_blocks(hello, 1, 1).reshape(devices, -1)
    spans = [ASK, router_size, params_size, 2 * rows_loss, 1]
    edges = [sum(spans[:i]) for i in range(len(spans) + 1)]
    wanted, router_full, params_full, targets_full, crowded = [
        heard[:, edges[i] : edges[i + 1]] for i in range(len(spans))
    ]
    wanted = wanted.reshape(-1).astype(jnp.int32) - 1
    router_full = router_full.reshape(-1).astype(bf16)
    params_full = params_full.reshape(-1)
    targets_full = targets_full.reshape(-1, 2).astype(jnp.int32)
    crowded = jnp.any(crowded > 0.5)
    inward_full = lax.all_gather(inward_weights[0], "fsdp", axis=0, axis_index_groups=quads)
    outward_full = lax.all_gather(outward_weights[0], "fsdp", axis=0, axis_index_groups=quads)

    siblings = [(device, device + 1 - 2 * (device % 2)) for device in range(devices)]
    chips = devices // 2
    core = lax.rem(me, 2)
    vocab_pad = -(-vocab_rows // 256) * 256
    fill = ((0, vocab_pad - vocab_rows), (0, 0))
    chip_table = jnp.concatenate(
        [jnp.pad(embedding, fill), jnp.pad(lax.ppermute(embedding, "fsdp", siblings), fill)], axis=0
    )
    vocab_lines = jnp.arange(vocab_pad, dtype=jnp.int32)
    chip_ids = jnp.concatenate(
        [
            jnp.where(vocab_lines < vocab_rows, vocab_lines + side * vocab_rows, -1)
            for side in (me, me + 1 - 2 * core)
        ]
    )[:, None]

    wanted_mask = wanted[:, None] == jnp.arange(vocab_rows, dtype=jnp.int32)[None, :]
    served = take_rows(wanted_mask, embedding).astype(bf16).reshape(devices, ASK, model_width)
    attention_rows = attention_weights.shape[0]
    attention_pad = -attention_rows % 16
    served, attention_full = head_exchange(
        served, jnp.pad(attention_weights, ((0, attention_pad), (0, 0))), 2
    )
    served = served.reshape(devices * ASK, model_width)
    attention_full = attention_full[:, :, :attention_rows].reshape(-1, model_width)
    ask_mask = ask_row[:, None] == ask_lines[None, :]
    embedded_low = lax.cond(
        crowded,
        lambda: lax.all_gather(embedding, "fsdp", axis=0, tiled=True)[token_ids],
        lambda: take_rows(ask_mask, served).astype(bf16),
    )
    embedded = embedded_low.astype(f32) * math.sqrt(model_width)
    gain_first = params_full[:model_width]
    gain_second = params_full[model_width : 2 * model_width]
    gain_final = params_full[2 * model_width : 3 * model_width]
    bias_table = params_full[3 * model_width :].reshape(HEADS, NB)
    router_matrix = router_full.reshape(model_width, experts_all)
    buckets, prefix, edges = tree_layout(segment_ids, parent_segments[0])
    normed_first = rms_norm(embedded, gain_first).astype(bf16)
    queries, keys_all, values_all = [
        jnp.dot(
            normed_first,
            attention_full[part * model_width : (part + 1) * model_width],
            preferred_element_type=f32,
        ).astype(bf16)
        for part in range(3)
    ]
    bias_lines = jnp.pad(
        jnp.concatenate([bias_table, jnp.full((HEADS, 1), -1e30, f32)], axis=1),
        ((0, 16 - HEADS), (0, 127 - NB)),
    )
    mixed_all, log_totals = attend(queries, keys_all, values_all, buckets, bias_lines, block_rows)
    after_attn = embedded + jnp.dot(
        mixed_all, attention_full[3 * model_width :], preferred_element_type=f32
    )
    routed_in = rms_norm(after_attn, gain_second).astype(bf16)
    route_logits = jnp.dot(routed_in, router_matrix, preferred_element_type=f32)
    choice_onehot = (
        expert_choice[:, :, None] == jnp.arange(experts_all, dtype=jnp.int32)[None, None, :]
    ).astype(f32)
    chosen = jnp.sum(choice_onehot * route_logits[:, None, :], axis=-1)
    gate_peak = jnp.max(chosen, axis=1, keepdims=True)
    raised_gate = jnp.exp(chosen - gate_peak)
    gate_weights = raised_gate / jnp.sum(raised_gate, axis=1, keepdims=True)
    drop_rank = drop_order[0]
    flat_choice = expert_choice.reshape(-1)
    slot_index = jnp.sum(
        (
            (flat_choice[None, :] == flat_choice[:, None])
            & (drop_rank[None, :] < drop_rank[:, None])
        ).astype(jnp.int32),
        axis=1,
    ).reshape(length, 2)
    target_row = jnp.where(
        slot_index < capacity, expert_choice * slots + slot_index, experts_all * slots
    )
    slot_lines = jnp.arange(experts_all * slots, dtype=jnp.int32)
    first_out = target_row[:, 0][None, :] == slot_lines[:, None]
    second_out = target_row[:, 1][None, :] == slot_lines[:, None]
    first_in = target_row[:, 0][:, None] == slot_lines[None, :]
    second_in = target_row[:, 1][:, None] == slot_lines[None, :]
    outgoing = take_rows(first_out | second_out, routed_in).astype(bf16)
    expert_rows, returned_low = run_experts(
        outgoing.reshape(experts_all, slots, model_width), inward_full, outward_full, 7
    )
    returned_low = returned_low.reshape(experts_all * slots, model_width)
    returned_first = take_rows(first_in, returned_low)
    returned_second = take_rows(second_in, returned_low)
    after_moe = (
        after_attn + gate_weights[:, 0:1] * returned_first + gate_weights[:, 1:2] * returned_second
    )
    normed_final = rms_norm(after_moe, gain_final).astype(bf16)
    loss_mask = loss_positions[:, None] == order[None, :]
    picked = take_rows(loss_mask, normed_final).astype(bf16)
    scale_rows = 1.0 / (devices * rows_loss)

    targets_here = jnp.where(
        core == 0,
        targets_full.reshape(chips, 2, rows_loss, 2)[:, 0],
        targets_full.reshape(chips, 2, rows_loss, 2)[:, 1],
    ).reshape(chips // BLOCK, BLOCK * rows_loss, 2)
    targets_here = jnp.pad(targets_here.swapaxes(1, 2), ((0, 0), (0, 6), (0, 0)))
    picked_grad, chip_grad, loss_rows = loss_exchange(
        picked, chip_table, chip_ids, targets_here, chips, scale_rows, 5
    )
    loss_local = jnp.sum(loss_rows[0])
    table_grad = chip_grad[:vocab_rows] + lax.ppermute(
        chip_grad[vocab_pad : vocab_pad + vocab_rows], "fsdp", siblings
    )
    grad_normed = take_rows_wide(loss_mask.T, picked_grad.T)
    _, final_back = jax.vjp(rms_norm, after_moe, gain_final)
    grad_after_moe, grad_gain_final = final_back(grad_normed)
    grad_gates = jnp.stack(
        [
            jnp.sum(returned_first * grad_after_moe, axis=-1),
            jnp.sum(returned_second * grad_after_moe, axis=-1),
        ],
        axis=1,
    )
    grad_chosen = gate_weights * (
        grad_gates - jnp.sum(gate_weights * grad_gates, axis=1, keepdims=True)
    )
    grad_route = jnp.sum(choice_onehot * grad_chosen[:, :, None], axis=1).astype(bf16)
    router_grad = jnp.einsum(
        "td,te->de", routed_in, grad_route, preferred_element_type=f32
    ).reshape(-1)
    grad_routed = jnp.einsum("te,de->td", grad_route, router_matrix, preferred_element_type=f32)
    grad_slots = take_rows(
        first_out, (gate_weights[:, 0:1] * grad_after_moe).astype(bf16)
    ) + take_rows(second_out, (gate_weights[:, 1:2] * grad_after_moe).astype(bf16))
    grad_returned, inward_parts, outward_parts = run_experts_back(
        grad_slots.astype(bf16).reshape(experts_all, slots, model_width),
        expert_rows,
        inward_full,
        outward_full,
        8,
    )
    grad_returned = grad_returned.reshape(experts_all * slots, model_width)
    inward_grad = lax.psum_scatter(
        inward_parts, "fsdp", scatter_dimension=0, axis_index_groups=quads
    )[None]
    outward_grad = lax.psum_scatter(
        outward_parts, "fsdp", scatter_dimension=0, axis_index_groups=quads
    )[None]
    grad_routed = grad_routed + take_rows(first_in | second_in, grad_returned)
    _, second_back = jax.vjp(rms_norm, after_attn, gain_second)
    grad_norm_in, grad_gain_second = second_back(grad_routed)
    grad_after_attn = grad_after_moe + grad_norm_in
    grad_attn_low = grad_after_attn.astype(bf16)
    output_grad = jnp.einsum("td,te->de", mixed_all, grad_attn_low, preferred_element_type=f32)
    grad_mixed = jnp.einsum(
        "te,de->td", grad_attn_low, attention_full[3 * model_width :], preferred_element_type=f32
    ).astype(bf16)
    grad_queries_low, grad_keys_low, grad_values_low, edge_sums = attend_back(
        queries,
        keys_all,
        values_all,
        grad_mixed,
        log_totals,
        buckets,
        bias_lines,
        prefix,
        edges,
        block_rows,
    )
    grad_queries_low, grad_keys_low, grad_values_low, edge_sums, inward_grad = (
        lax.optimization_barrier(
            (grad_queries_low, grad_keys_low, grad_values_low, edge_sums, inward_grad)
        )
    )
    edge_sums = jnp.sum(edge_sums, axis=1)[:, :NB]
    grad_bias = edge_sums - jnp.pad(edge_sums[:, 1:], ((0, 0), (0, 1)))
    projection_grads = []
    grad_normed_first = jnp.zeros((length, model_width), f32)
    for position, gradient_low in enumerate((grad_queries_low, grad_keys_low, grad_values_low)):
        projection_grads.append(
            jnp.einsum("td,te->de", normed_first, gradient_low, preferred_element_type=f32)
        )
        grad_normed_first = grad_normed_first + jnp.einsum(
            "te,de->td",
            gradient_low,
            attention_full[position * model_width : (position + 1) * model_width],
            preferred_element_type=f32,
        )
    attention_grad = jnp.concatenate(projection_grads + [output_grad], axis=0)
    _, first_back = jax.vjp(rms_norm, embedded, gain_first)
    grad_embed_in, grad_gain_first = first_back(grad_normed_first)
    grad_embedded = (grad_after_attn + grad_embed_in) * math.sqrt(model_width)
    params_grad = jnp.concatenate(
        [grad_gain_first, grad_gain_second, grad_gain_final, grad_bias.reshape(-1)]
    )
    ask_sums = take_rows_wide(ask_mask.T, grad_embedded).astype(bf16)
    attention_blocks = jnp.pad(
        attention_grad.astype(bf16).reshape(devices // 2, 2, attention_rows, model_width),
        ((0, 0), (0, 0), (0, attention_pad), (0, 0)),
    )
    small_blocks = pack_blocks(
        (router_grad.reshape(devices, router_size), params_grad.reshape(devices, params_size)),
        devices,
    )
    ask_sums, small_sums, attention_share = tail_exchange(
        ask_sums.reshape(devices, ASK, model_width), small_blocks, attention_blocks, 9
    )
    ask_sums, small_sums, attention_share, outward_grad = lax.optimization_barrier(
        (ask_sums, small_sums, attention_share, outward_grad)
    )
    attention_share = attention_share[:attention_rows]
    small_share = jnp.sum(small_sums.reshape(devices, -1), axis=0)

    def lookup_wide():
        whole = jnp.zeros((devices * vocab_rows, model_width), f32).at[token_ids].add(grad_embedded)
        return lax.psum_scatter(whole, "fsdp", scatter_dimension=0, tiled=True)

    table_share = table_grad + lax.cond(
        crowded,
        lookup_wide,
        lambda: take_rows(wanted_mask.T, ask_sums.reshape(devices * ASK, model_width)),
    )
    router_share = small_share[:router_size]
    params_share = small_share[router_size : router_size + params_size]
    local_square = (
        jnp.sum(table_share * table_share)
        + jnp.sum(attention_share * attention_share)
        + jnp.sum(router_share * router_share)
        + jnp.sum(params_share * params_share)
        + jnp.sum(inward_grad * inward_grad)
        + jnp.sum(outward_grad * outward_grad)
    )
    total_square = jnp.sum(
        swap_blocks(pack_blocks((local_square.reshape(1, 1),), devices), 1, 11).reshape(devices, -1)[
            :, 0
        ]
    )
    grad_norm = jnp.sqrt(total_square)
    threshold = clip_base / math.sqrt(devices * rows_loss)
    factor = jnp.minimum(1.0, threshold / grad_norm)
    loss_parts = (loss_local * scale_rows).reshape(1)
    table_m, table_s, table_u = adam_step(
        embedding, embedding_moment, embedding_square, table_share, factor
    )
    attention_m, attention_s, attention_u = adam_step(
        attention_weights, attention_moment, attention_square, attention_share, factor
    )
    router_m, router_s, router_u = adam_step(
        router_weights, router_moment, router_square, router_share, factor
    )
    params_m, params_s, params_u = adam_step(
        small_params, params_moment, params_square, params_share, factor
    )
    inward_m, inward_s, inward_u = adam_step(
        inward_weights, inward_moment, inward_square, inward_grad, factor
    )
    outward_m, outward_s, outward_u = adam_step(
        outward_weights, outward_moment, outward_square, outward_grad, factor
    )
    return (
        loss_parts,
        grad_norm,
        table_m,
        table_s,
        table_u,
        attention_m,
        attention_s,
        attention_u,
        router_m,
        router_s,
        router_u,
        params_m,
        params_s,
        params_u,
        inward_m,
        inward_s,
        inward_u,
        outward_m,
        outward_s,
        outward_u,
    )


def solution(mesh):
    placed = (
        P("fsdp"),
        P("fsdp"),
        P("fsdp", None),
        P("fsdp", None),
        P("fsdp", None),
        P("fsdp"),
        P("fsdp", None),
        P("fsdp", None),
        P("fsdp", None),
        P("fsdp"),
        P("fsdp"),
        P("fsdp", None, None),
        P("fsdp", None, None),
        P("fsdp", None),
        P("fsdp", None),
        P("fsdp", None),
        P("fsdp", None),
        P("fsdp"),
        P("fsdp"),
        P("fsdp"),
        P("fsdp"),
        P("fsdp", None, None),
        P("fsdp", None, None),
        P("fsdp", None, None),
        P("fsdp", None, None),
    )
    return jax.shard_map(
        local,
        mesh=mesh,
        in_specs=placed,
        out_specs=(
            P("fsdp"),
            P(),
            P("fsdp", None),
            P("fsdp", None),
            P("fsdp", None),
            P("fsdp", None),
            P("fsdp", None),
            P("fsdp", None),
            P("fsdp"),
            P("fsdp"),
            P("fsdp"),
            P("fsdp"),
            P("fsdp"),
            P("fsdp"),
            P("fsdp", None, None),
            P("fsdp", None, None),
            P("fsdp", None, None),
            P("fsdp", None, None),
            P("fsdp", None, None),
            P("fsdp", None, None),
        ),
        check_vma=False,
    )
```

```python
import functools
import math

import jax
import jax.numpy as jnp
from jax import lax
from jax.experimental import pallas as pl
from jax.experimental.pallas import tpu as pltpu
from jax.sharding import PartitionSpec as P

HEADS = 12
NB = 32
SPLIT = 4
STEP = 10
ASK = 48
BLOCK = 4
WINDOW = 3
NT = (((1,), (1,)), ((), ()))
TN = (((0,), (0,)), ((), ()))
MESH = pl.DeviceIdType.MESH


bucket_marks = (16, 23, 32, 45, 64, 91, 128, 181, 256, 362, 512, 724, 1024, 1448, 2048, 2896)
learn_rate = 0.02
weight_decay = 0.1
clip_base = 8.0


def rms_norm(values, gains):
    return values * lax.rsqrt(jnp.mean(values * values, axis=-1, keepdims=True) + 1e-06) * gains


def bucket_of(distance):
    distance = jnp.maximum(distance, 0)
    bucket = jnp.minimum(distance, 15)
    for border in bucket_marks:
        bucket = bucket + (distance >= border).astype(jnp.int32)
    return bucket


def tree_layout(segments, parents):
    segment_count = parents.shape[0]
    identity_rows = jnp.eye(segment_count, dtype=jnp.float32)
    parent_rows = (parents[:, None] == jnp.arange(segment_count, dtype=jnp.int32)[None, :]).astype(
        jnp.float32
    )
    ancestry = jnp.minimum(identity_rows + parent_rows, 1.0)
    reached = 1
    while reached < segment_count - 1:
        ancestry = jnp.minimum(jnp.dot(ancestry, ancestry), 1.0)
        reached = 2 * reached
    member = (segments[:, None] == jnp.arange(segment_count, dtype=jnp.int32)[None, :]).astype(
        jnp.int32
    )
    lengths = jnp.sum(member, axis=0)
    starts = jnp.cumsum(lengths) - lengths
    before = jnp.sum((ancestry - identity_rows).astype(jnp.int32) * lengths[None, :], axis=1)
    tree_depth = jnp.sum(member * (before - starts)[None, :], axis=1) + jnp.arange(
        segments.shape[0], dtype=jnp.int32
    )
    reach_rows = jnp.dot(member.astype(jnp.float32), ancestry)
    linked = jnp.dot(reach_rows, member.astype(jnp.float32).T) > 0.5
    order = jnp.arange(segments.shape[0], dtype=jnp.int32)
    allowed = linked & (order[None, :] <= order[:, None])
    buckets = jnp.where(allowed, bucket_of(tree_depth[:, None] - tree_depth[None, :]), NB)
    prefix = (tree_depth[:, None] <= order[None, :]).astype(jnp.bfloat16)
    begins = jnp.asarray(tuple(range(16)) + bucket_marks, jnp.int32)
    edges = jnp.pad(
        tree_depth[:, None] - begins[None, :], ((0, 0), (0, 128 - NB)), constant_values=-1
    )
    return (buckets.astype(jnp.int32), prefix, edges)


def swap_kernel(peers, stride, src, dst, send_sems, recv_sems, own_sem):
    me = lax.axis_index("fsdp")
    spot, lane = me // stride, lax.rem(me, stride)
    barrier = pltpu.get_barrier_semaphore()

    def greet(step, carry):
        other = lax.rem(spot + step, peers) * stride + lane
        pl.semaphore_signal(barrier, inc=1, device_id=(other,), device_id_type=MESH)
        return carry

    lax.fori_loop(1, peers, greet, 0)
    pl.semaphore_wait(barrier, peers - 1)

    def transfer(step):
        other = lax.rem(spot + step, peers)
        return pltpu.make_async_remote_copy(
            src_ref=src.at[other],
            dst_ref=dst.at[spot],
            send_sem=send_sems.at[step],
            recv_sem=recv_sems.at[step],
            device_id=(other * stride + lane,),
            device_id_type=MESH,
        )

    def begin(step, carry):
        transfer(step).start()
        return carry

    lax.fori_loop(1, peers, begin, 0)
    own = pltpu.make_async_copy(src.at[spot], dst.at[spot], own_sem)
    own.start()

    def finish(step, carry):
        origin = lax.rem(spot + peers - step, peers)
        transfer(step).wait_send()
        pltpu.make_async_remote_copy(
            src_ref=src.at[origin],
            dst_ref=dst.at[origin],
            send_sem=send_sems.at[step],
            recv_sem=recv_sems.at[step],
            device_id=(origin * stride + lane,),
            device_id_type=MESH,
        ).wait_recv()
        return carry

    lax.fori_loop(1, peers, finish, 0)
    own.wait()


def swap_blocks(blocks, stride, call_id):
    peers = blocks.shape[0]
    return pl.pallas_call(
        functools.partial(swap_kernel, peers, stride),
        out_shape=jax.ShapeDtypeStruct(blocks.shape, blocks.dtype),
        in_specs=[pl.BlockSpec(memory_space=pl.ANY)],
        out_specs=pl.BlockSpec(memory_space=pl.ANY),
        scratch_shapes=[
            pltpu.SemaphoreType.DMA((peers,)),
            pltpu.SemaphoreType.DMA((peers,)),
            pltpu.SemaphoreType.DMA,
        ],
        compiler_params=pltpu.CompilerParams(collective_id=call_id, has_side_effects=True),
    )(blocks)


def around(step, size, at):
    return lax.rem(at + step, size)


def meet(others):
    barrier = pltpu.get_barrier_semaphore()
    for other in others:
        pl.semaphore_signal(barrier, inc=1, device_id=(other,), device_id_type=MESH)
    pl.semaphore_wait(barrier, len(others))


def chip_place(chips):
    me = lax.axis_index("fsdp")
    core = lax.rem(me, 2)
    chip = me // 2
    layers = chips // BLOCK
    layer, col = chip // BLOCK, lax.rem(chip, BLOCK)

    def device(other_layer, other_col):
        return (other_layer * BLOCK + other_col) * 2 + core

    others = [device(around(step, layers, layer), col) for step in range(1, layers)]
    others += [device(layer, around(turn, BLOCK, col)) for turn in range(1, BLOCK)]
    return layers, layer, col, device, others


def loss_kernel(
    chips,
    scale,
    picked,
    table,
    ids,
    targets,
    out,
    table_grad,
    loss_rows,
    rows,
    scores,
    pulls,
    picks,
    stat_out,
    stat_in,
    log_out,
    log_in,
    col_in,
    layer_out,
    layer_in,
    table_t,
    own_sem,
    layer_send,
    layer_recv,
    col_send,
    col_recv,
    sum_layer_send,
    sum_layer_recv,
    sum_col_send,
    sum_col_recv,
    stat_send,
    stat_recv,
    log_send,
    log_recv,
):
    layers, layer, col, device, _ = chip_place(chips)
    core = lax.rem(lax.axis_index("fsdp"), 2)
    chip = layer * BLOCK + col
    f32 = jnp.float32
    bf16 = jnp.bfloat16
    count, width = picked.shape
    group = BLOCK * count
    lines_all = table.shape[0]
    lines_step = min(512, lines_all)
    line_steps = lines_all // lines_step
    barrier = pltpu.get_barrier_semaphore()

    def far_chip(shift):
        return lax.rem(chip + shift, chips)

    def greet(shift, carry):
        pl.semaphore_signal(
            barrier, inc=1, device_id=(far_chip(shift) * 2 + core,), device_id_type=MESH
        )
        return carry

    lax.fori_loop(1, chips, greet, 0)
    pl.semaphore_wait(barrier, chips - 1)

    def to_layer(step, at):
        return pltpu.make_async_remote_copy(
            src_ref=picked,
            dst_ref=rows.at[at],
            send_sem=layer_send.at[step],
            recv_sem=layer_recv.at[step],
            device_id=(device(around(step, layers, layer), col),),
            device_id_type=MESH,
        )

    def to_col(step, turn, source, at):
        return pltpu.make_async_remote_copy(
            src_ref=source,
            dst_ref=rows.at[at],
            send_sem=col_send.at[step, turn],
            recv_sem=col_recv.at[step, turn],
            device_id=(device(layer, around(turn, BLOCK, col)),),
            device_id_type=MESH,
        )

    def origin(step, turn):
        return around(layers - step, layers, layer) * BLOCK + around(BLOCK - turn, BLOCK, col)

    def layer_start(step, carry):
        to_layer(step, chip).start()
        return carry

    lax.fori_loop(1, layers, layer_start, 0)
    for turn in range(1, BLOCK):
        to_col(0, turn, picked, chip).start()
    own = pltpu.make_async_copy(picked, rows.at[chip], own_sem)
    own.start()
    table_grad[...] = jnp.zeros_like(table_grad)
    stat_out[...] = jnp.zeros_like(stat_out)
    for number in range(line_steps):
        lines = slice(number * lines_step, (number + 1) * lines_step)
        table_t[:, lines] = table[lines, :].T
    own.wait()

    def lines_of(number):
        return pl.ds(pl.multiple_of(number * lines_step, lines_step), lines_step)

    def layer_rows(far):
        return rows[pl.ds(far * BLOCK, BLOCK)].reshape(group, width)

    def score(lines, block):
        values = lax.dot_general(table[lines, :], block, NT, preferred_element_type=f32)
        return jnp.where(ids[lines, :] >= 0, values, -1e30)

    def to_owner(at):
        return pltpu.make_async_remote_copy(
            src_ref=stat_out.at[at],
            dst_ref=stat_in.at[chip],
            send_sem=stat_send.at[at],
            recv_sem=stat_recv.at[chip],
            device_id=(at * 2 + core,),
            device_id_type=MESH,
        )

    def from_chip(at):
        return pltpu.make_async_remote_copy(
            src_ref=stat_out.at[at],
            dst_ref=stat_in.at[at],
            send_sem=stat_send.at[at],
            recv_sem=stat_recv.at[at],
            device_id=(at * 2 + core,),
            device_id_type=MESH,
        )

    def measure(step, far):
        block = layer_rows(far)
        first = targets[far, 0:1, :]
        second = targets[far, 1:2, :]

        def peak_of(number, peak):
            lines = lines_of(number)
            values = score(lines, block)
            scores[lines, :] = values
            return jnp.maximum(peak, jnp.max(values, axis=0, keepdims=True))

        peak = lax.fori_loop(0, line_steps, peak_of, jnp.full((1, group), -1e30, f32))

        def total_of(number, carry):
            total, first_sum, second_sum = carry
            lines = lines_of(number)
            values = scores[lines, :]
            vocab = ids[lines, :]
            total = total + jnp.sum(jnp.exp(values - peak), axis=0, keepdims=True)
            first_sum = first_sum + jnp.sum(
                jnp.where(vocab == first, values, 0.0), axis=0, keepdims=True
            )
            second_sum = second_sum + jnp.sum(
                jnp.where(vocab == second, values, 0.0), axis=0, keepdims=True
            )
            return total, first_sum, second_sum

        zero = jnp.zeros((1, group), f32)
        sums = lax.fori_loop(0, line_steps, total_of, (zero, zero, zero))
        for part in range(BLOCK):
            lanes = slice(part * count, (part + 1) * count)
            at = far * BLOCK + part
            stat_out[at, 0:1, :] = peak[:, lanes]
            for number in range(3):
                stat_out[at, number + 1 : number + 2, :] = sums[number][:, lanes]

            @pl.when(jnp.logical_or(step != 0, part != col))
            def _():
                to_owner(at).start()

    def layer_pass(step, carry):
        at = origin(step, 0)

        @pl.when(step > 0)
        def _():
            to_layer(step, at).wait_recv()
            for turn in range(1, BLOCK):
                to_col(step, turn, rows.at[at], at).start()

        return carry

    def layer_measure(step, carry):
        for turn in range(1, BLOCK):
            at = origin(step, turn)
            to_col(step, turn, rows.at[at], at).wait_recv()
        measure(step, around(layers - step, layers, layer))
        return carry

    lax.fori_loop(0, layers, layer_pass, 0)
    lax.fori_loop(0, layers, layer_measure, 0)
    stat_in[chip] = stat_out[chip]

    def stat_wait(shift, carry):
        from_chip(far_chip(shift)).wait_recv()
        return carry

    lax.fori_loop(1, chips, stat_wait, 0)
    peaks = stat_in[:, 0, :]
    peak = jnp.max(peaks, axis=0, keepdims=True)
    total = jnp.sum(stat_in[:, 1, :] * jnp.exp(peaks - peak), axis=0, keepdims=True)
    first_hit = jnp.sum(stat_in[:, 2, :], axis=0, keepdims=True)
    second_hit = jnp.sum(stat_in[:, 3, :], axis=0, keepdims=True)
    log_rows = peak + jnp.log(total)
    loss_rows[...] = jnp.broadcast_to(
        log_rows - first_hit + 0.3 * (log_rows - second_hit), loss_rows.shape
    )
    log_out[...] = jnp.broadcast_to(log_rows, log_out.shape)
    log_in[chip] = log_out[...]

    def to_chip(shift, at):
        return pltpu.make_async_remote_copy(
            src_ref=log_out,
            dst_ref=log_in.at[at],
            send_sem=log_send.at[shift],
            recv_sem=log_recv.at[at],
            device_id=(far_chip(shift) * 2 + core,),
            device_id_type=MESH,
        )

    def log_begin(shift, carry):
        to_chip(shift, chip).start()
        return carry

    def log_wait(shift, carry):
        to_chip(shift, far_chip(shift)).wait_recv()
        return carry

    lax.fori_loop(1, chips, log_begin, 0)
    lax.fori_loop(1, chips, log_wait, 0)

    def pull_back(step):
        far = around(step, layers, layer)
        block = layer_rows(far)
        first = targets[far, 0:1, :]
        second = targets[far, 1:2, :]
        logs = jnp.concatenate(
            [log_in[far * BLOCK + part, 0:1, :] for part in range(BLOCK)], axis=1
        )

        def pull_of(number, carry):
            lines = lines_of(number)
            vocab = ids[lines, :]
            pull = (
                1.3 * jnp.exp(score(lines, block) - logs)
                - (vocab == first).astype(f32)
                - 0.3 * (vocab == second).astype(f32)
            )
            pull = (pull * scale).astype(bf16)
            pulls[lines, :] = pull
            table_grad[lines, :] += jnp.dot(pull, block, preferred_element_type=f32)
            return carry

        lax.fori_loop(0, line_steps, pull_of, 0)
        grads = jnp.dot(table_t[...], pulls[...], preferred_element_type=f32).astype(bf16)
        for part in range(BLOCK):
            picks[step, part] = grads[:, part * count : (part + 1) * count]

    def sum_to_col(step, turn):
        return pltpu.make_async_remote_copy(
            src_ref=picks.at[step, around(turn, BLOCK, col)],
            dst_ref=col_in.at[step, turn],
            send_sem=sum_col_send.at[step, turn],
            recv_sem=sum_col_recv.at[step, turn],
            device_id=(device(layer, around(turn, BLOCK, col)),),
            device_id_type=MESH,
        )

    def sum_to_layer(step):
        return pltpu.make_async_remote_copy(
            src_ref=layer_out.at[step],
            dst_ref=layer_in.at[step],
            send_sem=sum_layer_send.at[step],
            recv_sem=sum_layer_recv.at[step],
            device_id=(device(around(step, layers, layer), col),),
            device_id_type=MESH,
        )

    def block_sum(step):
        total = picks[step, col].astype(f32)
        for turn in range(1, BLOCK):
            sum_to_col(step, turn).wait_recv()
            total = total + col_in[step, turn].astype(f32)
        return total

    def pull_pass(number, carry):
        step = lax.rem(number + 1, layers)
        pull_back(step)
        for turn in range(1, BLOCK):
            sum_to_col(step, turn).start()

        @pl.when(number > 0)
        def _():
            layer_out[number] = block_sum(number).astype(bf16)
            sum_to_layer(number).start()

        return carry

    lax.fori_loop(0, layers, pull_pass, 0)
    out[...] = block_sum(0)

    def layer_finish(step, carry):
        sum_to_layer(step).wait_recv()
        out[...] += layer_in[step].astype(f32)
        sum_to_layer(step).wait_send()
        to_layer(step, chip).wait_send()
        return carry

    def col_finish(step, carry):
        for turn in range(1, BLOCK):
            to_col(step, turn, picked, chip).wait_send()
            sum_to_col(step, turn).wait_send()
        return carry

    def small_finish(shift, carry):
        from_chip(far_chip(shift)).wait_send()
        to_chip(shift, chip).wait_send()
        return carry

    lax.fori_loop(1, layers, layer_finish, 0)
    lax.fori_loop(0, layers, col_finish, 0)
    lax.fori_loop(1, chips, small_finish, 0)


def loss_exchange(picked, table, ids, targets, chips, scale, call_id):
    count, width = picked.shape
    layers = chips // BLOCK
    group = BLOCK * count
    lines_all = table.shape[0]
    f32 = jnp.float32
    bf16 = jnp.bfloat16
    near = pl.BlockSpec(memory_space=pltpu.VMEM)
    return pl.pallas_call(
        functools.partial(loss_kernel, chips, scale),
        out_shape=[
            jax.ShapeDtypeStruct((width, count), f32),
            jax.ShapeDtypeStruct((lines_all, width), f32),
            jax.ShapeDtypeStruct((8, count), f32),
        ],
        in_specs=[pl.BlockSpec(memory_space=pl.ANY)] + [near] * 3,
        out_specs=[near] * 3,
        scratch_shapes=[
            pltpu.VMEM((chips, count, width), bf16),
            pltpu.VMEM((lines_all, group), f32),
            pltpu.VMEM((lines_all, group), bf16),
            pltpu.VMEM((layers, BLOCK, width, count), bf16),
            pltpu.VMEM((chips, 8, count), f32),
            pltpu.VMEM((chips, 8, count), f32),
            pltpu.VMEM((8, count), f32),
            pltpu.VMEM((chips, 8, count), f32),
            pltpu.VMEM((layers, BLOCK, width, count), bf16),
            pltpu.VMEM((layers, width, count), bf16),
            pltpu.VMEM((layers, width, count), bf16),
            pltpu.VMEM((width, lines_all), bf16),
            pltpu.SemaphoreType.DMA,
        ]
        + (
            [pltpu.SemaphoreType.DMA((layers,))] * 2
            + [pltpu.SemaphoreType.DMA((layers, BLOCK))] * 2
        )
        * 2
        + [pltpu.SemaphoreType.DMA((chips,))] * 4,
        compiler_params=pltpu.CompilerParams(
            collective_id=call_id, has_side_effects=True, vmem_limit_bytes=60 * 1024 * 1024
        ),
    )(picked, table, ids, targets)


def gelu_parts(values):
    root = math.sqrt(2.0 / math.pi)
    squared = values * values
    bend = jnp.tanh(root * (values + 0.044715 * (squared * values)))
    half = 0.5 * (1.0 + bend)
    slope = half + 0.5 * values * (1.0 - bend * bend) * (root * (1.0 + 0.134145 * squared))
    return values * half, slope


def trade_copies(peers, src, landed, done, returned, sems):
    me = lax.axis_index("fsdp")
    spot, lane = me // SPLIT, lax.rem(me, SPLIT)
    go_send, go_recv, back_send, back_recv = sems

    def device(other):
        return (other * SPLIT + lane,)

    def ahead(step):
        return lax.rem(spot + step, peers)

    def behind(step):
        return lax.rem(spot + peers - step, peers)

    def go(step, at):
        return pltpu.make_async_remote_copy(
            src_ref=src.at[ahead(step)],
            dst_ref=landed.at[at],
            send_sem=go_send.at[step],
            recv_sem=go_recv.at[step],
            device_id=device(ahead(step)),
            device_id_type=MESH,
        )

    def back(step, source, at):
        return pltpu.make_async_remote_copy(
            src_ref=done.at[source],
            dst_ref=returned.at[at],
            send_sem=back_send.at[step],
            recv_sem=back_recv.at[step],
            device_id=device(behind(step)),
            device_id_type=MESH,
        )

    barrier = pltpu.get_barrier_semaphore()

    def greet(step, carry):
        pl.semaphore_signal(barrier, inc=1, device_id=device(ahead(step)), device_id_type=MESH)
        return carry

    lax.fori_loop(1, peers, greet, 0)
    pl.semaphore_wait(barrier, peers - 1)
    return spot, behind, ahead, go, back


def trade_loop(peers, copies, build, work, collect):
    spot, behind, ahead, go, back = copies
    window = min(WINDOW, peers - 1)

    def begin(step, carry):
        build(ahead(step))
        go(step, spot).start()
        return carry

    lax.fori_loop(1, window + 1, begin, 0)
    build(spot)
    work(spot, True)

    def visit(step, carry):
        origin = behind(step)

        @pl.when(step + window < peers)
        def _():
            build(ahead(step + window))
            go(step + window, spot).start()

        go(step, origin).wait_recv()
        work(origin, False)
        back(step, origin, spot).start()
        return carry

    lax.fori_loop(1, peers, visit, 0)
    collect(spot, True)

    def finish(step, carry):
        back(step, spot, ahead(step)).wait_recv()
        collect(ahead(step), False)
        return carry

    def close(step, carry):
        go(step, spot).wait_send()
        back(step, behind(step), spot).wait_send()
        return carry

    lax.fori_loop(1, peers, finish, 0)
    lax.fori_loop(1, peers, close, 0)


def slot_mask(marks, at, slots):
    slot = at * slots + lax.broadcasted_iota(jnp.int32, (slots, 1), 0)
    return [jnp.where(mark == slot, 1.0, 0.0).astype(jnp.bfloat16) for mark in marks]


def experts_kernel(
    peers,
    tokens,
    marks,
    places,
    inward,
    outward,
    landed,
    first_out,
    second_out,
    src,
    done,
    returned,
    *sems,
):
    copies = trade_copies(peers, src, landed, done, returned, sems)
    spot = copies[0]
    f32 = jnp.float32
    slots = src.shape[1]

    def build(at):
        first, second = slot_mask((marks[0:1, :], marks[1:2, :]), at, slots)
        block = jnp.dot(first + second, tokens[...], preferred_element_type=f32)
        src[at] = block.astype(jnp.bfloat16)

    def work(at, own):
        rows = src[at] if own else landed[at]
        if own:
            landed[at] = rows
        total = jnp.zeros(rows.shape, f32)
        for quarter in range(SPLIT):
            before = jnp.dot(rows, inward[quarter], preferred_element_type=f32)
            hidden = gelu_parts(before)[0].astype(jnp.bfloat16)
            total = total + jnp.dot(hidden, outward[quarter], preferred_element_type=f32).astype(
                jnp.bfloat16
            ).astype(f32)
        done[at] = total.astype(jnp.bfloat16)

    def collect(at, own):
        rows = done[at] if own else returned[at]
        slot = at * slots + lax.broadcasted_iota(jnp.int32, (1, slots), 1)
        for number, out in enumerate((first_out, second_out)):
            mask = jnp.where(places[:, number : number + 1] == slot, 1.0, 0.0).astype(jnp.bfloat16)
            picked = jnp.dot(mask, rows, preferred_element_type=f32)
            if own:
                out[...] = picked
            else:
                out[...] += picked

    trade_loop(peers, copies, build, work, collect)


def experts_back_kernel(
    peers,
    first_grads,
    second_grads,
    marks,
    rows_ref,
    inward,
    outward,
    returned,
    inward_grad,
    outward_grad,
    src,
    landed,
    done,
    own_sem,
    *sems,
):
    copies = trade_copies(peers, src, landed, done, returned, sems)
    spot = copies[0]
    f32 = jnp.float32
    slots = src.shape[1]

    def build(at):
        first, second = slot_mask((marks[0:1, :], marks[1:2, :]), at, slots)
        block = jnp.dot(first, first_grads[...], preferred_element_type=f32)
        block = block + jnp.dot(second, second_grads[...], preferred_element_type=f32)
        src[at] = block.astype(jnp.bfloat16)

    def work(at, own):
        rows = rows_ref[at]
        grads = src[at] if own else landed[at]
        total = jnp.zeros(rows.shape, f32)
        for quarter in range(SPLIT):
            before = jnp.dot(rows, inward[quarter], preferred_element_type=f32)
            hidden, slope = gelu_parts(before)
            grad_hidden = lax.dot_general(grads, outward[quarter], NT, preferred_element_type=f32)
            grad_before = (grad_hidden * slope).astype(jnp.bfloat16)
            total = total + lax.dot_general(
                grad_before, inward[quarter], NT, preferred_element_type=f32
            ).astype(jnp.bfloat16).astype(f32)
            for grad, left, right in (
                (inward_grad, rows, grad_before),
                (outward_grad, hidden.astype(jnp.bfloat16), grads),
            ):
                part = lax.dot_general(left, right, TN, preferred_element_type=f32)
                if own:
                    grad[quarter] = part
                else:
                    grad[quarter] += part
        done[at] = total.astype(jnp.bfloat16)

    def collect(at, own):
        if own:
            copy = pltpu.make_async_copy(done.at[at], returned.at[at], own_sem)
            copy.start()
            copy.wait()

    trade_loop(peers, copies, build, work, collect)


def experts_call(body, call_id, operands, outs, scratch, peers):
    anywhere = pl.BlockSpec(memory_space=pl.ANY)
    near = pl.BlockSpec(memory_space=pltpu.VMEM)
    return pl.pallas_call(
        functools.partial(body, peers),
        out_shape=[shape for shape, _ in outs],
        in_specs=[near] * len(operands),
        out_specs=[near if inside else anywhere for _, inside in outs],
        scratch_shapes=scratch + [pltpu.SemaphoreType.DMA((peers,))] * 4,
        compiler_params=pltpu.CompilerParams(
            collective_id=call_id, has_side_effects=True, vmem_limit_bytes=60 * 1024 * 1024
        ),
    )(*operands)


def run_experts(tokens, marks, places, inward, outward, peers, slots, call_id):
    block = (peers, slots, tokens.shape[1])
    low = jax.ShapeDtypeStruct(block, tokens.dtype)
    wide = jax.ShapeDtypeStruct(tokens.shape, jnp.float32)
    return experts_call(
        experts_kernel,
        call_id,
        (tokens, marks, places, inward, outward),
        [(low, True), (wide, True), (wide, True)],
        [pltpu.VMEM(block, tokens.dtype)] * 3,
        peers,
    )


def run_experts_back(first_grads, second_grads, marks, rows, inward, outward, call_id):
    low = jax.ShapeDtypeStruct(rows.shape, rows.dtype)
    wide = jax.ShapeDtypeStruct(inward.shape, jnp.float32)
    return experts_call(
        experts_back_kernel,
        call_id,
        (first_grads, second_grads, marks, rows, inward, outward),
        [(low, False), (wide, True), (wide, True)],
        [pltpu.VMEM(rows.shape, rows.dtype)] * 3 + [pltpu.SemaphoreType.DMA],
        rows.shape[0],
    )


def meet_all(devices):
    me = lax.axis_index("fsdp")
    barrier = pltpu.get_barrier_semaphore()

    def greet(step, carry):
        other = lax.rem(me + step, devices)
        pl.semaphore_signal(barrier, inc=1, device_id=(other,), device_id_type=MESH)
        return carry

    lax.fori_loop(1, devices, greet, 0)
    pl.semaphore_wait(barrier, devices - 1)


def swap_parts(devices, src, dst, send_sems, recv_sems, own_sem):
    me = lax.axis_index("fsdp")

    def transfer(step, at):
        other = lax.rem(me + step, devices)
        return pltpu.make_async_remote_copy(
            src_ref=src.at[other],
            dst_ref=dst.at[at],
            send_sem=send_sems.at[step],
            recv_sem=recv_sems.at[step],
            device_id=(other,),
            device_id_type=MESH,
        )

    own = pltpu.make_async_copy(src.at[me], dst.at[me], own_sem)

    def begin():
        def one(step, carry):
            transfer(step, me).start()
            return carry

        lax.fori_loop(1, devices, one, 0)
        own.start()

    def finish():
        def one(step, carry):
            transfer(step, me).wait_send()
            transfer(step, lax.rem(me + devices - step, devices)).wait_recv()
            return carry

        lax.fori_loop(1, devices, one, 0)
        own.wait()

    return begin, finish


def tail_kernel(
    chips,
    token_src,
    small_src,
    src,
    token_dst,
    small_dst,
    out,
    core_in,
    col_out,
    col_in,
    layer_out,
    layer_in,
    core_send,
    core_recv,
    layer_send,
    layer_recv,
    col_send,
    col_recv,
    *swap_sems,
):
    layers, layer, col, device, _ = chip_place(chips)
    me = lax.axis_index("fsdp")
    core = lax.rem(me, 2)
    f32 = jnp.float32
    token_begin, token_finish = swap_parts(2 * chips, token_src, token_dst, *swap_sems[:3])
    small_begin, small_finish = swap_parts(2 * chips, small_src, small_dst, *swap_sems[3:])
    meet_all(2 * chips)

    def place(step, turn):
        return around(step, layers, layer) * BLOCK + around(turn, BLOCK, col)

    def to_core(step, turn):
        return pltpu.make_async_remote_copy(
            src_ref=src.at[place(step, turn), 1 - core],
            dst_ref=core_in.at[step, turn],
            send_sem=core_send.at[step, turn],
            recv_sem=core_recv.at[step, turn],
            device_id=(me + 1 - 2 * core,),
            device_id_type=MESH,
        )

    def to_col(step, turn):
        return pltpu.make_async_remote_copy(
            src_ref=col_out.at[step, turn],
            dst_ref=col_in.at[step, turn],
            send_sem=col_send.at[step, turn],
            recv_sem=col_recv.at[step, turn],
            device_id=(device(layer, around(turn, BLOCK, col)),),
            device_id_type=MESH,
        )

    def to_layer(step):
        return pltpu.make_async_remote_copy(
            src_ref=layer_out.at[step],
            dst_ref=layer_in.at[step],
            send_sem=layer_send.at[step],
            recv_sem=layer_recv.at[step],
            device_id=(device(around(step, layers, layer), col),),
            device_id_type=MESH,
        )

    def chip_sum(step, turn):
        to_core(step, turn).wait_recv()
        return src[place(step, turn), core].astype(f32) + core_in[step, turn].astype(f32)

    def block_sum(step):
        total = chip_sum(step, 0)
        for turn in range(1, BLOCK):
            to_col(step, turn).wait_recv()
            total = total + col_in[step, turn].astype(f32)
        return total

    def step_of(number):
        return lax.rem(number + 1, layers)

    def core_begin(number, carry):
        for turn in range(BLOCK):
            to_core(step_of(number), lax.rem(turn + 1, BLOCK)).start()
        return carry

    def col_begin(number, carry):
        step = step_of(number)
        for turn in range(1, BLOCK):
            col_out[step, turn] = chip_sum(step, turn).astype(jnp.bfloat16)
            to_col(step, turn).start()
        return carry

    def layer_begin(step, carry):
        layer_out[step] = block_sum(step).astype(jnp.bfloat16)
        to_layer(step).start()
        return carry

    lax.fori_loop(0, layers, core_begin, 0)
    small_begin()
    token_begin()
    lax.fori_loop(0, layers, col_begin, 0)
    lax.fori_loop(1, layers, layer_begin, 0)
    out[...] = block_sum(0)

    def layer_finish(step, carry):
        to_layer(step).wait_recv()
        out[...] += layer_in[step].astype(f32)
        to_layer(step).wait_send()
        return carry

    def send_finish(step, carry):
        for turn in range(BLOCK):
            to_core(step, turn).wait_send()
        for turn in range(1, BLOCK):
            to_col(step, turn).wait_send()
        return carry

    lax.fori_loop(1, layers, layer_finish, 0)
    lax.fori_loop(0, layers, send_finish, 0)
    small_finish()
    token_finish()


def tail_exchange(tokens, small, blocks, call_id):
    chips, _, rows, width = blocks.shape
    layers = chips // BLOCK
    devices = 2 * chips
    near = pl.BlockSpec(memory_space=pltpu.VMEM)
    anywhere = pl.BlockSpec(memory_space=pl.ANY)
    grid_block = pltpu.VMEM((layers, BLOCK, rows, width), jnp.bfloat16)
    line_block = pltpu.VMEM((layers, rows, width), jnp.bfloat16)
    return pl.pallas_call(
        functools.partial(tail_kernel, chips),
        out_shape=[
            jax.ShapeDtypeStruct(tokens.shape, tokens.dtype),
            jax.ShapeDtypeStruct(small.shape, small.dtype),
            jax.ShapeDtypeStruct((rows, width), jnp.float32),
        ],
        in_specs=[anywhere, anywhere, near],
        out_specs=[anywhere, anywhere, near],
        scratch_shapes=[grid_block] * 3
        + [line_block] * 2
        + [pltpu.SemaphoreType.DMA((layers, BLOCK))] * 2
        + [pltpu.SemaphoreType.DMA((layers,))] * 2
        + [pltpu.SemaphoreType.DMA((layers, BLOCK))] * 2
        + [
            pltpu.SemaphoreType.DMA((devices,)),
            pltpu.SemaphoreType.DMA((devices,)),
            pltpu.SemaphoreType.DMA,
        ]
        * 2,
        compiler_params=pltpu.CompilerParams(
            collective_id=call_id, has_side_effects=True, vmem_limit_bytes=48 * 1024 * 1024
        ),
    )(tokens, small, blocks)


def head_kernel(
    chips,
    token_src,
    src,
    token_dst,
    dst,
    core_send,
    core_recv,
    layer_send,
    layer_recv,
    col_send,
    col_recv,
    own_sem,
    *swap_sems,
):
    layers, layer, col, device, _ = chip_place(chips)
    me = lax.axis_index("fsdp")
    core = lax.rem(me, 2)
    chip = layer * BLOCK + col
    token_begin, token_finish = swap_parts(2 * chips, token_src, token_dst, *swap_sems)
    meet_all(2 * chips)

    def to_layer(step, at):
        return pltpu.make_async_remote_copy(
            src_ref=src,
            dst_ref=dst.at[at, core],
            send_sem=layer_send.at[step],
            recv_sem=layer_recv.at[step],
            device_id=(device(around(step, layers, layer), col),),
            device_id_type=MESH,
        )

    def to_col(step, turn, source, at):
        return pltpu.make_async_remote_copy(
            src_ref=source,
            dst_ref=dst.at[at, core],
            send_sem=col_send.at[step, turn],
            recv_sem=col_recv.at[step, turn],
            device_id=(device(layer, around(turn, BLOCK, col)),),
            device_id_type=MESH,
        )

    def to_core(step, turn, source, at, side):
        return pltpu.make_async_remote_copy(
            src_ref=source,
            dst_ref=dst.at[at, side],
            send_sem=core_send.at[step, turn],
            recv_sem=core_recv.at[step, turn],
            device_id=(me + 1 - 2 * core,),
            device_id_type=MESH,
        )

    def origin(step, turn):
        return around(layers - step, layers, layer) * BLOCK + around(BLOCK - turn, BLOCK, col)

    def layer_start(step, carry):
        to_layer(step, chip).start()
        return carry

    lax.fori_loop(1, layers, layer_start, 0)
    for turn in range(1, BLOCK):
        to_col(0, turn, src, chip).start()
    to_core(0, 0, src, chip, core).start()
    own = pltpu.make_async_copy(src, dst.at[chip, core], own_sem)
    own.start()
    token_begin()

    def layer_pass(step, carry):
        at = origin(step, 0)
        to_layer(step, at).wait_recv()
        for turn in range(1, BLOCK):
            to_col(step, turn, dst.at[at, core], at).start()
        to_core(step, 0, dst.at[at, core], at, core).start()
        return carry

    lax.fori_loop(1, layers, layer_pass, 0)

    def col_pass(step, carry):
        for turn in range(1, BLOCK):
            at = origin(step, turn)
            to_col(step, turn, dst.at[at, core], at).wait_recv()
            to_core(step, turn, dst.at[at, core], at, core).start()
        return carry

    lax.fori_loop(0, layers, col_pass, 0)

    def layer_done(step, carry):
        to_layer(step, chip).wait_send()
        return carry

    def done(step, carry):
        for turn in range(BLOCK):
            if turn:
                to_col(step, turn, src, chip).wait_send()
            at = origin(step, turn)
            to_core(step, turn, src, at, 1 - core).wait_recv()
            to_core(step, turn, src, at, core).wait_send()
        return carry

    lax.fori_loop(1, layers, layer_done, 0)
    lax.fori_loop(0, layers, done, 0)
    own.wait()
    token_finish()


def head_exchange(tokens, block, call_id):
    devices = tokens.shape[0]
    chips = devices // 2
    layers = chips // BLOCK
    anywhere = pl.BlockSpec(memory_space=pl.ANY)
    return pl.pallas_call(
        functools.partial(head_kernel, chips),
        out_shape=[
            jax.ShapeDtypeStruct(tokens.shape, tokens.dtype),
            jax.ShapeDtypeStruct((chips, 2, *block.shape), block.dtype),
        ],
        in_specs=[anywhere] * 2,
        out_specs=[anywhere] * 2,
        scratch_shapes=[pltpu.SemaphoreType.DMA((layers, BLOCK))] * 2
        + [pltpu.SemaphoreType.DMA((layers,))] * 2
        + [pltpu.SemaphoreType.DMA((layers, BLOCK))] * 2
        + [
            pltpu.SemaphoreType.DMA,
            pltpu.SemaphoreType.DMA((devices,)),
            pltpu.SemaphoreType.DMA((devices,)),
            pltpu.SemaphoreType.DMA,
        ],
        compiler_params=pltpu.CompilerParams(collective_id=call_id, has_side_effects=True),
    )(tokens, block)


def pack_blocks(parts, devices):
    flat = jnp.concatenate(
        [jnp.broadcast_to(part, (devices, part.shape[-1])) for part in parts], axis=1
    )
    rows = -(-flat.shape[1] // 1024) * 8
    flat = jnp.pad(flat, ((0, 0), (0, rows * 128 - flat.shape[1])))
    return flat.reshape(devices, rows, 128)


def take_rows(mask, rows):
    return jnp.dot(mask.astype(jnp.bfloat16), rows, preferred_element_type=jnp.float32)


def take_rows_wide(mask, rows):
    high = lax.reduce_precision(rows, 8, 7)
    both = jnp.concatenate([high, rows - high], axis=1).astype(jnp.bfloat16)
    picked = take_rows(mask, both)
    width = rows.shape[1]
    return picked[:, :width] + picked[:, width:]


def bias_tile(table_row, buckets):
    rows, cols = buckets.shape
    spread = jnp.broadcast_to(table_row, (rows, 128))
    return jnp.concatenate(
        [
            jnp.take_along_axis(
                spread, buckets[:, at : at + 128], axis=1, mode="promise_in_bounds"
            )
            for at in range(0, cols, 128)
        ],
        axis=1,
    )


def attend_kernel(block, length, q_ref, k_ref, v_ref, bucket_ref, table_ref, out_ref, log_ref):
    lower = lax.broadcasted_iota(jnp.int32, (1, 128), 1) < 64
    pair = pl.program_id(0)
    zero = jnp.zeros((), jnp.bfloat16)
    for start in range(0, length, block):
        rows = pl.ds(start, block)
        seen = start + block
        logs = []
        mixed = []
        for half in range(2):
            mine = lower if half == 0 else ~lower
            queries = jnp.where(mine, q_ref[rows, :], zero) * 0.125
            values = jnp.where(mine, v_ref[0:seen, :], zero)
            scores = lax.dot_general(
                queries, k_ref[0:seen, :], NT, preferred_element_type=jnp.float32
            )
            table_row = table_ref[pl.ds(2 * pair + half, 1), :]
            scores = scores + bias_tile(table_row, bucket_ref[rows, 0:seen])
            peak = jnp.max(scores, axis=1, keepdims=True)
            raised = jnp.exp(scores - peak)
            totals = jnp.sum(raised, axis=1, keepdims=True)
            probs = (raised * (1.0 / totals)).astype(jnp.bfloat16)
            mixed.append(jnp.dot(probs, values, preferred_element_type=jnp.float32))
            logs.append(peak + jnp.log(totals))
        out_ref[rows, :] = (mixed[0] + mixed[1]).astype(jnp.bfloat16)
        log_ref[0, rows, :] = jnp.where(lower, logs[0], logs[1])


def attend(queries, keys, values, buckets, table, block):
    length, width = queries.shape
    cols = pl.BlockSpec((length, 128), lambda pair: (0, pair))
    return pl.pallas_call(
        functools.partial(attend_kernel, block, length),
        grid=(width // 128,),
        in_specs=[
            cols,
            cols,
            cols,
            pl.BlockSpec(buckets.shape, lambda pair: (0, 0)),
            pl.BlockSpec(table.shape, lambda pair: (0, 0)),
        ],
        out_specs=[cols, pl.BlockSpec((1, length, 128), lambda pair: (pair, 0, 0))],
        out_shape=[
            jax.ShapeDtypeStruct((length, width), jnp.bfloat16),
            jax.ShapeDtypeStruct((width // 128, length, 128), jnp.float32),
        ],
        compiler_params=pltpu.CompilerParams(vmem_limit_bytes=40 * 1024 * 1024),
    )(queries, keys, values, buckets, table)


def attend_back_kernel(
    block,
    length,
    q_ref,
    k_ref,
    v_ref,
    g_ref,
    log_ref,
    bucket_ref,
    table_ref,
    prefix_ref,
    edge_ref,
    dq_ref,
    dk_ref,
    dv_ref,
    edge_sum_ref,
    dk_acc,
    dv_acc,
):
    lower = lax.broadcasted_iota(jnp.int32, (1, 128), 1) < 64
    pair = pl.program_id(0)
    zero = jnp.zeros((), jnp.bfloat16)
    f32 = jnp.float32
    dk_acc[...] = jnp.zeros_like(dk_acc)
    dv_acc[...] = jnp.zeros_like(dv_acc)
    edge_sums = [jnp.zeros((8, 128), f32)] * 2
    for start in range(0, length, block):
        rows = pl.ds(start, block)
        seen = start + block
        edges = edge_ref[rows, :]
        lane_at = edges & 127
        dq_parts = []
        for half in range(2):
            mine = lower if half == 0 else ~lower
            queries = jnp.where(mine, q_ref[rows, :], zero) * 0.125
            grads = jnp.where(mine, g_ref[rows, :], zero)
            keys = jnp.where(mine, k_ref[0:seen, :], zero)
            scores = lax.dot_general(queries, keys, NT, preferred_element_type=f32)
            table_row = table_ref[pl.ds(2 * pair + half, 1), :]
            scores = scores + bias_tile(table_row, bucket_ref[rows, 0:seen])
            probs = jnp.exp(scores - log_ref[0, rows, 64 * half : 64 * half + 1])
            grad_probs = lax.dot_general(
                grads, v_ref[0:seen, :], NT, preferred_element_type=f32
            )
            inner_sum = jnp.sum(probs * grad_probs, axis=1, keepdims=True)
            grad_scores = (probs * (grad_probs - inner_sum)).astype(jnp.bfloat16)
            dq_parts.append(jnp.dot(grad_scores, keys, preferred_element_type=f32))
            dk_acc[0:seen, :] += lax.dot_general(
                grad_scores, queries, TN, preferred_element_type=f32
            )
            dv_acc[0:seen, :] += lax.dot_general(
                probs.astype(jnp.bfloat16), grads, TN, preferred_element_type=f32
            )
            upto = jnp.dot(grad_scores, prefix_ref[0:seen, 0:seen], preferred_element_type=f32)
            for at in range(0, seen, 128):
                read = jnp.take_along_axis(
                    upto[:, at : at + 128], lane_at, axis=1, mode="promise_in_bounds"
                )
                read = jnp.where((edges >= at) & (edges < at + 128), read, 0.0)
                edge_sums[half] = edge_sums[half] + jnp.sum(
                    read.reshape(block // 8, 8, 128), axis=0
                )
        dq_ref[rows, :] = ((dq_parts[0] + dq_parts[1]) * 0.125).astype(jnp.bfloat16)
    dk_ref[...] = dk_acc[...].astype(jnp.bfloat16)
    dv_ref[...] = dv_acc[...].astype(jnp.bfloat16)
    edge_sum_ref[0] = edge_sums[0]
    edge_sum_ref[1] = edge_sums[1]


def attend_back(queries, keys, values, grads, logs, buckets, table, prefix, edges, block):
    length, width = queries.shape
    cols = pl.BlockSpec((length, 128), lambda pair: (0, pair))
    low = jax.ShapeDtypeStruct((length, width), jnp.bfloat16)
    return pl.pallas_call(
        functools.partial(attend_back_kernel, block, length),
        grid=(width // 128,),
        in_specs=[
            cols,
            cols,
            cols,
            cols,
            pl.BlockSpec((1, length, 128), lambda pair: (pair, 0, 0)),
            pl.BlockSpec(buckets.shape, lambda pair: (0, 0)),
            pl.BlockSpec(table.shape, lambda pair: (0, 0)),
            pl.BlockSpec(prefix.shape, lambda pair: (0, 0)),
            pl.BlockSpec(edges.shape, lambda pair: (0, 0)),
        ],
        out_specs=[cols, cols, cols, pl.BlockSpec((2, 8, 128), lambda pair: (pair, 0, 0))],
        out_shape=[low, low, low, jax.ShapeDtypeStruct((width // 64, 8, 128), jnp.float32)],
        scratch_shapes=[pltpu.VMEM((length, 128), jnp.float32)] * 2,
        compiler_params=pltpu.CompilerParams(vmem_limit_bytes=48 * 1024 * 1024),
    )(queries, keys, values, grads, logs, buckets, table, prefix, edges)


def adam_step(weight, moment, square, gradient, factor):
    clipped = gradient * factor
    moment_next = 0.9 * moment + 0.1 * clipped
    square_next = 0.95 * square + 0.05 * clipped * clipped
    corrected_moment = moment_next / (1.0 - 0.9**STEP)
    corrected_square = square_next / (1.0 - 0.95**STEP)
    update = -learn_rate * (
        corrected_moment / (jnp.sqrt(corrected_square) + 1e-08)
        + weight_decay * weight.astype(jnp.float32)
    )
    return (moment_next, square_next, update)


def local(
    token_ids,
    segment_ids,
    parent_segments,
    expert_choice,
    drop_order,
    loss_positions,
    target_ids,
    embedding,
    attention_weights,
    router_weights,
    small_params,
    inward_weights,
    outward_weights,
    embedding_moment,
    embedding_square,
    attention_moment,
    attention_square,
    router_moment,
    router_square,
    params_moment,
    params_square,
    inward_moment,
    inward_square,
    outward_moment,
    outward_square,
):
    devices = lax.axis_size("fsdp")
    me = lax.axis_index("fsdp")
    length = token_ids.shape[0]
    vocab_rows, model_width = embedding.shape
    rows_loss = loss_positions.shape[0]
    experts_all = devices // SPLIT
    capacity = 9 * 2 * length // (8 * experts_all)
    slots = -(-capacity // 16) * 16
    block_rows = 128
    f32 = jnp.float32
    bf16 = jnp.bfloat16
    quads = [[SPLIT * e + q for q in range(SPLIT)] for e in range(experts_all)]
    router_size = router_weights.shape[0]
    params_size = small_params.shape[0]

    owner = token_ids // vocab_rows
    place = token_ids - owner * vocab_rows
    order = jnp.arange(length, dtype=jnp.int32)
    repeated = jnp.any(
        (token_ids[:, None] == token_ids[None, :]) & (order[None, :] < order[:, None]), axis=1
    )
    fresh = ~repeated
    rank = jnp.sum(
        (
            fresh[None, :]
            & (owner[None, :] == owner[:, None])
            & (token_ids[None, :] < token_ids[:, None])
        ).astype(jnp.int32),
        axis=1,
    )
    too_many = jnp.any(rank >= ASK).astype(f32)
    ask_row = jnp.where(rank < ASK, owner * ASK + rank, devices * ASK)
    ask_lines = jnp.arange(devices * ASK, dtype=jnp.int32)
    asked = jnp.sum(
        jnp.where(
            (ask_lines[:, None] == ask_row[None, :]) & fresh[None, :], place[None, :] + 1, 0
        ),
        axis=1,
    )
    hello = pack_blocks(
        (
            asked.reshape(devices, ASK).astype(f32),
            router_weights.astype(f32)[None],
            small_params.astype(f32)[None],
            target_ids.astype(f32).reshape(1, -1),
            too_many.reshape(1, 1),
        ),
        devices,
    )
    heard = swap_blocks(hello, 1, 1).reshape(devices, -1)
    spans = [ASK, router_size, params_size, 2 * rows_loss, 1]
    edges = [sum(spans[:i]) for i in range(len(spans) + 1)]
    wanted, router_full, params_full, targets_full, crowded = [
        heard[:, edges[i] : edges[i + 1]] for i in range(len(spans))
    ]
    wanted = wanted.reshape(-1).astype(jnp.int32) - 1
    router_full = router_full.reshape(-1).astype(bf16)
    params_full = params_full.reshape(-1)
    targets_full = targets_full.reshape(-1, 2).astype(jnp.int32)
    crowded = jnp.any(crowded > 0.5)
    inward_full = lax.all_gather(inward_weights[0], "fsdp", axis=0, axis_index_groups=quads)
    outward_full = lax.all_gather(outward_weights[0], "fsdp", axis=0, axis_index_groups=quads)

    siblings = [(device, device + 1 - 2 * (device % 2)) for device in range(devices)]
    chips = devices // 2
    core = lax.rem(me, 2)
    vocab_pad = -(-vocab_rows // 256) * 256
    fill = ((0, vocab_pad - vocab_rows), (0, 0))
    chip_table = jnp.concatenate(
        [jnp.pad(embedding, fill), jnp.pad(lax.ppermute(embedding, "fsdp", siblings), fill)], axis=0
    )
    vocab_lines = jnp.arange(vocab_pad, dtype=jnp.int32)
    chip_ids = jnp.concatenate(
        [
            jnp.where(vocab_lines < vocab_rows, vocab_lines + side * vocab_rows, -1)
            for side in (me, me + 1 - 2 * core)
        ]
    )[:, None]

    wanted_mask = wanted[:, None] == jnp.arange(vocab_rows, dtype=jnp.int32)[None, :]
    served = take_rows(wanted_mask, embedding).astype(bf16).reshape(devices, ASK, model_width)
    attention_rows = attention_weights.shape[0]
    attention_pad = -attention_rows % 16
    served, attention_full = head_exchange(
        served, jnp.pad(attention_weights, ((0, attention_pad), (0, 0))), 2
    )
    served = served.reshape(devices * ASK, model_width)
    attention_full = attention_full[:, :, :attention_rows].reshape(-1, model_width)
    ask_mask = ask_row[:, None] == ask_lines[None, :]
    embedded_low = lax.cond(
        crowded,
        lambda: lax.all_gather(embedding, "fsdp", axis=0, tiled=True)[token_ids],
        lambda: take_rows(ask_mask, served).astype(bf16),
    )
    embedded = embedded_low.astype(f32) * math.sqrt(model_width)
    gain_first = params_full[:model_width]
    gain_second = params_full[model_width : 2 * model_width]
    gain_final = params_full[2 * model_width : 3 * model_width]
    bias_table = params_full[3 * model_width :].reshape(HEADS, NB)
    router_matrix = router_full.reshape(model_width, experts_all)
    buckets, prefix, edges = tree_layout(segment_ids, parent_segments[0])
    normed_first = rms_norm(embedded, gain_first).astype(bf16)
    queries, keys_all, values_all = [
        jnp.dot(
            normed_first,
            attention_full[part * model_width : (part + 1) * model_width],
            preferred_element_type=f32,
        ).astype(bf16)
        for part in range(3)
    ]
    bias_lines = jnp.pad(
        jnp.concatenate([bias_table, jnp.full((HEADS, 1), -1e30, f32)], axis=1),
        ((0, 16 - HEADS), (0, 127 - NB)),
    )
    mixed_all, log_totals = attend(queries, keys_all, values_all, buckets, bias_lines, block_rows)
    after_attn = embedded + jnp.dot(
        mixed_all, attention_full[3 * model_width :], preferred_element_type=f32
    )
    routed_in = rms_norm(after_attn, gain_second).astype(bf16)
    route_logits = jnp.dot(routed_in, router_matrix, preferred_element_type=f32)
    choice_onehot = (
        expert_choice[:, :, None] == jnp.arange(experts_all, dtype=jnp.int32)[None, None, :]
    ).astype(f32)
    chosen = jnp.sum(choice_onehot * route_logits[:, None, :], axis=-1)
    gate_peak = jnp.max(chosen, axis=1, keepdims=True)
    raised_gate = jnp.exp(chosen - gate_peak)
    gate_weights = raised_gate / jnp.sum(raised_gate, axis=1, keepdims=True)
    drop_rank = drop_order[0]
    flat_choice = expert_choice.reshape(-1)
    slot_index = jnp.sum(
        (
            (flat_choice[None, :] == flat_choice[:, None])
            & (drop_rank[None, :] < drop_rank[:, None])
        ).astype(jnp.int32),
        axis=1,
    ).reshape(length, 2)
    target_row = jnp.where(
        slot_index < capacity, expert_choice * slots + slot_index, experts_all * slots
    )
    slot_lines = jnp.arange(experts_all * slots, dtype=jnp.int32)
    first_in = target_row[:, 0][:, None] == slot_lines[None, :]
    second_in = target_row[:, 1][:, None] == slot_lines[None, :]
    marks = jnp.pad(target_row.T, ((0, 6), (0, 0)), constant_values=-1)
    expert_rows, returned_first, returned_second = run_experts(
        routed_in, marks, target_row, inward_full, outward_full, experts_all, slots, 7
    )
    after_moe = (
        after_attn + gate_weights[:, 0:1] * returned_first + gate_weights[:, 1:2] * returned_second
    )
    normed_final = rms_norm(after_moe, gain_final).astype(bf16)
    loss_mask = loss_positions[:, None] == order[None, :]
    picked = take_rows(loss_mask, normed_final).astype(bf16)
    scale_rows = 1.0 / (devices * rows_loss)

    targets_here = jnp.where(
        core == 0,
        targets_full.reshape(chips, 2, rows_loss, 2)[:, 0],
        targets_full.reshape(chips, 2, rows_loss, 2)[:, 1],
    ).reshape(chips // BLOCK, BLOCK * rows_loss, 2)
    targets_here = jnp.pad(targets_here.swapaxes(1, 2), ((0, 0), (0, 6), (0, 0)))
    picked_grad, chip_grad, loss_rows = loss_exchange(
        picked, chip_table, chip_ids, targets_here, chips, scale_rows, 5
    )
    loss_local = jnp.sum(loss_rows[0])
    table_grad = chip_grad[:vocab_rows] + lax.ppermute(
        chip_grad[vocab_pad : vocab_pad + vocab_rows], "fsdp", siblings
    )
    grad_normed = take_rows_wide(loss_mask.T, picked_grad.T)
    _, final_back = jax.vjp(rms_norm, after_moe, gain_final)
    grad_after_moe, grad_gain_final = final_back(grad_normed)
    grad_gates = jnp.stack(
        [
            jnp.sum(returned_first * grad_after_moe, axis=-1),
            jnp.sum(returned_second * grad_after_moe, axis=-1),
        ],
        axis=1,
    )
    grad_chosen = gate_weights * (
        grad_gates - jnp.sum(gate_weights * grad_gates, axis=1, keepdims=True)
    )
    grad_route = jnp.sum(choice_onehot * grad_chosen[:, :, None], axis=1).astype(bf16)
    router_grad = jnp.einsum(
        "td,te->de", routed_in, grad_route, preferred_element_type=f32
    ).reshape(-1)
    grad_routed = jnp.einsum("te,de->td", grad_route, router_matrix, preferred_element_type=f32)
    grad_returned, inward_parts, outward_parts = run_experts_back(
        (gate_weights[:, 0:1] * grad_after_moe).astype(bf16),
        (gate_weights[:, 1:2] * grad_after_moe).astype(bf16),
        marks,
        expert_rows,
        inward_full,
        outward_full,
        8,
    )
    grad_returned = grad_returned.reshape(experts_all * slots, model_width)
    inward_grad = lax.psum_scatter(
        inward_parts, "fsdp", scatter_dimension=0, axis_index_groups=quads
    )[None]
    outward_grad = lax.psum_scatter(
        outward_parts, "fsdp", scatter_dimension=0, axis_index_groups=quads
    )[None]
    grad_routed = grad_routed + take_rows(first_in | second_in, grad_returned)
    _, second_back = jax.vjp(rms_norm, after_attn, gain_second)
    grad_norm_in, grad_gain_second = second_back(grad_routed)
    grad_after_attn = grad_after_moe + grad_norm_in
    grad_attn_low = grad_after_attn.astype(bf16)
    output_grad = jnp.einsum("td,te->de", mixed_all, grad_attn_low, preferred_element_type=f32)
    grad_mixed = jnp.einsum(
        "te,de->td", grad_attn_low, attention_full[3 * model_width :], preferred_element_type=f32
    ).astype(bf16)
    grad_queries_low, grad_keys_low, grad_values_low, edge_sums = attend_back(
        queries,
        keys_all,
        values_all,
        grad_mixed,
        log_totals,
        buckets,
        bias_lines,
        prefix,
        edges,
        block_rows,
    )
    grad_queries_low, grad_keys_low, grad_values_low, edge_sums, inward_grad = (
        lax.optimization_barrier(
            (grad_queries_low, grad_keys_low, grad_values_low, edge_sums, inward_grad)
        )
    )
    edge_sums = jnp.sum(edge_sums, axis=1)[:, :NB]
    grad_bias = edge_sums - jnp.pad(edge_sums[:, 1:], ((0, 0), (0, 1)))
    projection_grads = []
    grad_normed_first = jnp.zeros((length, model_width), f32)
    for position, gradient_low in enumerate((grad_queries_low, grad_keys_low, grad_values_low)):
        projection_grads.append(
            jnp.einsum("td,te->de", normed_first, gradient_low, preferred_element_type=f32)
        )
        grad_normed_first = grad_normed_first + jnp.einsum(
            "te,de->td",
            gradient_low,
            attention_full[position * model_width : (position + 1) * model_width],
            preferred_element_type=f32,
        )
    attention_grad = jnp.concatenate(projection_grads + [output_grad], axis=0)
    _, first_back = jax.vjp(rms_norm, embedded, gain_first)
    grad_embed_in, grad_gain_first = first_back(grad_normed_first)
    grad_embedded = (grad_after_attn + grad_embed_in) * math.sqrt(model_width)
    params_grad = jnp.concatenate(
        [grad_gain_first, grad_gain_second, grad_gain_final, grad_bias.reshape(-1)]
    )
    ask_sums = take_rows_wide(ask_mask.T, grad_embedded).astype(bf16)
    attention_blocks = jnp.pad(
        attention_grad.astype(bf16).reshape(devices // 2, 2, attention_rows, model_width),
        ((0, 0), (0, 0), (0, attention_pad), (0, 0)),
    )
    small_blocks = pack_blocks(
        (router_grad.reshape(devices, router_size), params_grad.reshape(devices, params_size)),
        devices,
    )
    ask_sums, small_sums, attention_share = tail_exchange(
        ask_sums.reshape(devices, ASK, model_width), small_blocks, attention_blocks, 9
    )
    ask_sums, small_sums, attention_share, outward_grad = lax.optimization_barrier(
        (ask_sums, small_sums, attention_share, outward_grad)
    )
    attention_share = attention_share[:attention_rows]
    small_share = jnp.sum(small_sums.reshape(devices, -1), axis=0)

    def lookup_wide():
        whole = jnp.zeros((devices * vocab_rows, model_width), f32).at[token_ids].add(grad_embedded)
        return lax.psum_scatter(whole, "fsdp", scatter_dimension=0, tiled=True)

    table_share = table_grad + lax.cond(
        crowded,
        lookup_wide,
        lambda: take_rows(wanted_mask.T, ask_sums.reshape(devices * ASK, model_width)),
    )
    router_share = small_share[:router_size]
    params_share = small_share[router_size : router_size + params_size]
    local_square = (
        jnp.sum(table_share * table_share)
        + jnp.sum(attention_share * attention_share)
        + jnp.sum(router_share * router_share)
        + jnp.sum(params_share * params_share)
        + jnp.sum(inward_grad * inward_grad)
        + jnp.sum(outward_grad * outward_grad)
    )
    total_square = jnp.sum(
        swap_blocks(pack_blocks((local_square.reshape(1, 1),), devices), 1, 11).reshape(devices, -1)[
            :, 0
        ]
    )
    grad_norm = jnp.sqrt(total_square)
    threshold = clip_base / math.sqrt(devices * rows_loss)
    factor = jnp.minimum(1.0, threshold / grad_norm)
    loss_parts = (loss_local * scale_rows).reshape(1)
    table_m, table_s, table_u = adam_step(
        embedding, embedding_moment, embedding_square, table_share, factor
    )
    attention_m, attention_s, attention_u = adam_step(
        attention_weights, attention_moment, attention_square, attention_share, factor
    )
    router_m, router_s, router_u = adam_step(
        router_weights, router_moment, router_square, router_share, factor
    )
    params_m, params_s, params_u = adam_step(
        small_params, params_moment, params_square, params_share, factor
    )
    inward_m, inward_s, inward_u = adam_step(
        inward_weights, inward_moment, inward_square, inward_grad, factor
    )
    outward_m, outward_s, outward_u = adam_step(
        outward_weights, outward_moment, outward_square, outward_grad, factor
    )
    return (
        loss_parts,
        grad_norm,
        table_m,
        table_s,
        table_u,
        attention_m,
        attention_s,
        attention_u,
        router_m,
        router_s,
        router_u,
        params_m,
        params_s,
        params_u,
        inward_m,
        inward_s,
        inward_u,
        outward_m,
        outward_s,
        outward_u,
    )


def solution(mesh):
    placed = (
        P("fsdp"),
        P("fsdp"),
        P("fsdp", None),
        P("fsdp", None),
        P("fsdp", None),
        P("fsdp"),
        P("fsdp", None),
        P("fsdp", None),
        P("fsdp", None),
        P("fsdp"),
        P("fsdp"),
        P("fsdp", None, None),
        P("fsdp", None, None),
        P("fsdp", None),
        P("fsdp", None),
        P("fsdp", None),
        P("fsdp", None),
        P("fsdp"),
        P("fsdp"),
        P("fsdp"),
        P("fsdp"),
        P("fsdp", None, None),
        P("fsdp", None, None),
        P("fsdp", None, None),
        P("fsdp", None, None),
    )
    return jax.shard_map(
        local,
        mesh=mesh,
        in_specs=placed,
        out_specs=(
            P("fsdp"),
            P(),
            P("fsdp", None),
            P("fsdp", None),
            P("fsdp", None),
            P("fsdp", None),
            P("fsdp", None),
            P("fsdp", None),
            P("fsdp"),
            P("fsdp"),
            P("fsdp"),
            P("fsdp"),
            P("fsdp"),
            P("fsdp"),
            P("fsdp", None, None),
            P("fsdp", None, None),
            P("fsdp", None, None),
            P("fsdp", None, None),
            P("fsdp", None, None),
            P("fsdp", None, None),
        ),
        check_vma=False,
    )
```

```python
import functools
import math

import jax
import jax.numpy as jnp
from jax import lax
from jax.experimental import pallas as pl
from jax.experimental.pallas import tpu as pltpu
from jax.sharding import PartitionSpec as P

HEADS = 12
NB = 32
SPLIT = 4
STEP = 10
ASK = 48
BLOCK = 4
WINDOW = 3
NT = (((1,), (1,)), ((), ()))
TN = (((0,), (0,)), ((), ()))
MESH = pl.DeviceIdType.MESH


bucket_marks = (16, 23, 32, 45, 64, 91, 128, 181, 256, 362, 512, 724, 1024, 1448, 2048, 2896)
learn_rate = 0.02
weight_decay = 0.1
clip_base = 8.0


def rms_norm(values, gains):
    return values * lax.rsqrt(jnp.mean(values * values, axis=-1, keepdims=True) + 1e-06) * gains


def bucket_of(distance):
    distance = jnp.maximum(distance, 0)
    bucket = jnp.minimum(distance, 15)
    for border in bucket_marks:
        bucket = bucket + (distance >= border).astype(jnp.int32)
    return bucket


def tree_layout(segments, parents):
    segment_count = parents.shape[0]
    identity_rows = jnp.eye(segment_count, dtype=jnp.float32)
    parent_rows = (parents[:, None] == jnp.arange(segment_count, dtype=jnp.int32)[None, :]).astype(
        jnp.float32
    )
    ancestry = jnp.minimum(identity_rows + parent_rows, 1.0)
    reached = 1
    while reached < segment_count - 1:
        ancestry = jnp.minimum(jnp.dot(ancestry, ancestry), 1.0)
        reached = 2 * reached
    member = (segments[:, None] == jnp.arange(segment_count, dtype=jnp.int32)[None, :]).astype(
        jnp.int32
    )
    lengths = jnp.sum(member, axis=0)
    starts = jnp.cumsum(lengths) - lengths
    before = jnp.sum((ancestry - identity_rows).astype(jnp.int32) * lengths[None, :], axis=1)
    tree_depth = jnp.sum(member * (before - starts)[None, :], axis=1) + jnp.arange(
        segments.shape[0], dtype=jnp.int32
    )
    reach_rows = jnp.dot(member.astype(jnp.float32), ancestry)
    linked = jnp.dot(reach_rows, member.astype(jnp.float32).T) > 0.5
    order = jnp.arange(segments.shape[0], dtype=jnp.int32)
    allowed = linked & (order[None, :] <= order[:, None])
    buckets = jnp.where(allowed, bucket_of(tree_depth[:, None] - tree_depth[None, :]), NB)
    prefix = (tree_depth[:, None] <= order[None, :]).astype(jnp.bfloat16)
    begins = jnp.asarray(tuple(range(16)) + bucket_marks, jnp.int32)
    edges = jnp.pad(
        tree_depth[:, None] - begins[None, :], ((0, 0), (0, 128 - NB)), constant_values=-1
    )
    return (buckets.astype(jnp.int32), prefix, edges)


def swap_kernel(peers, stride, src, dst, send_sems, recv_sems, own_sem):
    me = lax.axis_index("fsdp")
    spot, lane = me // stride, lax.rem(me, stride)
    barrier = pltpu.get_barrier_semaphore()

    def greet(step, carry):
        other = lax.rem(spot + step, peers) * stride + lane
        pl.semaphore_signal(barrier, inc=1, device_id=(other,), device_id_type=MESH)
        return carry

    lax.fori_loop(1, peers, greet, 0)
    pl.semaphore_wait(barrier, peers - 1)

    def transfer(step):
        other = lax.rem(spot + step, peers)
        return pltpu.make_async_remote_copy(
            src_ref=src.at[other],
            dst_ref=dst.at[spot],
            send_sem=send_sems.at[step],
            recv_sem=recv_sems.at[step],
            device_id=(other * stride + lane,),
            device_id_type=MESH,
        )

    def begin(step, carry):
        transfer(step).start()
        return carry

    lax.fori_loop(1, peers, begin, 0)
    own = pltpu.make_async_copy(src.at[spot], dst.at[spot], own_sem)
    own.start()

    def finish(step, carry):
        origin = lax.rem(spot + peers - step, peers)
        transfer(step).wait_send()
        pltpu.make_async_remote_copy(
            src_ref=src.at[origin],
            dst_ref=dst.at[origin],
            send_sem=send_sems.at[step],
            recv_sem=recv_sems.at[step],
            device_id=(origin * stride + lane,),
            device_id_type=MESH,
        ).wait_recv()
        return carry

    lax.fori_loop(1, peers, finish, 0)
    own.wait()


def swap_blocks(blocks, stride, call_id):
    peers = blocks.shape[0]
    return pl.pallas_call(
        functools.partial(swap_kernel, peers, stride),
        out_shape=jax.ShapeDtypeStruct(blocks.shape, blocks.dtype),
        in_specs=[pl.BlockSpec(memory_space=pl.ANY)],
        out_specs=pl.BlockSpec(memory_space=pl.ANY),
        scratch_shapes=[
            pltpu.SemaphoreType.DMA((peers,)),
            pltpu.SemaphoreType.DMA((peers,)),
            pltpu.SemaphoreType.DMA,
        ],
        compiler_params=pltpu.CompilerParams(collective_id=call_id, has_side_effects=True),
    )(blocks)


def around(step, size, at):
    return lax.rem(at + step, size)


def meet(others):
    barrier = pltpu.get_barrier_semaphore()
    for other in others:
        pl.semaphore_signal(barrier, inc=1, device_id=(other,), device_id_type=MESH)
    pl.semaphore_wait(barrier, len(others))


def chip_place(chips):
    me = lax.axis_index("fsdp")
    core = lax.rem(me, 2)
    chip = me // 2
    layers = chips // BLOCK
    layer, col = chip // BLOCK, lax.rem(chip, BLOCK)

    def device(other_layer, other_col):
        return (other_layer * BLOCK + other_col) * 2 + core

    others = [device(around(step, layers, layer), col) for step in range(1, layers)]
    others += [device(layer, around(turn, BLOCK, col)) for turn in range(1, BLOCK)]
    return layers, layer, col, device, others


def loss_kernel(
    chips,
    scale,
    picked,
    table,
    ids,
    targets,
    out,
    own_grad,
    far_grad,
    loss_rows,
    rows,
    scores,
    pulls,
    picks,
    stat_out,
    stat_in,
    log_out,
    log_in,
    col_in,
    layer_out,
    layer_in,
    table_t,
    own_sem,
    layer_send,
    layer_recv,
    col_send,
    col_recv,
    sum_layer_send,
    sum_layer_recv,
    sum_col_send,
    sum_col_recv,
    stat_send,
    stat_recv,
    log_send,
    log_recv,
):
    layers, layer, col, device, _ = chip_place(chips)
    core = lax.rem(lax.axis_index("fsdp"), 2)
    chip = layer * BLOCK + col
    f32 = jnp.float32
    bf16 = jnp.bfloat16
    count, width = picked.shape
    group = BLOCK * count
    lines_all = table.shape[0]
    half_lines = lines_all // 2
    lines_step = min(512, half_lines)
    line_steps = lines_all // lines_step
    barrier = pltpu.get_barrier_semaphore()

    def far_chip(shift):
        return lax.rem(chip + shift, chips)

    def greet(shift, carry):
        pl.semaphore_signal(
            barrier, inc=1, device_id=(far_chip(shift) * 2 + core,), device_id_type=MESH
        )
        return carry

    lax.fori_loop(1, chips, greet, 0)
    pl.semaphore_wait(barrier, chips - 1)

    def to_layer(step, at):
        return pltpu.make_async_remote_copy(
            src_ref=picked,
            dst_ref=rows.at[at],
            send_sem=layer_send.at[step],
            recv_sem=layer_recv.at[step],
            device_id=(device(around(step, layers, layer), col),),
            device_id_type=MESH,
        )

    def to_col(step, turn, source, at):
        return pltpu.make_async_remote_copy(
            src_ref=source,
            dst_ref=rows.at[at],
            send_sem=col_send.at[step, turn],
            recv_sem=col_recv.at[step, turn],
            device_id=(device(layer, around(turn, BLOCK, col)),),
            device_id_type=MESH,
        )

    def origin(step, turn):
        return around(layers - step, layers, layer) * BLOCK + around(BLOCK - turn, BLOCK, col)

    def layer_start(step, carry):
        to_layer(step, chip).start()
        return carry

    lax.fori_loop(1, layers, layer_start, 0)
    for turn in range(1, BLOCK):
        to_col(0, turn, picked, chip).start()
    own = pltpu.make_async_copy(picked, rows.at[chip], own_sem)
    own.start()
    own_grad[...] = jnp.zeros_like(own_grad)
    far_grad[...] = jnp.zeros_like(far_grad)
    stat_out[...] = jnp.zeros_like(stat_out)
    for number in range(line_steps):
        lines = slice(number * lines_step, (number + 1) * lines_step)
        table_t[:, lines] = table[lines, :].T
    own.wait()

    def lines_of(number):
        return pl.ds(pl.multiple_of(number * lines_step, lines_step), lines_step)

    def layer_rows(far):
        return rows[pl.ds(far * BLOCK, BLOCK)].reshape(group, width)

    def score(lines, block):
        values = lax.dot_general(table[lines, :], block, NT, preferred_element_type=f32)
        return jnp.where(ids[lines, :] >= 0, values, -1e30)

    def to_owner(at):
        return pltpu.make_async_remote_copy(
            src_ref=stat_out.at[at],
            dst_ref=stat_in.at[chip],
            send_sem=stat_send.at[at],
            recv_sem=stat_recv.at[chip],
            device_id=(at * 2 + core,),
            device_id_type=MESH,
        )

    def from_chip(at):
        return pltpu.make_async_remote_copy(
            src_ref=stat_out.at[at],
            dst_ref=stat_in.at[at],
            send_sem=stat_send.at[at],
            recv_sem=stat_recv.at[at],
            device_id=(at * 2 + core,),
            device_id_type=MESH,
        )

    def measure(step, far):
        block = layer_rows(far)
        first = targets[far, 0:1, :]
        second = targets[far, 1:2, :]

        def peak_of(number, peak):
            lines = lines_of(number)
            values = score(lines, block)
            scores[lines, :] = values
            return jnp.maximum(peak, jnp.max(values, axis=0, keepdims=True))

        peak = lax.fori_loop(0, line_steps, peak_of, jnp.full((1, group), -1e30, f32))

        def total_of(number, carry):
            total, first_sum, second_sum = carry
            lines = lines_of(number)
            values = scores[lines, :]
            vocab = ids[lines, :]
            total = total + jnp.sum(jnp.exp(values - peak), axis=0, keepdims=True)
            first_sum = first_sum + jnp.sum(
                jnp.where(vocab == first, values, 0.0), axis=0, keepdims=True
            )
            second_sum = second_sum + jnp.sum(
                jnp.where(vocab == second, values, 0.0), axis=0, keepdims=True
            )
            return total, first_sum, second_sum

        zero = jnp.zeros((1, group), f32)
        sums = lax.fori_loop(0, line_steps, total_of, (zero, zero, zero))
        for part in range(BLOCK):
            lanes = slice(part * count, (part + 1) * count)
            at = far * BLOCK + part
            stat_out[at, 0:1, :] = peak[:, lanes]
            for number in range(3):
                stat_out[at, number + 1 : number + 2, :] = sums[number][:, lanes]

            @pl.when(jnp.logical_or(step != 0, part != col))
            def _():
                to_owner(at).start()

    def layer_pass(step, carry):
        at = origin(step, 0)

        @pl.when(step > 0)
        def _():
            to_layer(step, at).wait_recv()
            for turn in range(1, BLOCK):
                to_col(step, turn, rows.at[at], at).start()

        return carry

    def layer_measure(step, carry):
        for turn in range(1, BLOCK):
            at = origin(step, turn)
            to_col(step, turn, rows.at[at], at).wait_recv()
        measure(step, around(layers - step, layers, layer))
        return carry

    lax.fori_loop(0, layers, layer_pass, 0)
    lax.fori_loop(0, layers, layer_measure, 0)
    stat_in[chip] = stat_out[chip]

    def stat_wait(shift, carry):
        from_chip(far_chip(shift)).wait_recv()
        return carry

    lax.fori_loop(1, chips, stat_wait, 0)
    peaks = stat_in[:, 0, :]
    peak = jnp.max(peaks, axis=0, keepdims=True)
    total = jnp.sum(stat_in[:, 1, :] * jnp.exp(peaks - peak), axis=0, keepdims=True)
    first_hit = jnp.sum(stat_in[:, 2, :], axis=0, keepdims=True)
    second_hit = jnp.sum(stat_in[:, 3, :], axis=0, keepdims=True)
    log_rows = peak + jnp.log(total)
    loss_rows[...] = jnp.broadcast_to(
        log_rows - first_hit + 0.3 * (log_rows - second_hit), loss_rows.shape
    )
    log_out[...] = jnp.broadcast_to(log_rows, log_out.shape)
    log_in[chip] = log_out[...]

    def to_chip(shift, at):
        return pltpu.make_async_remote_copy(
            src_ref=log_out,
            dst_ref=log_in.at[at],
            send_sem=log_send.at[shift],
            recv_sem=log_recv.at[at],
            device_id=(far_chip(shift) * 2 + core,),
            device_id_type=MESH,
        )

    def log_begin(shift, carry):
        to_chip(shift, chip).start()
        return carry

    def log_wait(shift, carry):
        to_chip(shift, far_chip(shift)).wait_recv()
        return carry

    lax.fori_loop(1, chips, log_begin, 0)
    lax.fori_loop(1, chips, log_wait, 0)

    def pull_back(step):
        far = around(step, layers, layer)
        block = layer_rows(far)
        first = targets[far, 0:1, :]
        second = targets[far, 1:2, :]
        logs = jnp.concatenate(
            [log_in[far * BLOCK + part, 0:1, :] for part in range(BLOCK)], axis=1
        )

        for number in range(line_steps):
            start = number * lines_step
            lines = slice(start, start + lines_step)
            grad = own_grad if start < half_lines else far_grad
            place = slice(start % half_lines, start % half_lines + lines_step)
            vocab = ids[lines, :]
            pull = (
                1.3 * jnp.exp(score(lines, block) - logs)
                - (vocab == first).astype(f32)
                - 0.3 * (vocab == second).astype(f32)
            )
            pull = (pull * scale).astype(bf16)
            pulls[lines, :] = pull
            grad[place, :] += jnp.dot(pull, block, preferred_element_type=f32)
        grads = jnp.dot(table_t[...], pulls[...], preferred_element_type=f32).astype(bf16)
        for part in range(BLOCK):
            picks[step, part] = grads[:, part * count : (part + 1) * count]

    def sum_to_col(step, turn):
        return pltpu.make_async_remote_copy(
            src_ref=picks.at[step, around(turn, BLOCK, col)],
            dst_ref=col_in.at[step, turn],
            send_sem=sum_col_send.at[step, turn],
            recv_sem=sum_col_recv.at[step, turn],
            device_id=(device(layer, around(turn, BLOCK, col)),),
            device_id_type=MESH,
        )

    def sum_to_layer(step):
        return pltpu.make_async_remote_copy(
            src_ref=layer_out.at[step],
            dst_ref=layer_in.at[step],
            send_sem=sum_layer_send.at[step],
            recv_sem=sum_layer_recv.at[step],
            device_id=(device(around(step, layers, layer), col),),
            device_id_type=MESH,
        )

    def block_sum(step):
        total = picks[step, col].astype(f32)
        for turn in range(1, BLOCK):
            sum_to_col(step, turn).wait_recv()
            total = total + col_in[step, turn].astype(f32)
        return total

    def pull_pass(number, carry):
        step = lax.rem(number + 1, layers)
        pull_back(step)
        for turn in range(1, BLOCK):
            sum_to_col(step, turn).start()

        @pl.when(number > 0)
        def _():
            layer_out[number] = block_sum(number).astype(bf16)
            sum_to_layer(number).start()

        return carry

    lax.fori_loop(0, layers, pull_pass, 0)
    out[...] = block_sum(0)

    def layer_finish(step, carry):
        sum_to_layer(step).wait_recv()
        out[...] += layer_in[step].astype(f32)
        sum_to_layer(step).wait_send()
        to_layer(step, chip).wait_send()
        return carry

    def col_finish(step, carry):
        for turn in range(1, BLOCK):
            to_col(step, turn, picked, chip).wait_send()
            sum_to_col(step, turn).wait_send()
        return carry

    def small_finish(shift, carry):
        from_chip(far_chip(shift)).wait_send()
        to_chip(shift, chip).wait_send()
        return carry

    lax.fori_loop(1, layers, layer_finish, 0)
    lax.fori_loop(0, layers, col_finish, 0)
    lax.fori_loop(1, chips, small_finish, 0)


def loss_exchange(picked, table, ids, targets, chips, scale, call_id):
    count, width = picked.shape
    layers = chips // BLOCK
    group = BLOCK * count
    lines_all = table.shape[0]
    f32 = jnp.float32
    bf16 = jnp.bfloat16
    near = pl.BlockSpec(memory_space=pltpu.VMEM)
    return pl.pallas_call(
        functools.partial(loss_kernel, chips, scale),
        out_shape=[
            jax.ShapeDtypeStruct((width, count), f32),
            jax.ShapeDtypeStruct((lines_all // 2, width), f32),
            jax.ShapeDtypeStruct((lines_all // 2, width), f32),
            jax.ShapeDtypeStruct((8, count), f32),
        ],
        in_specs=[pl.BlockSpec(memory_space=pl.ANY)] + [near] * 3,
        out_specs=[near] * 4,
        scratch_shapes=[
            pltpu.VMEM((chips, count, width), bf16),
            pltpu.VMEM((lines_all, group), f32),
            pltpu.VMEM((lines_all, group), bf16),
            pltpu.VMEM((layers, BLOCK, width, count), bf16),
            pltpu.VMEM((chips, 8, count), f32),
            pltpu.VMEM((chips, 8, count), f32),
            pltpu.VMEM((8, count), f32),
            pltpu.VMEM((chips, 8, count), f32),
            pltpu.VMEM((layers, BLOCK, width, count), bf16),
            pltpu.VMEM((layers, width, count), bf16),
            pltpu.VMEM((layers, width, count), bf16),
            pltpu.VMEM((width, lines_all), bf16),
            pltpu.SemaphoreType.DMA,
        ]
        + (
            [pltpu.SemaphoreType.DMA((layers,))] * 2
            + [pltpu.SemaphoreType.DMA((layers, BLOCK))] * 2
        )
        * 2
        + [pltpu.SemaphoreType.DMA((chips,))] * 4,
        compiler_params=pltpu.CompilerParams(
            collective_id=call_id, has_side_effects=True, vmem_limit_bytes=60 * 1024 * 1024
        ),
    )(picked, table, ids, targets)


def gelu_parts(values):
    root = math.sqrt(2.0 / math.pi)
    squared = values * values
    bend = jnp.tanh(root * (values + 0.044715 * (squared * values)))
    half = 0.5 * (1.0 + bend)
    slope = half + 0.5 * values * (1.0 - bend * bend) * (root * (1.0 + 0.134145 * squared))
    return values * half, slope


def trade_copies(peers, src, landed, done, returned, sems):
    me = lax.axis_index("fsdp")
    spot, lane = me // SPLIT, lax.rem(me, SPLIT)
    go_send, go_recv, back_send, back_recv = sems

    def device(other):
        return (other * SPLIT + lane,)

    def ahead(step):
        return lax.rem(spot + step, peers)

    def behind(step):
        return lax.rem(spot + peers - step, peers)

    def go(step, at):
        return pltpu.make_async_remote_copy(
            src_ref=src.at[ahead(step)],
            dst_ref=landed.at[at],
            send_sem=go_send.at[step],
            recv_sem=go_recv.at[step],
            device_id=device(ahead(step)),
            device_id_type=MESH,
        )

    def back(step, source, at):
        return pltpu.make_async_remote_copy(
            src_ref=done.at[source],
            dst_ref=returned.at[at],
            send_sem=back_send.at[step],
            recv_sem=back_recv.at[step],
            device_id=device(behind(step)),
            device_id_type=MESH,
        )

    barrier = pltpu.get_barrier_semaphore()

    def greet(step, carry):
        pl.semaphore_signal(barrier, inc=1, device_id=device(ahead(step)), device_id_type=MESH)
        return carry

    lax.fori_loop(1, peers, greet, 0)
    pl.semaphore_wait(barrier, peers - 1)
    return spot, behind, ahead, go, back


def trade_loop(peers, copies, build, work, collect):
    spot, behind, ahead, go, back = copies
    window = min(WINDOW, peers - 1)

    def begin(step, carry):
        build(ahead(step))
        go(step, spot).start()
        return carry

    lax.fori_loop(1, window + 1, begin, 0)
    build(spot)
    work(spot, True)

    def visit(step, carry):
        origin = behind(step)

        @pl.when(step + window < peers)
        def _():
            build(ahead(step + window))
            go(step + window, spot).start()

        go(step, origin).wait_recv()
        work(origin, False)
        back(step, origin, spot).start()
        return carry

    lax.fori_loop(1, peers, visit, 0)
    collect(spot, True)

    def finish(step, carry):
        back(step, spot, ahead(step)).wait_recv()
        collect(ahead(step), False)
        return carry

    def close(step, carry):
        go(step, spot).wait_send()
        back(step, behind(step), spot).wait_send()
        return carry

    lax.fori_loop(1, peers, finish, 0)
    lax.fori_loop(1, peers, close, 0)


def slot_mask(marks, at, slots):
    slot = at * slots + lax.broadcasted_iota(jnp.int32, (slots, 1), 0)
    return [jnp.where(mark == slot, 1.0, 0.0).astype(jnp.bfloat16) for mark in marks]


def experts_kernel(
    peers,
    tokens,
    marks,
    places,
    inward,
    outward,
    landed,
    first_out,
    second_out,
    src,
    done,
    returned,
    *sems,
):
    copies = trade_copies(peers, src, landed, done, returned, sems)
    spot = copies[0]
    f32 = jnp.float32
    slots = src.shape[1]

    def build(at):
        first, second = slot_mask((marks[0:1, :], marks[1:2, :]), at, slots)
        block = jnp.dot(first + second, tokens[...], preferred_element_type=f32)
        src[at] = block.astype(jnp.bfloat16)

    def work(at, own):
        rows = src[at] if own else landed[at]
        if own:
            landed[at] = rows
        total = jnp.zeros(rows.shape, f32)
        for quarter in range(SPLIT):
            before = jnp.dot(rows, inward[quarter], preferred_element_type=f32)
            hidden = gelu_parts(before)[0].astype(jnp.bfloat16)
            total = total + jnp.dot(hidden, outward[quarter], preferred_element_type=f32).astype(
                jnp.bfloat16
            ).astype(f32)
        done[at] = total.astype(jnp.bfloat16)

    def collect(at, own):
        rows = done[at] if own else returned[at]
        slot = at * slots + lax.broadcasted_iota(jnp.int32, (1, slots), 1)
        for number, out in enumerate((first_out, second_out)):
            mask = jnp.where(places[:, number : number + 1] == slot, 1.0, 0.0).astype(jnp.bfloat16)
            picked = jnp.dot(mask, rows, preferred_element_type=f32)
            if own:
                out[...] = picked
            else:
                out[...] += picked

    trade_loop(peers, copies, build, work, collect)


def experts_back_kernel(
    peers,
    first_grads,
    second_grads,
    marks,
    rows_ref,
    inward,
    outward,
    returned,
    inward_grad,
    outward_grad,
    src,
    landed,
    done,
    own_sem,
    *sems,
):
    copies = trade_copies(peers, src, landed, done, returned, sems)
    spot = copies[0]
    f32 = jnp.float32
    slots = src.shape[1]

    def build(at):
        first, second = slot_mask((marks[0:1, :], marks[1:2, :]), at, slots)
        block = jnp.dot(first, first_grads[...], preferred_element_type=f32)
        block = block + jnp.dot(second, second_grads[...], preferred_element_type=f32)
        src[at] = block.astype(jnp.bfloat16)

    def work(at, own):
        rows = rows_ref[at]
        grads = src[at] if own else landed[at]
        total = jnp.zeros(rows.shape, f32)
        for quarter in range(SPLIT):
            before = jnp.dot(rows, inward[quarter], preferred_element_type=f32)
            hidden, slope = gelu_parts(before)
            grad_hidden = lax.dot_general(grads, outward[quarter], NT, preferred_element_type=f32)
            grad_before = (grad_hidden * slope).astype(jnp.bfloat16)
            total = total + lax.dot_general(
                grad_before, inward[quarter], NT, preferred_element_type=f32
            ).astype(jnp.bfloat16).astype(f32)
            for grad, left, right in (
                (inward_grad, rows, grad_before),
                (outward_grad, hidden.astype(jnp.bfloat16), grads),
            ):
                part = lax.dot_general(left, right, TN, preferred_element_type=f32)
                if own:
                    grad[quarter] = part
                else:
                    grad[quarter] += part
        done[at] = total.astype(jnp.bfloat16)

    def collect(at, own):
        if own:
            copy = pltpu.make_async_copy(done.at[at], returned.at[at], own_sem)
            copy.start()
            copy.wait()

    trade_loop(peers, copies, build, work, collect)


def experts_call(body, call_id, operands, outs, scratch, peers):
    anywhere = pl.BlockSpec(memory_space=pl.ANY)
    near = pl.BlockSpec(memory_space=pltpu.VMEM)
    return pl.pallas_call(
        functools.partial(body, peers),
        out_shape=[shape for shape, _ in outs],
        in_specs=[near] * len(operands),
        out_specs=[near if inside else anywhere for _, inside in outs],
        scratch_shapes=scratch + [pltpu.SemaphoreType.DMA((peers,))] * 4,
        compiler_params=pltpu.CompilerParams(
            collective_id=call_id, has_side_effects=True, vmem_limit_bytes=60 * 1024 * 1024
        ),
    )(*operands)


def run_experts(tokens, marks, places, inward, outward, peers, slots, call_id):
    block = (peers, slots, tokens.shape[1])
    low = jax.ShapeDtypeStruct(block, tokens.dtype)
    wide = jax.ShapeDtypeStruct(tokens.shape, jnp.float32)
    return experts_call(
        experts_kernel,
        call_id,
        (tokens, marks, places, inward, outward),
        [(low, True), (wide, True), (wide, True)],
        [pltpu.VMEM(block, tokens.dtype)] * 3,
        peers,
    )


def run_experts_back(first_grads, second_grads, marks, rows, inward, outward, call_id):
    low = jax.ShapeDtypeStruct(rows.shape, rows.dtype)
    wide = jax.ShapeDtypeStruct(inward.shape, jnp.float32)
    return experts_call(
        experts_back_kernel,
        call_id,
        (first_grads, second_grads, marks, rows, inward, outward),
        [(low, False), (wide, True), (wide, True)],
        [pltpu.VMEM(rows.shape, rows.dtype)] * 3 + [pltpu.SemaphoreType.DMA],
        rows.shape[0],
    )


def meet_all(devices):
    me = lax.axis_index("fsdp")
    barrier = pltpu.get_barrier_semaphore()

    def greet(step, carry):
        other = lax.rem(me + step, devices)
        pl.semaphore_signal(barrier, inc=1, device_id=(other,), device_id_type=MESH)
        return carry

    lax.fori_loop(1, devices, greet, 0)
    pl.semaphore_wait(barrier, devices - 1)


def swap_parts(devices, src, dst, send_sems, recv_sems, own_sem):
    me = lax.axis_index("fsdp")

    def transfer(step, at):
        other = lax.rem(me + step, devices)
        return pltpu.make_async_remote_copy(
            src_ref=src.at[other],
            dst_ref=dst.at[at],
            send_sem=send_sems.at[step],
            recv_sem=recv_sems.at[step],
            device_id=(other,),
            device_id_type=MESH,
        )

    own = pltpu.make_async_copy(src.at[me], dst.at[me], own_sem)

    def begin():
        def one(step, carry):
            transfer(step, me).start()
            return carry

        lax.fori_loop(1, devices, one, 0)
        own.start()

    def finish():
        def one(step, carry):
            transfer(step, me).wait_send()
            transfer(step, lax.rem(me + devices - step, devices)).wait_recv()
            return carry

        lax.fori_loop(1, devices, one, 0)
        own.wait()

    return begin, finish


def tail_kernel(
    chips,
    token_src,
    small_src,
    src,
    token_dst,
    small_dst,
    out,
    core_in,
    col_out,
    col_in,
    layer_out,
    layer_in,
    core_send,
    core_recv,
    layer_send,
    layer_recv,
    col_send,
    col_recv,
    *swap_sems,
):
    layers, layer, col, device, _ = chip_place(chips)
    me = lax.axis_index("fsdp")
    core = lax.rem(me, 2)
    f32 = jnp.float32
    token_begin, token_finish = swap_parts(2 * chips, token_src, token_dst, *swap_sems[:3])
    small_begin, small_finish = swap_parts(2 * chips, small_src, small_dst, *swap_sems[3:])
    meet_all(2 * chips)

    def place(step, turn):
        return around(step, layers, layer) * BLOCK + around(turn, BLOCK, col)

    def to_core(step, turn):
        return pltpu.make_async_remote_copy(
            src_ref=src.at[place(step, turn), 1 - core],
            dst_ref=core_in.at[step, turn],
            send_sem=core_send.at[step, turn],
            recv_sem=core_recv.at[step, turn],
            device_id=(me + 1 - 2 * core,),
            device_id_type=MESH,
        )

    def to_col(step, turn):
        return pltpu.make_async_remote_copy(
            src_ref=col_out.at[step, turn],
            dst_ref=col_in.at[step, turn],
            send_sem=col_send.at[step, turn],
            recv_sem=col_recv.at[step, turn],
            device_id=(device(layer, around(turn, BLOCK, col)),),
            device_id_type=MESH,
        )

    def to_layer(step):
        return pltpu.make_async_remote_copy(
            src_ref=layer_out.at[step],
            dst_ref=layer_in.at[step],
            send_sem=layer_send.at[step],
            recv_sem=layer_recv.at[step],
            device_id=(device(around(step, layers, layer), col),),
            device_id_type=MESH,
        )

    def chip_sum(step, turn):
        to_core(step, turn).wait_recv()
        return src[place(step, turn), core].astype(f32) + core_in[step, turn].astype(f32)

    def block_sum(step):
        total = chip_sum(step, 0)
        for turn in range(1, BLOCK):
            to_col(step, turn).wait_recv()
            total = total + col_in[step, turn].astype(f32)
        return total

    def step_of(number):
        return lax.rem(number + 1, layers)

    def core_begin(number, carry):
        for turn in range(BLOCK):
            to_core(step_of(number), lax.rem(turn + 1, BLOCK)).start()
        return carry

    def col_begin(number, carry):
        step = step_of(number)
        for turn in range(1, BLOCK):
            col_out[step, turn] = chip_sum(step, turn).astype(jnp.bfloat16)
            to_col(step, turn).start()
        return carry

    def layer_begin(step, carry):
        layer_out[step] = block_sum(step).astype(jnp.bfloat16)
        to_layer(step).start()
        return carry

    lax.fori_loop(0, layers, core_begin, 0)
    small_begin()
    token_begin()
    lax.fori_loop(0, layers, col_begin, 0)
    lax.fori_loop(1, layers, layer_begin, 0)
    out[...] = block_sum(0)

    def layer_finish(step, carry):
        to_layer(step).wait_recv()
        out[...] += layer_in[step].astype(f32)
        to_layer(step).wait_send()
        return carry

    def send_finish(step, carry):
        for turn in range(BLOCK):
            to_core(step, turn).wait_send()
        for turn in range(1, BLOCK):
            to_col(step, turn).wait_send()
        return carry

    lax.fori_loop(1, layers, layer_finish, 0)
    lax.fori_loop(0, layers, send_finish, 0)
    small_finish()
    token_finish()


def tail_exchange(tokens, small, blocks, call_id):
    chips, _, rows, width = blocks.shape
    layers = chips // BLOCK
    devices = 2 * chips
    near = pl.BlockSpec(memory_space=pltpu.VMEM)
    anywhere = pl.BlockSpec(memory_space=pl.ANY)
    grid_block = pltpu.VMEM((layers, BLOCK, rows, width), jnp.bfloat16)
    line_block = pltpu.VMEM((layers, rows, width), jnp.bfloat16)
    return pl.pallas_call(
        functools.partial(tail_kernel, chips),
        out_shape=[
            jax.ShapeDtypeStruct(tokens.shape, tokens.dtype),
            jax.ShapeDtypeStruct(small.shape, small.dtype),
            jax.ShapeDtypeStruct((rows, width), jnp.float32),
        ],
        in_specs=[anywhere, anywhere, near],
        out_specs=[anywhere, anywhere, near],
        scratch_shapes=[grid_block] * 3
        + [line_block] * 2
        + [pltpu.SemaphoreType.DMA((layers, BLOCK))] * 2
        + [pltpu.SemaphoreType.DMA((layers,))] * 2
        + [pltpu.SemaphoreType.DMA((layers, BLOCK))] * 2
        + [
            pltpu.SemaphoreType.DMA((devices,)),
            pltpu.SemaphoreType.DMA((devices,)),
            pltpu.SemaphoreType.DMA,
        ]
        * 2,
        compiler_params=pltpu.CompilerParams(
            collective_id=call_id, has_side_effects=True, vmem_limit_bytes=48 * 1024 * 1024
        ),
    )(tokens, small, blocks)


def head_kernel(
    chips,
    token_src,
    src,
    token_dst,
    dst,
    core_send,
    core_recv,
    layer_send,
    layer_recv,
    col_send,
    col_recv,
    own_sem,
    *swap_sems,
):
    layers, layer, col, device, _ = chip_place(chips)
    me = lax.axis_index("fsdp")
    core = lax.rem(me, 2)
    chip = layer * BLOCK + col
    token_begin, token_finish = swap_parts(2 * chips, token_src, token_dst, *swap_sems)
    meet_all(2 * chips)

    def to_layer(step, at):
        return pltpu.make_async_remote_copy(
            src_ref=src,
            dst_ref=dst.at[at, core],
            send_sem=layer_send.at[step],
            recv_sem=layer_recv.at[step],
            device_id=(device(around(step, layers, layer), col),),
            device_id_type=MESH,
        )

    def to_col(step, turn, source, at):
        return pltpu.make_async_remote_copy(
            src_ref=source,
            dst_ref=dst.at[at, core],
            send_sem=col_send.at[step, turn],
            recv_sem=col_recv.at[step, turn],
            device_id=(device(layer, around(turn, BLOCK, col)),),
            device_id_type=MESH,
        )

    def to_core(step, turn, source, at, side):
        return pltpu.make_async_remote_copy(
            src_ref=source,
            dst_ref=dst.at[at, side],
            send_sem=core_send.at[step, turn],
            recv_sem=core_recv.at[step, turn],
            device_id=(me + 1 - 2 * core,),
            device_id_type=MESH,
        )

    def origin(step, turn):
        return around(layers - step, layers, layer) * BLOCK + around(BLOCK - turn, BLOCK, col)

    def layer_start(step, carry):
        to_layer(step, chip).start()
        return carry

    lax.fori_loop(1, layers, layer_start, 0)
    for turn in range(1, BLOCK):
        to_col(0, turn, src, chip).start()
    to_core(0, 0, src, chip, core).start()
    own = pltpu.make_async_copy(src, dst.at[chip, core], own_sem)
    own.start()
    token_begin()

    def layer_pass(step, carry):
        at = origin(step, 0)
        to_layer(step, at).wait_recv()
        for turn in range(1, BLOCK):
            to_col(step, turn, dst.at[at, core], at).start()
        to_core(step, 0, dst.at[at, core], at, core).start()
        return carry

    lax.fori_loop(1, layers, layer_pass, 0)

    def col_pass(step, carry):
        for turn in range(1, BLOCK):
            at = origin(step, turn)
            to_col(step, turn, dst.at[at, core], at).wait_recv()
            to_core(step, turn, dst.at[at, core], at, core).start()
        return carry

    lax.fori_loop(0, layers, col_pass, 0)

    def layer_done(step, carry):
        to_layer(step, chip).wait_send()
        return carry

    def done(step, carry):
        for turn in range(BLOCK):
            if turn:
                to_col(step, turn, src, chip).wait_send()
            at = origin(step, turn)
            to_core(step, turn, src, at, 1 - core).wait_recv()
            to_core(step, turn, src, at, core).wait_send()
        return carry

    lax.fori_loop(1, layers, layer_done, 0)
    lax.fori_loop(0, layers, done, 0)
    own.wait()
    token_finish()


def head_exchange(tokens, block, call_id):
    devices = tokens.shape[0]
    chips = devices // 2
    layers = chips // BLOCK
    anywhere = pl.BlockSpec(memory_space=pl.ANY)
    return pl.pallas_call(
        functools.partial(head_kernel, chips),
        out_shape=[
            jax.ShapeDtypeStruct(tokens.shape, tokens.dtype),
            jax.ShapeDtypeStruct((chips, 2, *block.shape), block.dtype),
        ],
        in_specs=[anywhere] * 2,
        out_specs=[anywhere] * 2,
        scratch_shapes=[pltpu.SemaphoreType.DMA((layers, BLOCK))] * 2
        + [pltpu.SemaphoreType.DMA((layers,))] * 2
        + [pltpu.SemaphoreType.DMA((layers, BLOCK))] * 2
        + [
            pltpu.SemaphoreType.DMA,
            pltpu.SemaphoreType.DMA((devices,)),
            pltpu.SemaphoreType.DMA((devices,)),
            pltpu.SemaphoreType.DMA,
        ],
        compiler_params=pltpu.CompilerParams(collective_id=call_id, has_side_effects=True),
    )(tokens, block)


def pack_blocks(parts, devices):
    flat = jnp.concatenate(
        [jnp.broadcast_to(part, (devices, part.shape[-1])) for part in parts], axis=1
    )
    rows = -(-flat.shape[1] // 1024) * 8
    flat = jnp.pad(flat, ((0, 0), (0, rows * 128 - flat.shape[1])))
    return flat.reshape(devices, rows, 128)


def take_rows(mask, rows):
    return jnp.dot(mask.astype(jnp.bfloat16), rows, preferred_element_type=jnp.float32)


def take_rows_wide(mask, rows):
    high = lax.reduce_precision(rows, 8, 7)
    both = jnp.concatenate([high, rows - high], axis=1).astype(jnp.bfloat16)
    picked = take_rows(mask, both)
    width = rows.shape[1]
    return picked[:, :width] + picked[:, width:]


def bias_tile(table_row, buckets):
    rows, cols = buckets.shape
    spread = jnp.broadcast_to(table_row, (rows, 128))
    return jnp.concatenate(
        [
            jnp.take_along_axis(
                spread, buckets[:, at : at + 128], axis=1, mode="promise_in_bounds"
            )
            for at in range(0, cols, 128)
        ],
        axis=1,
    )


def attend_kernel(block, length, q_ref, k_ref, v_ref, bucket_ref, table_ref, out_ref, log_ref):
    lower = lax.broadcasted_iota(jnp.int32, (1, 128), 1) < 64
    pair = pl.program_id(0)
    zero = jnp.zeros((), jnp.bfloat16)
    for start in range(0, length, block):
        rows = pl.ds(start, block)
        seen = start + block
        logs = []
        mixed = []
        for half in range(2):
            mine = lower if half == 0 else ~lower
            queries = jnp.where(mine, q_ref[rows, :], zero) * 0.125
            values = jnp.where(mine, v_ref[0:seen, :], zero)
            scores = lax.dot_general(
                queries, k_ref[0:seen, :], NT, preferred_element_type=jnp.float32
            )
            table_row = table_ref[pl.ds(2 * pair + half, 1), :]
            scores = scores + bias_tile(table_row, bucket_ref[rows, 0:seen])
            peak = jnp.max(scores, axis=1, keepdims=True)
            raised = jnp.exp(scores - peak)
            totals = jnp.sum(raised, axis=1, keepdims=True)
            probs = (raised * (1.0 / totals)).astype(jnp.bfloat16)
            mixed.append(jnp.dot(probs, values, preferred_element_type=jnp.float32))
            logs.append(peak + jnp.log(totals))
        out_ref[rows, :] = (mixed[0] + mixed[1]).astype(jnp.bfloat16)
        log_ref[0, rows, :] = jnp.where(lower, logs[0], logs[1])


def attend(queries, keys, values, buckets, table, block):
    length, width = queries.shape
    cols = pl.BlockSpec((length, 128), lambda pair: (0, pair))
    return pl.pallas_call(
        functools.partial(attend_kernel, block, length),
        grid=(width // 128,),
        in_specs=[
            cols,
            cols,
            cols,
            pl.BlockSpec(buckets.shape, lambda pair: (0, 0)),
            pl.BlockSpec(table.shape, lambda pair: (0, 0)),
        ],
        out_specs=[cols, pl.BlockSpec((1, length, 128), lambda pair: (pair, 0, 0))],
        out_shape=[
            jax.ShapeDtypeStruct((length, width), jnp.bfloat16),
            jax.ShapeDtypeStruct((width // 128, length, 128), jnp.float32),
        ],
        compiler_params=pltpu.CompilerParams(vmem_limit_bytes=40 * 1024 * 1024),
    )(queries, keys, values, buckets, table)


def attend_back_kernel(
    block,
    length,
    q_ref,
    k_ref,
    v_ref,
    g_ref,
    log_ref,
    bucket_ref,
    table_ref,
    prefix_ref,
    edge_ref,
    dq_ref,
    dk_ref,
    dv_ref,
    edge_sum_ref,
    dk_acc,
    dv_acc,
):
    lower = lax.broadcasted_iota(jnp.int32, (1, 128), 1) < 64
    pair = pl.program_id(0)
    zero = jnp.zeros((), jnp.bfloat16)
    f32 = jnp.float32
    dk_acc[...] = jnp.zeros_like(dk_acc)
    dv_acc[...] = jnp.zeros_like(dv_acc)
    edge_sums = [jnp.zeros((8, 128), f32)] * 2
    for start in range(0, length, block):
        rows = pl.ds(start, block)
        seen = start + block
        edges = edge_ref[rows, :]
        lane_at = edges & 127
        dq_parts = []
        for half in range(2):
            mine = lower if half == 0 else ~lower
            queries = jnp.where(mine, q_ref[rows, :], zero) * 0.125
            grads = jnp.where(mine, g_ref[rows, :], zero)
            keys = jnp.where(mine, k_ref[0:seen, :], zero)
            scores = lax.dot_general(queries, keys, NT, preferred_element_type=f32)
            table_row = table_ref[pl.ds(2 * pair + half, 1), :]
            scores = scores + bias_tile(table_row, bucket_ref[rows, 0:seen])
            probs = jnp.exp(scores - log_ref[0, rows, 64 * half : 64 * half + 1])
            grad_probs = lax.dot_general(
                grads, v_ref[0:seen, :], NT, preferred_element_type=f32
            )
            inner_sum = jnp.sum(probs * grad_probs, axis=1, keepdims=True)
            grad_scores = (probs * (grad_probs - inner_sum)).astype(jnp.bfloat16)
            dq_parts.append(jnp.dot(grad_scores, keys, preferred_element_type=f32))
            dk_acc[0:seen, :] += lax.dot_general(
                grad_scores, queries, TN, preferred_element_type=f32
            )
            dv_acc[0:seen, :] += lax.dot_general(
                probs.astype(jnp.bfloat16), grads, TN, preferred_element_type=f32
            )
            upto = jnp.dot(grad_scores, prefix_ref[0:seen, 0:seen], preferred_element_type=f32)
            for at in range(0, seen, 128):
                read = jnp.take_along_axis(
                    upto[:, at : at + 128], lane_at, axis=1, mode="promise_in_bounds"
                )
                read = jnp.where((edges >= at) & (edges < at + 128), read, 0.0)
                edge_sums[half] = edge_sums[half] + jnp.sum(
                    read.reshape(block // 8, 8, 128), axis=0
                )
        dq_ref[rows, :] = ((dq_parts[0] + dq_parts[1]) * 0.125).astype(jnp.bfloat16)
    dk_ref[...] = dk_acc[...].astype(jnp.bfloat16)
    dv_ref[...] = dv_acc[...].astype(jnp.bfloat16)
    edge_sum_ref[0] = edge_sums[0]
    edge_sum_ref[1] = edge_sums[1]


def attend_back(queries, keys, values, grads, logs, buckets, table, prefix, edges, block):
    length, width = queries.shape
    cols = pl.BlockSpec((length, 128), lambda pair: (0, pair))
    low = jax.ShapeDtypeStruct((length, width), jnp.bfloat16)
    return pl.pallas_call(
        functools.partial(attend_back_kernel, block, length),
        grid=(width // 128,),
        in_specs=[
            cols,
            cols,
            cols,
            cols,
            pl.BlockSpec((1, length, 128), lambda pair: (pair, 0, 0)),
            pl.BlockSpec(buckets.shape, lambda pair: (0, 0)),
            pl.BlockSpec(table.shape, lambda pair: (0, 0)),
            pl.BlockSpec(prefix.shape, lambda pair: (0, 0)),
            pl.BlockSpec(edges.shape, lambda pair: (0, 0)),
        ],
        out_specs=[cols, cols, cols, pl.BlockSpec((2, 8, 128), lambda pair: (pair, 0, 0))],
        out_shape=[low, low, low, jax.ShapeDtypeStruct((width // 64, 8, 128), jnp.float32)],
        scratch_shapes=[pltpu.VMEM((length, 128), jnp.float32)] * 2,
        compiler_params=pltpu.CompilerParams(vmem_limit_bytes=48 * 1024 * 1024),
    )(queries, keys, values, grads, logs, buckets, table, prefix, edges)


def adam_step(weight, moment, square, gradient, factor):
    clipped = gradient * factor
    moment_next = 0.9 * moment + 0.1 * clipped
    square_next = 0.95 * square + 0.05 * clipped * clipped
    corrected_moment = moment_next / (1.0 - 0.9**STEP)
    corrected_square = square_next / (1.0 - 0.95**STEP)
    update = -learn_rate * (
        corrected_moment / (jnp.sqrt(corrected_square) + 1e-08)
        + weight_decay * weight.astype(jnp.float32)
    )
    return (moment_next, square_next, update)


def local(
    token_ids,
    segment_ids,
    parent_segments,
    expert_choice,
    drop_order,
    loss_positions,
    target_ids,
    embedding,
    attention_weights,
    router_weights,
    small_params,
    inward_weights,
    outward_weights,
    embedding_moment,
    embedding_square,
    attention_moment,
    attention_square,
    router_moment,
    router_square,
    params_moment,
    params_square,
    inward_moment,
    inward_square,
    outward_moment,
    outward_square,
):
    devices = lax.axis_size("fsdp")
    me = lax.axis_index("fsdp")
    length = token_ids.shape[0]
    vocab_rows, model_width = embedding.shape
    rows_loss = loss_positions.shape[0]
    experts_all = devices // SPLIT
    capacity = 9 * 2 * length // (8 * experts_all)
    slots = -(-capacity // 16) * 16
    block_rows = 128
    f32 = jnp.float32
    bf16 = jnp.bfloat16
    quads = [[SPLIT * e + q for q in range(SPLIT)] for e in range(experts_all)]
    router_size = router_weights.shape[0]
    params_size = small_params.shape[0]

    owner = token_ids // vocab_rows
    place = token_ids - owner * vocab_rows
    order = jnp.arange(length, dtype=jnp.int32)
    repeated = jnp.any(
        (token_ids[:, None] == token_ids[None, :]) & (order[None, :] < order[:, None]), axis=1
    )
    fresh = ~repeated
    rank = jnp.sum(
        (
            fresh[None, :]
            & (owner[None, :] == owner[:, None])
            & (token_ids[None, :] < token_ids[:, None])
        ).astype(jnp.int32),
        axis=1,
    )
    too_many = jnp.any(rank >= ASK).astype(f32)
    ask_row = jnp.where(rank < ASK, owner * ASK + rank, devices * ASK)
    ask_lines = jnp.arange(devices * ASK, dtype=jnp.int32)
    asked = jnp.sum(
        jnp.where(
            (ask_lines[:, None] == ask_row[None, :]) & fresh[None, :], place[None, :] + 1, 0
        ),
        axis=1,
    )
    hello = pack_blocks(
        (
            asked.reshape(devices, ASK).astype(f32),
            router_weights.astype(f32)[None],
            small_params.astype(f32)[None],
            target_ids.astype(f32).reshape(1, -1),
            too_many.reshape(1, 1),
        ),
        devices,
    )
    heard = swap_blocks(hello, 1, 1).reshape(devices, -1)
    spans = [ASK, router_size, params_size, 2 * rows_loss, 1]
    edges = [sum(spans[:i]) for i in range(len(spans) + 1)]
    wanted, router_full, params_full, targets_full, crowded = [
        heard[:, edges[i] : edges[i + 1]] for i in range(len(spans))
    ]
    wanted = wanted.reshape(-1).astype(jnp.int32) - 1
    router_full = router_full.reshape(-1).astype(bf16)
    params_full = params_full.reshape(-1)
    targets_full = targets_full.reshape(-1, 2).astype(jnp.int32)
    crowded = jnp.any(crowded > 0.5)
    inward_full = lax.all_gather(inward_weights[0], "fsdp", axis=0, axis_index_groups=quads)
    outward_full = lax.all_gather(outward_weights[0], "fsdp", axis=0, axis_index_groups=quads)

    siblings = [(device, device + 1 - 2 * (device % 2)) for device in range(devices)]
    chips = devices // 2
    core = lax.rem(me, 2)
    vocab_pad = -(-vocab_rows // 256) * 256
    fill = ((0, vocab_pad - vocab_rows), (0, 0))
    chip_table = jnp.concatenate(
        [jnp.pad(embedding, fill), jnp.pad(lax.ppermute(embedding, "fsdp", siblings), fill)], axis=0
    )
    vocab_lines = jnp.arange(vocab_pad, dtype=jnp.int32)
    chip_ids = jnp.concatenate(
        [
            jnp.where(vocab_lines < vocab_rows, vocab_lines + side * vocab_rows, -1)
            for side in (me, me + 1 - 2 * core)
        ]
    )[:, None]

    wanted_mask = wanted[:, None] == jnp.arange(vocab_rows, dtype=jnp.int32)[None, :]
    served = take_rows(wanted_mask, embedding).astype(bf16).reshape(devices, ASK, model_width)
    attention_rows = attention_weights.shape[0]
    attention_pad = -attention_rows % 16
    served, attention_full = head_exchange(
        served, jnp.pad(attention_weights, ((0, attention_pad), (0, 0))), 2
    )
    served = served.reshape(devices * ASK, model_width)
    attention_full = attention_full[:, :, :attention_rows].reshape(-1, model_width)
    ask_mask = ask_row[:, None] == ask_lines[None, :]
    embedded_low = lax.cond(
        crowded,
        lambda: lax.all_gather(embedding, "fsdp", axis=0, tiled=True)[token_ids],
        lambda: take_rows(ask_mask, served).astype(bf16),
    )
    embedded = embedded_low.astype(f32) * math.sqrt(model_width)
    gain_first = params_full[:model_width]
    gain_second = params_full[model_width : 2 * model_width]
    gain_final = params_full[2 * model_width : 3 * model_width]
    bias_table = params_full[3 * model_width :].reshape(HEADS, NB)
    router_matrix = router_full.reshape(model_width, experts_all)
    buckets, prefix, edges = tree_layout(segment_ids, parent_segments[0])
    normed_first = rms_norm(embedded, gain_first).astype(bf16)
    queries, keys_all, values_all = [
        jnp.dot(
            normed_first,
            attention_full[part * model_width : (part + 1) * model_width],
            preferred_element_type=f32,
        ).astype(bf16)
        for part in range(3)
    ]
    bias_lines = jnp.pad(
        jnp.concatenate([bias_table, jnp.full((HEADS, 1), -1e30, f32)], axis=1),
        ((0, 16 - HEADS), (0, 127 - NB)),
    )
    mixed_all, log_totals = attend(queries, keys_all, values_all, buckets, bias_lines, block_rows)
    after_attn = embedded + jnp.dot(
        mixed_all, attention_full[3 * model_width :], preferred_element_type=f32
    )
    routed_in = rms_norm(after_attn, gain_second).astype(bf16)
    route_logits = jnp.dot(routed_in, router_matrix, preferred_element_type=f32)
    choice_onehot = (
        expert_choice[:, :, None] == jnp.arange(experts_all, dtype=jnp.int32)[None, None, :]
    ).astype(f32)
    chosen = jnp.sum(choice_onehot * route_logits[:, None, :], axis=-1)
    gate_peak = jnp.max(chosen, axis=1, keepdims=True)
    raised_gate = jnp.exp(chosen - gate_peak)
    gate_weights = raised_gate / jnp.sum(raised_gate, axis=1, keepdims=True)
    drop_rank = drop_order[0]
    flat_choice = expert_choice.reshape(-1)
    slot_index = jnp.sum(
        (
            (flat_choice[None, :] == flat_choice[:, None])
            & (drop_rank[None, :] < drop_rank[:, None])
        ).astype(jnp.int32),
        axis=1,
    ).reshape(length, 2)
    target_row = jnp.where(
        slot_index < capacity, expert_choice * slots + slot_index, experts_all * slots
    )
    slot_lines = jnp.arange(experts_all * slots, dtype=jnp.int32)
    first_in = target_row[:, 0][:, None] == slot_lines[None, :]
    second_in = target_row[:, 1][:, None] == slot_lines[None, :]
    marks = jnp.pad(target_row.T, ((0, 6), (0, 0)), constant_values=-1)
    expert_rows, returned_first, returned_second = run_experts(
        routed_in, marks, target_row, inward_full, outward_full, experts_all, slots, 7
    )
    after_moe = (
        after_attn + gate_weights[:, 0:1] * returned_first + gate_weights[:, 1:2] * returned_second
    )
    normed_final = rms_norm(after_moe, gain_final).astype(bf16)
    loss_mask = loss_positions[:, None] == order[None, :]
    picked = take_rows(loss_mask, normed_final).astype(bf16)
    scale_rows = 1.0 / (devices * rows_loss)

    targets_here = jnp.where(
        core == 0,
        targets_full.reshape(chips, 2, rows_loss, 2)[:, 0],
        targets_full.reshape(chips, 2, rows_loss, 2)[:, 1],
    ).reshape(chips // BLOCK, BLOCK * rows_loss, 2)
    targets_here = jnp.pad(targets_here.swapaxes(1, 2), ((0, 0), (0, 6), (0, 0)))
    picked_grad, own_grad, far_grad, loss_rows = loss_exchange(
        picked, chip_table, chip_ids, targets_here, chips, scale_rows, 5
    )
    loss_local = jnp.sum(loss_rows[0])
    table_grad = (own_grad + lax.ppermute(far_grad, "fsdp", siblings))[:vocab_rows]
    grad_normed = take_rows_wide(loss_mask.T, picked_grad.T)
    _, final_back = jax.vjp(rms_norm, after_moe, gain_final)
    grad_after_moe, grad_gain_final = final_back(grad_normed)
    grad_gates = jnp.stack(
        [
            jnp.sum(returned_first * grad_after_moe, axis=-1),
            jnp.sum(returned_second * grad_after_moe, axis=-1),
        ],
        axis=1,
    )
    grad_chosen = gate_weights * (
        grad_gates - jnp.sum(gate_weights * grad_gates, axis=1, keepdims=True)
    )
    grad_route = jnp.sum(choice_onehot * grad_chosen[:, :, None], axis=1).astype(bf16)
    router_grad = jnp.einsum(
        "td,te->de", routed_in, grad_route, preferred_element_type=f32
    ).reshape(-1)
    grad_routed = jnp.einsum("te,de->td", grad_route, router_matrix, preferred_element_type=f32)
    grad_returned, inward_parts, outward_parts = run_experts_back(
        (gate_weights[:, 0:1] * grad_after_moe).astype(bf16),
        (gate_weights[:, 1:2] * grad_after_moe).astype(bf16),
        marks,
        expert_rows,
        inward_full,
        outward_full,
        8,
    )
    grad_returned = grad_returned.reshape(experts_all * slots, model_width)
    inward_grad = lax.psum_scatter(
        inward_parts, "fsdp", scatter_dimension=0, axis_index_groups=quads
    )[None]
    outward_grad = lax.psum_scatter(
        outward_parts, "fsdp", scatter_dimension=0, axis_index_groups=quads
    )[None]
    grad_routed = grad_routed + take_rows(first_in | second_in, grad_returned)
    _, second_back = jax.vjp(rms_norm, after_attn, gain_second)
    grad_norm_in, grad_gain_second = second_back(grad_routed)
    grad_after_attn = grad_after_moe + grad_norm_in
    grad_attn_low = grad_after_attn.astype(bf16)
    output_grad = jnp.einsum("td,te->de", mixed_all, grad_attn_low, preferred_element_type=f32)
    grad_mixed = jnp.einsum(
        "te,de->td", grad_attn_low, attention_full[3 * model_width :], preferred_element_type=f32
    ).astype(bf16)
    grad_queries_low, grad_keys_low, grad_values_low, edge_sums = attend_back(
        queries,
        keys_all,
        values_all,
        grad_mixed,
        log_totals,
        buckets,
        bias_lines,
        prefix,
        edges,
        block_rows,
    )
    grad_queries_low, grad_keys_low, grad_values_low, edge_sums, inward_grad = (
        lax.optimization_barrier(
            (grad_queries_low, grad_keys_low, grad_values_low, edge_sums, inward_grad)
        )
    )
    edge_sums = jnp.sum(edge_sums, axis=1)[:, :NB]
    grad_bias = edge_sums - jnp.pad(edge_sums[:, 1:], ((0, 0), (0, 1)))
    projection_grads = []
    grad_normed_first = jnp.zeros((length, model_width), f32)
    for position, gradient_low in enumerate((grad_queries_low, grad_keys_low, grad_values_low)):
        projection_grads.append(
            jnp.einsum("td,te->de", normed_first, gradient_low, preferred_element_type=f32)
        )
        grad_normed_first = grad_normed_first + jnp.einsum(
            "te,de->td",
            gradient_low,
            attention_full[position * model_width : (position + 1) * model_width],
            preferred_element_type=f32,
        )
    attention_grad = jnp.concatenate(projection_grads + [output_grad], axis=0)
    _, first_back = jax.vjp(rms_norm, embedded, gain_first)
    grad_embed_in, grad_gain_first = first_back(grad_normed_first)
    grad_embedded = (grad_after_attn + grad_embed_in) * math.sqrt(model_width)
    params_grad = jnp.concatenate(
        [grad_gain_first, grad_gain_second, grad_gain_final, grad_bias.reshape(-1)]
    )
    ask_sums = take_rows_wide(ask_mask.T, grad_embedded).astype(bf16)
    attention_blocks = jnp.pad(
        attention_grad.astype(bf16).reshape(devices // 2, 2, attention_rows, model_width),
        ((0, 0), (0, 0), (0, attention_pad), (0, 0)),
    )
    small_blocks = pack_blocks(
        (router_grad.reshape(devices, router_size), params_grad.reshape(devices, params_size)),
        devices,
    )
    ask_sums, small_sums, attention_share = tail_exchange(
        ask_sums.reshape(devices, ASK, model_width), small_blocks, attention_blocks, 9
    )
    ask_sums, small_sums, attention_share, outward_grad = lax.optimization_barrier(
        (ask_sums, small_sums, attention_share, outward_grad)
    )
    attention_share = attention_share[:attention_rows]
    small_share = jnp.sum(small_sums.reshape(devices, -1), axis=0)

    def lookup_wide():
        whole = jnp.zeros((devices * vocab_rows, model_width), f32).at[token_ids].add(grad_embedded)
        return lax.psum_scatter(whole, "fsdp", scatter_dimension=0, tiled=True)

    table_share = table_grad + lax.cond(
        crowded,
        lookup_wide,
        lambda: take_rows(wanted_mask.T, ask_sums.reshape(devices * ASK, model_width)),
    )
    router_share = small_share[:router_size]
    params_share = small_share[router_size : router_size + params_size]
    local_square = (
        jnp.sum(table_share * table_share)
        + jnp.sum(attention_share * attention_share)
        + jnp.sum(router_share * router_share)
        + jnp.sum(params_share * params_share)
        + jnp.sum(inward_grad * inward_grad)
        + jnp.sum(outward_grad * outward_grad)
    )
    total_square = jnp.sum(
        swap_blocks(pack_blocks((local_square.reshape(1, 1),), devices), 1, 11).reshape(devices, -1)[
            :, 0
        ]
    )
    grad_norm = jnp.sqrt(total_square)
    threshold = clip_base / math.sqrt(devices * rows_loss)
    factor = jnp.minimum(1.0, threshold / grad_norm)
    loss_parts = (loss_local * scale_rows).reshape(1)
    table_m, table_s, table_u = adam_step(
        embedding, embedding_moment, embedding_square, table_share, factor
    )
    attention_m, attention_s, attention_u = adam_step(
        attention_weights, attention_moment, attention_square, attention_share, factor
    )
    router_m, router_s, router_u = adam_step(
        router_weights, router_moment, router_square, router_share, factor
    )
    params_m, params_s, params_u = adam_step(
        small_params, params_moment, params_square, params_share, factor
    )
    inward_m, inward_s, inward_u = adam_step(
        inward_weights, inward_moment, inward_square, inward_grad, factor
    )
    outward_m, outward_s, outward_u = adam_step(
        outward_weights, outward_moment, outward_square, outward_grad, factor
    )
    return (
        loss_parts,
        grad_norm,
        table_m,
        table_s,
        table_u,
        attention_m,
        attention_s,
        attention_u,
        router_m,
        router_s,
        router_u,
        params_m,
        params_s,
        params_u,
        inward_m,
        inward_s,
        inward_u,
        outward_m,
        outward_s,
        outward_u,
    )


def solution(mesh):
    placed = (
        P("fsdp"),
        P("fsdp"),
        P("fsdp", None),
        P("fsdp", None),
        P("fsdp", None),
        P("fsdp"),
        P("fsdp", None),
        P("fsdp", None),
        P("fsdp", None),
        P("fsdp"),
        P("fsdp"),
        P("fsdp", None, None),
        P("fsdp", None, None),
        P("fsdp", None),
        P("fsdp", None),
        P("fsdp", None),
        P("fsdp", None),
        P("fsdp"),
        P("fsdp"),
        P("fsdp"),
        P("fsdp"),
        P("fsdp", None, None),
        P("fsdp", None, None),
        P("fsdp", None, None),
        P("fsdp", None, None),
    )
    return jax.shard_map(
        local,
        mesh=mesh,
        in_specs=placed,
        out_specs=(
            P("fsdp"),
            P(),
            P("fsdp", None),
            P("fsdp", None),
            P("fsdp", None),
            P("fsdp", None),
            P("fsdp", None),
            P("fsdp", None),
            P("fsdp"),
            P("fsdp"),
            P("fsdp"),
            P("fsdp"),
            P("fsdp"),
            P("fsdp"),
            P("fsdp", None, None),
            P("fsdp", None, None),
            P("fsdp", None, None),
            P("fsdp", None, None),
            P("fsdp", None, None),
            P("fsdp", None, None),
        ),
        check_vma=False,
    )
```
